32 devices in a mesh: dp: 2 (over core), ep: 4 (over z), tp: 4 (over y, x).
Axes of the slice: x: 2, y: 2, z: 4, core: 2. Of those that a mesh axis runs over, the one named last changes fastest.
Arguments:
- block_input_rows: float32 [4096, 768], P(('dp', 'ep')), may hold values from -6 to 6
- passage_number: int32 [4096], P(('dp', 'ep')), may hold values from 0 to 31, never falling along the last dimension, each value on 1 to 256 neighbouring positions
- initial_layernorm_gain: float32 [768], replicated, may hold values from 0.25 to 1.75
- asker_weights: float32 [768, 768], P(None, 'tp'), may hold values from -0.21875 to 0.21875
- lookup_weights: float32 [768, 768], P(None, 'tp'), may hold values from -0.21875 to 0.21875
- payload_weights: float32 [768, 768], P(None, 'tp'), may hold values from -0.21875 to 0.21875
- heads_merge_weights: float32 [768, 768], P('tp'), may hold values from -1.25 to 1.25
- latter_layernorm_gain: float32 [768], replicated, may hold values from 0.25 to 1.75
- dispatcher_weights: float32 [768, 16], replicated, may hold values from -0.21875 to 0.21875
- dispatcher_specialist_vectors: float32 [4, 16], replicated, may hold values from -5 to 5
- softness_factor: float32 [1], replicated, may hold values from 0.25 to 0.45
- specialist_raise_weights: float32 [4, 768, 3072], P('ep', None, ('dp', 'tp')), may hold values from -0.21875 to 0.21875
- specialist_lower_weights: float32 [4, 3072, 768], P('ep', ('dp', 'tp')), may hold values from -3.5 to 3.5
- chosen_specialist_number: int32 [4096], P(('dp', 'ep', 'tp')), may hold values from 0 to 3
- buffer_position_number: int32 [4096], P(('dp', 'ep', 'tp')), may hold values from -1 to 31, as said below
- block_result_cotangent: float32 [4096, 768], P(('dp', 'ep', 'tp')), may hold values from -6 to 6
Outputs:
- mixed: float32 [4096, 768], P(('dp', 'ep', 'tp'))
- grad_tokens: float32 [4096, 768], P(('dp', 'ep'))
- grad_norm1_gain: float32 [768], replicated
- grad_query: float32 [768, 768], P(None, 'tp')
- grad_key: float32 [768, 768], P(None, 'tp')
- grad_value: float32 [768, 768], P(None, 'tp')
- grad_output_weight: float32 [768, 768], P('tp')
- grad_norm2_gain: float32 [768], replicated
- grad_router_proj: float32 [768, 16], replicated
- grad_router_embed: float32 [4, 16], replicated
- grad_temperature: float32 [1], replicated
- grad_up: float32 [4, 768, 3072], P('ep', None, ('dp', 'tp'))
- grad_down: float32 [4, 3072, 768], P('ep', ('dp', 'tp'))
The draws below stay inside these ranges and needn't reach their ends.
Inputs may be any that keep to these rules, and one draw needn't show every extreme that they name: In each aligned block of 128 rows, buffer_position_number of a token is the number of earlier tokens of that block naming the same expert if that number is under 32, else -1; chosen_specialist_number and buffer_position_number come from one draw.
All inputs are finite; a program needn't handle non-finite values.
Results may differ from the reference program's by a relative error of at most 0.0003.
Values sent between devices are 32-bit elements; how exact they have to be, the bound alone decides.
No kernel may reach another device: no remote copies, remote signals or barrier semaphores. Data moves between devices by JAX's collectives and lax.ppermute only.
A program may use at most 128 MiB of HBM per device.

```python
import math
import jax
import jax.numpy as jnp
import numpy as np
from jax import lax

D = 768
HEADS = 12
HEAD_DIM = 64
FF = 3072
ROUTER_DIM = 16
SEQ = 512
EXPERTS = 4
TOKENS = 4096
ROWS = 128
CAPACITY = 32


def routing(key):
    base = jax.random.fold_in(key, 11)
    blocks = TOKENS // ROWS
    favored = jax.random.randint(jax.random.fold_in(base, 1), (), 0, EXPERTS)
    block_keys = jax.random.split(jax.random.fold_in(base, 2), blocks)

    def one_block(block_key):
        first, second, third, fourth = jax.random.split(block_key, 4)
        order = jax.random.permutation(first, EXPERTS)
        draw_a = jax.random.randint(second, (ROWS,), 0, EXPERTS)
        draw_b = jax.random.randint(third, (ROWS,), 0, EXPERTS)
        chosen = order[jnp.minimum(draw_a, draw_b)]
        forced = jax.random.permutation(fourth, ROWS)[:CAPACITY]
        chosen = chosen.at[forced].set(favored)
        onehot = (chosen[:, None] == jnp.arange(EXPERTS)[None, :]).astype(jnp.int32)
        before = jnp.cumsum(onehot, axis=0) - onehot
        place = jnp.sum(before * onehot, axis=1)
        slot_value = jnp.where(place < CAPACITY, place, -1)
        return (chosen.astype(jnp.int32), slot_value.astype(jnp.int32))
    chosen_all, slots_all = jax.vmap(one_block)(block_keys)
    return (chosen_all.reshape(TOKENS), slots_all.reshape(TOKENS))


def draw_chosen_specialist_number(key, part):
    shared = routing(key)
    return shared[0]


def draw_buffer_position_number(key, part):
    shared = routing(key)
    return shared[1]


def block_levels(own_key, shape, cuts, least, high):
    loudness = 1.0
    for position, shards_of in cuts:
        heights = jax.random.uniform(jax.random.fold_in(jax.random.fold_in(own_key, 6), position), (shards_of,), jnp.float32, least / len(cuts), high / len(cuts))
        loudness = loudness * jnp.repeat(jnp.exp(heights), shape[position] // shards_of).reshape((-1,) + (1,) * (len(shape) - 1 - position))
    return loudness


def length_profile(count, total, most, slope):
    portions = [(1 << 20) // math.isqrt(grade ** slope) + 1 for grade in range(2, count + 1)]
    spare, holding = total - most - (count - 1), [1] * (count - 1)
    while spare > 0:
        candidates = [i for i in range(count - 1) if holding[i] < most]
        whole, remaining = sum([portions[i] for i in candidates]), spare
        for i in candidates:
            more = min(most - holding[i], max(1, remaining * portions[i] // whole), spare)
            holding[i] = holding[i] + more
            spare = spare - more
    return np.array([most] + holding)


def uneven(key, amount, total, most, skew):
    if amount == 2:
        one = jax.random.randint(key, (), max(1, total - most), min(most, total - 1) + 1)
        return jnp.stack([one, total - one])
    lengths = jnp.asarray(length_profile(amount, total, most, skew), jnp.int32)
    pairs = (amount - 1) // 2
    giver, sink = lengths[1:1 + 2 * pairs:2], lengths[2:2 + 2 * pairs:2]
    slack = jnp.minimum(giver - 1, most - sink)
    moved = jax.random.randint(jax.random.fold_in(key, 1), (pairs,), 0, 1 << 20) % (slack + 1)
    lengths = lengths.at[1:1 + 2 * pairs:2].set(giver - moved).at[2:2 + 2 * pairs:2].set(sink + moved)
    return lengths[jax.random.permutation(jax.random.fold_in(key, 2), amount)]


def noise(rng, dims, scale, reach, cuts=(), kind=jnp.bfloat16):
    drawn = jax.random.normal(rng, dims, jnp.float32) * scale
    if len(cuts) > 0:
        drawn = block_levels(rng, dims, cuts, -0.22, 0.18) * drawn
    return jnp.clip(drawn, min=-reach, max=reach).astype(kind)


def setup_inputs(seed: int = 0) -> dict:
    arg_keys = jax.random.split(jax.random.key(seed), 17)
    block_input_rows = noise(arg_keys[0], (TOKENS, D), 1.0, 6.0, ((0, 8),), jnp.float32)
    passage_number = jnp.searchsorted(jnp.cumsum(uneven(arg_keys[1], 4 * TOKENS // SEQ, TOKENS, SEQ // 2, 1)), jnp.arange(TOKENS), side="right").astype(jnp.int32)
    initial_layernorm_gain = jnp.clip(1.0 + 0.15 * jax.random.normal(arg_keys[2], (D,), jnp.float32), 0.25, 1.75)
    asker_weights = noise(arg_keys[3], (D, D), D ** -0.5, 0.21875, ((1, 4),), jnp.float32)
    lookup_weights = noise(arg_keys[4], (D, D), D ** -0.5, 0.21875, ((1, 4),), jnp.float32)
    payload_weights = noise(arg_keys[5], (D, D), D ** -0.5, 0.21875, ((1, 4),), jnp.float32)
    heads_merge_weights = noise(arg_keys[6], (D, D), (D // 32) ** -0.5, 1.25, ((0, 4),), jnp.float32)
    latter_layernorm_gain = jnp.clip(1.0 + 0.15 * jax.random.normal(arg_keys[7], (D,), jnp.float32), 0.25, 1.75)
    dispatcher_weights = noise(arg_keys[8], (D, ROUTER_DIM), D ** -0.5, 0.21875, (), jnp.float32)
    dispatcher_specialist_vectors = noise(arg_keys[9], (EXPERTS, ROUTER_DIM), 1.0, 5.0, (), jnp.float32)
    softness_factor = jnp.clip(jax.random.uniform(arg_keys[10], (1,), jnp.float32, 0.25, 0.45), 0.25, 0.45)
    specialist_raise_weights = noise(arg_keys[11], (EXPERTS, D, FF), D ** -0.5, 0.21875, ((0, 4), (2, 8)), jnp.float32)
    specialist_lower_weights = noise(arg_keys[12], (EXPERTS, FF, D), (max(FF // 1024, 1)) ** -0.5, 3.5, ((0, 4), (1, 8)), jnp.float32)
    chosen_specialist_number = draw_chosen_specialist_number(jax.random.fold_in(arg_keys[16], 71), 0)
    buffer_position_number = draw_buffer_position_number(jax.random.fold_in(arg_keys[16], 71), 0)
    block_result_cotangent = noise(arg_keys[15], (TOKENS, D), 1.0, 6.0, ((0, 32),), jnp.float32)
    return {"block_input_rows": block_input_rows, "passage_number": passage_number, "initial_layernorm_gain": initial_layernorm_gain, "asker_weights": asker_weights, "lookup_weights": lookup_weights, "payload_weights": payload_weights, "heads_merge_weights": heads_merge_weights, "latter_layernorm_gain": latter_layernorm_gain, "dispatcher_weights": dispatcher_weights, "dispatcher_specialist_vectors": dispatcher_specialist_vectors, "softness_factor": softness_factor, "specialist_raise_weights": specialist_raise_weights, "specialist_lower_weights": specialist_lower_weights, "chosen_specialist_number": chosen_specialist_number, "buffer_position_number": buffer_position_number, "block_result_cotangent": block_result_cotangent}


@jax.custom_vjp
def low(v):
    return lax.optimization_barrier(v.astype(jnp.bfloat16)).astype(jnp.float32)

@jax.custom_vjp
def low_back(v):
    return v

def low_keep(v):
    return (low(v), None)

def low_pass(kept, grad):
    return (grad,)

def back_keep(v):
    return (v, None)

def back_low(kept, grad):
    return (low(grad),)
low.defvjp(low_keep, low_pass)
low_back.defvjp(back_keep, back_low)

def matmul(left, right):
    return jnp.dot(left, right, precision=lax.Precision.HIGHEST, preferred_element_type=jnp.float32)

def layer_norm(values, gain_vec):
    center = values - lax.optimization_barrier(jnp.mean(values, axis=-1, keepdims=True))
    spread = lax.optimization_barrier(jnp.mean(center * center, axis=-1, keepdims=True))
    return center * lax.rsqrt(spread + 1e-05) * gain_vec

def attend_item(operands):
    query_blk, key_blk, value_blk, seg_blk = operands
    query_heads = query_blk.reshape(SEQ, HEADS, HEAD_DIM)
    key_heads = key_blk.reshape(SEQ, HEADS, HEAD_DIM)
    value_heads = value_blk.reshape(SEQ, HEADS, HEAD_DIM)
    scores = jnp.einsum('qhd,khd->hqk', query_heads, key_heads, precision=lax.Precision.HIGHEST) * HEAD_DIM ** (-0.5)
    allowed = seg_blk[:, None] == seg_blk[None, :]
    scores = jnp.where(allowed[None], scores, -1e+30)
    weights = jax.nn.softmax(scores, axis=-1)
    context = jnp.einsum('hqk,khd->qhd', weights, value_heads, precision=lax.Precision.HIGHEST)
    return context.reshape(SEQ, D)

def expert_apply(operands):
    rows_in, first_w, second_w = operands
    return matmul(jax.nn.gelu(matmul(rows_in, first_w)), second_w)

def reference(block_input_rows, passage_number, initial_layernorm_gain, asker_weights, lookup_weights, payload_weights, heads_merge_weights, latter_layernorm_gain, dispatcher_weights, dispatcher_specialist_vectors, softness_factor, specialist_raise_weights, specialist_lower_weights, chosen_specialist_number, buffer_position_number, block_result_cotangent):
    passage_number = passage_number.astype(jnp.int32)
    chosen_specialist_number = chosen_specialist_number.astype(jnp.int32)
    buffer_position_number = buffer_position_number.astype(jnp.int32)
    blocks = TOKENS // ROWS
    block_index = (jnp.arange(TOKENS, dtype=jnp.int32) // ROWS).astype(jnp.int32)
    kept = buffer_position_number >= 0
    dump_row = EXPERTS * blocks * CAPACITY
    target = jnp.where(kept, (chosen_specialist_number * blocks + block_index) * CAPACITY + buffer_position_number, dump_row).astype(jnp.int32)
    choose = (chosen_specialist_number[:, None] == jnp.arange(EXPERTS, dtype=jnp.int32)[None, :]).astype(jnp.float32)

    def forward(inputs_f, gain_one, w_query, w_key, w_value, w_output, gain_two, w_router, embed_f, temp_f, w_first, w_second):
        normed1 = layer_norm(inputs_f, gain_one)
        queries = matmul(normed1, w_query)
        key_proj = matmul(normed1, w_key)
        value_proj = matmul(normed1, w_value)
        items = TOKENS // SEQ
        context = lax.map(jax.checkpoint(attend_item), (queries.reshape(items, SEQ, D), key_proj.reshape(items, SEQ, D), value_proj.reshape(items, SEQ, D), passage_number.reshape(items, SEQ)))
        hidden_state = inputs_f + matmul(context.reshape(TOKENS, D), w_output)
        normed2 = layer_norm(hidden_state, gain_two)
        routed = matmul(normed2, w_router)
        unit = routed * lax.rsqrt(lax.optimization_barrier(jnp.sum(routed * routed, axis=-1, keepdims=True)) + 1.0)
        embed_unit = embed_f * lax.rsqrt(lax.optimization_barrier(jnp.sum(embed_f * embed_f, axis=-1, keepdims=True)) + 1.0)
        logits = matmul(unit, embed_unit.T) / temp_f[0]
        gate_value = lax.optimization_barrier(jnp.sum(jax.nn.softmax(logits, axis=-1) * choose, axis=-1))
        buffer = jnp.zeros((dump_row + 1, D), jnp.float32).at[target].add(normed2)
        buffer = buffer[:dump_row].reshape(EXPERTS, blocks * CAPACITY, D)
        outputs = lax.map(expert_apply, (buffer, w_first, w_second))
        padded = jnp.concatenate([outputs.reshape(dump_row, D), jnp.zeros((1, D), jnp.float32)], axis=0)
        return hidden_state + gate_value[:, None] * padded[target]
    learnable_weights = (block_input_rows.astype(jnp.float32), initial_layernorm_gain.astype(jnp.float32), asker_weights.astype(jnp.float32), lookup_weights.astype(jnp.float32), payload_weights.astype(jnp.float32), heads_merge_weights.astype(jnp.float32), latter_layernorm_gain.astype(jnp.float32), dispatcher_weights.astype(jnp.float32), dispatcher_specialist_vectors.astype(jnp.float32), softness_factor.astype(jnp.float32), specialist_raise_weights.astype(jnp.float32), specialist_lower_weights.astype(jnp.float32))
    mixed, pullback = jax.vjp(forward, *learnable_weights)
    grads = pullback(block_result_cotangent.astype(jnp.float32))
    return (mixed, grads[0], grads[1], grads[2], grads[3], grads[4], grads[5], grads[6], grads[7], grads[8], grads[9], grads[10], grads[11])
```

```python
import jax
import jax.numpy as jnp
from jax import lax
from jax.sharding import PartitionSpec as P

HEAD_DIM = 64
EPS = 1e-05
PREC = lax.Precision.HIGH


def mm(left, right):
    return jnp.dot(left, right, precision=PREC, preferred_element_type=jnp.float32)


def mm_tn(left, right):
    return lax.dot_general(
        left, right, (((0,), (0,)), ((), ())), precision=PREC, preferred_element_type=jnp.float32
    )


def mm_nt(left, right):
    return lax.dot_general(
        left, right, (((1,), (1,)), ((), ())), precision=PREC, preferred_element_type=jnp.float32
    )


def exact_tn(onehot, rows):
    return lax.dot_general(
        onehot,
        rows,
        (((0,), (0,)), ((), ())),
        precision=lax.Precision.HIGHEST,
        preferred_element_type=jnp.float32,
    )


def exact(onehot, rows):
    return jnp.dot(
        onehot, rows, precision=lax.Precision.HIGHEST, preferred_element_type=jnp.float32
    )


def swap(value, axis, shift):
    count = lax.axis_size(axis)
    return lax.ppermute(value, axis, [(i, i ^ shift) for i in range(count)])


def normalize(values):
    center = values - jnp.mean(values, axis=-1, keepdims=True)
    inv = lax.rsqrt(jnp.mean(center * center, axis=-1, keepdims=True) + EPS)
    return center * inv, inv


def normalize_back(grad, gain, xhat, inv):
    scaled = grad * gain
    first = jnp.mean(scaled, axis=-1, keepdims=True)
    second = jnp.mean(scaled * xhat, axis=-1, keepdims=True)
    return inv * (scaled - first - xhat * second)


def over_experts(blocks):
    count = lax.axis_size("ep")
    if count <= 4:
        return [blocks[0]] + [swap(blocks[k], "ep", k) for k in range(1, count)]
    mine = lax.axis_index("ep")
    index = jnp.arange(count, dtype=jnp.int32) ^ mine
    stacked = jnp.take(jnp.stack(blocks), index, axis=0)
    moved = lax.all_to_all(stacked, "ep", split_axis=0, concat_axis=0, tiled=True)
    moved = jnp.take(moved, index, axis=0)
    return [moved[k] for k in range(count)]


def gather_plane(block):
    count = lax.axis_size("tp")
    same = [block] + [swap(block, "tp", d) for d in range(1, count)]
    other = [swap(b, "dp", 1) for b in same]
    return jnp.concatenate(same + other, axis=0)


def scatter_plane(parts):
    count = lax.axis_size("tp")
    rows = parts.shape[0] // (2 * count)
    half = parts[: count * rows] + swap(parts[count * rows :], "dp", 1)
    total = half[:rows]
    for d in range(1, count):
        total = total + swap(half[d * rows : (d + 1) * rows], "tp", d)
    return total


def body(
    x_in,
    passage,
    gain1,
    w_q,
    w_k,
    w_v,
    w_o,
    gain2,
    w_r,
    embed,
    temp,
    w_up,
    w_down,
    chosen,
    place,
    cot,
):
    tp_count = lax.axis_size("tp")
    tp_me = lax.axis_index("tp")
    ep_me = lax.axis_index("ep")
    tokens, width = x_in.shape
    rows = tokens // tp_count
    local = w_q.shape[1]
    heads = local // HEAD_DIM
    experts = embed.shape[0]
    capacity = rows // experts
    w_up, w_down = w_up[0], w_down[0]

    def pick(arr, d):
        return lax.dynamic_slice_in_dim(arr, (tp_me ^ d) * rows, rows, 0)

    x = jnp.concatenate([pick(x_in, d) for d in range(tp_count)], axis=0)
    seg = jnp.concatenate([pick(passage, d) for d in range(tp_count)], axis=0)

    column = (chosen ^ ep_me) * capacity + place
    placer = (
        (column[:, None] == jnp.arange(experts * capacity, dtype=jnp.int32)[None, :])
        & (place >= 0)[:, None]
    ).astype(jnp.float32)

    w_o_cat = jnp.concatenate([w_o] + [swap(w_o, "tp", d) for d in range(1, tp_count)], axis=0)

    def to_experts(slots):
        got = over_experts([slots[k * capacity : (k + 1) * capacity] for k in range(experts)])
        return jnp.concatenate(got, axis=0)

    cots = gather_plane(to_experts(exact_tn(placer, cot)))
    grad_act = mm_nt(cots, w_down)

    xhat, inv = normalize(x)
    normed1 = xhat * gain1
    q, k, v = mm(normed1, w_q), mm(normed1, w_k), mm(normed1, w_v)

    def split(arr):
        return arr.reshape(tokens, heads, HEAD_DIM)

    allowed = (seg[:, None] == seg[None, :])[None]
    scores = jnp.einsum("qhd,khd->hqk", split(q), split(k), precision=PREC) * HEAD_DIM**-0.5
    scores = jnp.where(allowed, scores, -1e30)
    top = jnp.max(scores, axis=-1, keepdims=True)
    expo = jnp.exp(scores - top)
    probs = expo / jnp.sum(expo, axis=-1, keepdims=True)
    ctx = jnp.einsum("hqk,khd->qhd", probs, split(v), precision=PREC).reshape(tokens, local)
    ctx_cat = jnp.concatenate(
        [ctx[:rows]]
        + [swap(ctx[d * rows : (d + 1) * rows], "tp", d) for d in range(1, tp_count)],
        axis=1,
    )
    hidden = x[:rows] + mm(ctx_cat, w_o_cat)
    xhat2, inv2 = normalize(hidden)
    normed2 = xhat2 * gain2
    feed = gather_plane(to_experts(exact_tn(placer, normed2)))

    pre = mm(feed, w_up)
    routed = jnp.dot(feed, w_r, precision=lax.Precision.HIGHEST)
    unit_inv = lax.rsqrt(jnp.sum(routed * routed, axis=-1, keepdims=True) + 1.0)
    unit = routed * unit_inv
    embed_inv = lax.rsqrt(jnp.sum(embed * embed, axis=-1, keepdims=True) + 1.0)
    embed_unit = embed * embed_inv
    raw = jnp.dot(unit, embed_unit.T, precision=lax.Precision.HIGHEST)
    logits = raw / temp[0]
    soft = jax.nn.softmax(logits, axis=-1)
    mine = (jnp.arange(experts, dtype=jnp.int32) == ep_me).astype(jnp.float32)[None, :]
    gate = jnp.sum(soft * mine, axis=-1, keepdims=True)

    act, gelu_back = jax.vjp(jax.nn.gelu, pre)
    grad_pre = gelu_back(grad_act * gate)[0]
    grad_gate = jnp.sum(act * grad_act, axis=-1, keepdims=True)
    grad_logits = grad_gate * gate * (mine - soft)
    grad_temp = -jnp.sum(grad_logits * logits) / temp[0]
    grad_raw = grad_logits / temp[0]
    grad_unit = jnp.dot(grad_raw, embed_unit, precision=lax.Precision.HIGHEST)
    grad_eu = lax.dot_general(
        grad_raw, unit, (((0,), (0,)), ((), ())), precision=lax.Precision.HIGHEST
    )
    grad_embed = embed_inv * (
        grad_eu - embed_unit * jnp.sum(grad_eu * embed_unit, axis=-1, keepdims=True)
    )
    grad_routed = unit_inv * (
        grad_unit - unit * jnp.sum(grad_unit * unit, axis=-1, keepdims=True)
    )
    grad_feed = mm_nt(grad_pre, w_up) + mm_nt(grad_routed, w_r)
    gated = act * gate
    out_part = mm(gated, w_down)
    grad_down = mm_tn(gated, cots)
    grad_up = mm_tn(feed, grad_pre)
    grad_proj = mm_tn(feed, grad_routed)

    grad_normed2 = exact(placer, to_experts(scatter_plane(grad_feed)))
    grad_gain2 = jnp.sum(grad_normed2 * xhat2, axis=0)
    grad_hidden = cot + normalize_back(grad_normed2, gain2, xhat2, inv2)
    grad_ctx_cat = mm_nt(grad_hidden, w_o_cat)
    grad_ctx = jnp.concatenate(
        [grad_ctx_cat[:, :local]]
        + [
            swap(grad_ctx_cat[:, d * local : (d + 1) * local], "tp", d)
            for d in range(1, tp_count)
        ],
        axis=0,
    )
    mixed = hidden + exact(placer, to_experts(scatter_plane(out_part)))

    hidden_cat = jnp.concatenate(
        [grad_hidden] + [swap(grad_hidden, "tp", d) for d in range(1, tp_count)], axis=0
    )
    grad_out = mm_tn(ctx, hidden_cat)

    delta = jnp.sum(split(grad_ctx * ctx), axis=-1).T[..., None]
    grad_probs = jnp.einsum("qhd,khd->hqk", split(grad_ctx), split(v), precision=PREC)
    grad_scores = probs * (grad_probs - delta) * HEAD_DIM**-0.5
    dq = jnp.einsum("hqk,khd->qhd", grad_scores, split(k), precision=PREC).reshape(tokens, local)
    dk = jnp.einsum("hqk,qhd->khd", grad_scores, split(q), precision=PREC).reshape(tokens, local)
    dv = jnp.einsum("hqk,qhd->khd", probs, split(grad_ctx), precision=PREC).reshape(tokens, local)
    grad_normed1 = mm_nt(dq, w_q) + mm_nt(dk, w_k) + mm_nt(dv, w_v)
    own = grad_normed1[:rows]
    for d in range(1, tp_count):
        own = own + swap(grad_normed1[d * rows : (d + 1) * rows], "tp", d)
    grad_gain1 = jnp.sum(grad_normed1 * xhat, axis=0)
    grad_x = grad_hidden + normalize_back(own, gain1, xhat[:rows], inv[:rows])
    grad_tokens = jnp.zeros((tokens, width), jnp.float32)
    for d in range(tp_count):
        block = grad_x if d == 0 else swap(grad_x, "tp", d)
        grad_tokens = lax.dynamic_update_slice_in_dim(
            grad_tokens, block, (tp_me ^ d) * rows, 0
        )
    grad_q, grad_k, grad_v = mm_tn(normed1, dq), mm_tn(normed1, dk), mm_tn(normed1, dv)
    grad_q, grad_k, grad_v, grad_out = lax.psum((grad_q, grad_k, grad_v, grad_out), ("dp", "ep"))
    grad_gain1, grad_gain2, grad_proj, grad_embed, grad_temp = lax.psum(
        (grad_gain1, grad_gain2, grad_proj, grad_embed, grad_temp), ("dp", "ep", "tp")
    )
    return (
        mixed,
        grad_tokens,
        grad_gain1,
        grad_q,
        grad_k,
        grad_v,
        grad_out,
        grad_gain2,
        grad_proj,
        grad_embed,
        grad_temp.reshape(1),
        grad_up[None],
        grad_down[None],
    )


def solution(mesh):
    in_specs = (
        P(("dp", "ep"), None),
        P(("dp", "ep")),
        P(),
        P(None, "tp"),
        P(None, "tp"),
        P(None, "tp"),
        P("tp", None),
        P(),
        P(),
        P(),
        P(),
        P("ep", None, ("dp", "tp")),
        P("ep", ("dp", "tp"), None),
        P(("dp", "ep", "tp")),
        P(("dp", "ep", "tp")),
        P(("dp", "ep", "tp"), None),
    )
    out_specs = (
        P(("dp", "ep", "tp"), None),
        P(("dp", "ep"), None),
        P(),
        P(None, "tp"),
        P(None, "tp"),
        P(None, "tp"),
        P("tp", None),
        P(),
        P(),
        P(),
        P(),
        P("ep", None, ("dp", "tp")),
        P("ep", ("dp", "tp"), None),
    )
    return jax.shard_map(body, mesh=mesh, in_specs=in_specs, out_specs=out_specs, check_vma=False)
```

```python
import functools

import jax
import jax.numpy as jnp
from jax import lax
from jax.experimental import pallas as pl
from jax.experimental.pallas import tpu as pltpu
from jax.sharding import PartitionSpec as P

HEAD_DIM = 64
EPS = 1e-05
F32 = jnp.float32
BF16 = jnp.bfloat16
NN = (((1,), (0,)), ((), ()))
NT = (((1,), (1,)), ((), ()))
TN = (((0,), (0,)), ((), ()))
VMEM_LIMIT = 14 * 1024 * 1024
GELU_C = 0.7978845608028654
GELU_A = 0.044715


def halves(value):
    high = value.astype(BF16)
    return high, (value - high.astype(F32)).astype(BF16)


def dot1(left, right, dims):
    return lax.dot_general(left, right, dims, preferred_element_type=F32)


def dot3(left, right, dims=NN):
    small = dot1(left[0], right[1], dims) + dot1(left[1], right[0], dims)
    return small + dot1(left[0], right[0], dims)


def dot_full(left, right, dims=NN):
    return lax.dot_general(
        left, right, dims, precision=lax.Precision.HIGHEST, preferred_element_type=F32
    )


def place_rows(onehot, value, dims=NN):
    first = value.astype(BF16)
    rest = value - first.astype(F32)
    second = rest.astype(BF16)
    third = (rest - second.astype(F32)).astype(BF16)
    small = dot1(onehot, second, dims) + dot1(onehot, third, dims)
    return dot1(onehot, first, dims) + small


def normalize(values):
    center = values - jnp.mean(values, axis=-1, keepdims=True)
    inv = lax.rsqrt(jnp.mean(center * center, axis=-1, keepdims=True) + EPS)
    return center * inv, inv


def normalize_back(grad, gain, xhat, inv):
    scaled = grad * gain
    first = jnp.mean(scaled, axis=-1, keepdims=True)
    second = jnp.mean(scaled * xhat, axis=-1, keepdims=True)
    return inv * (scaled - first - xhat * second)


def slot_matrix(chosen_row, place_row, base, capacity):
    count = chosen_row.shape[1]
    column = (chosen_row ^ base) * capacity + place_row
    column = jnp.where(place_row >= 0, column, -1)
    slots = lax.broadcasted_iota(jnp.int32, (count, count), 0)
    return jnp.where(slots == column, 1.0, 0.0)


def pick(ref, index, size):
    return ref[pl.ds(pl.multiple_of(index * size, size), size), :]


def put_blocks(outs, value):
    size = outs[0].shape[0]
    for k, out in enumerate(outs):
        out[...] = value[k * size : (k + 1) * size]


def prep_kernel(capacity, relative, ids, chosen, place, cot, *slots_out):
    onehot = slot_matrix(chosen[...], place[...], ids[1] if relative else 0, capacity)
    put_blocks(slots_out, place_rows(onehot.astype(BF16), cot[...]))


def relative_rows(ids, x, out, blocks):
    size = x.shape[0] // blocks
    for d in range(blocks):
        out[d * size : (d + 1) * size, :] = pick(x, ids[2] ^ d, size)


def item_mask(ids, seg):
    row = [seg[pl.ds(ids[2] ^ d, 1), :] for d in range(seg.shape[0])]
    row = jnp.concatenate(row, axis=1).astype(F32)
    return row, jnp.transpose(jnp.broadcast_to(row, (8, row.shape[1])))[:, :1]


def head_mask(width, head):
    lane = lax.broadcasted_iota(jnp.int32, (1, width), 1)
    return jnp.where(lane // HEAD_DIM == head, 1.0, 0.0)


def attend_kernel(blocks, ids, seg, gain, x, w_q, w_k, w_v, w_o, ctx_out, *rest):
    part_out, (rel, query, key, value) = rest[:blocks], rest[blocks:]
    tokens, width = x.shape[0], w_q.shape[0]
    relative_rows(ids, x, rel, blocks)
    xhat, _ = normalize(rel[...])
    normed = halves(xhat * gain[...].reshape(1, -1))
    query[...] = dot3(normed, halves(w_q[...]), NT) * HEAD_DIM**-0.5
    key[...] = dot3(normed, halves(w_k[...]), NT)
    value[...] = dot3(normed, halves(w_v[...]), NT)
    row, column = item_mask(ids, seg)
    keys = halves(key[...])
    weight = halves(w_o[...])
    chunk = 256
    rows = tokens // blocks
    for c in range(tokens // chunk):
        here = slice(c * chunk, (c + 1) * chunk)
        allowed = column[here] == row
        total = None
        for h in range(width // HEAD_DIM):
            mask = head_mask(width, h)
            scores = dot3(halves(query[here, :] * mask), keys, NT)
            scores = jnp.where(allowed, scores, -1e30)
            expo = jnp.exp(scores - jnp.max(scores, axis=-1, keepdims=True))
            norm = 1.0 / jnp.sum(expo, axis=-1, keepdims=True)
            part = dot3(halves(expo), halves(value[...] * mask)) * norm
            total = part if total is None else total + part
        ctx_out[here, :] = total
        product = dot3(halves(total), weight)
        for i in range(chunk // rows):
            part_out[c * (chunk // rows) + i][...] = product[i * rows : (i + 1) * rows]


def up_weights_kernel(w_up, w_r, u_high, u_low):
    hidden = w_up.shape[1]
    u_high[:, :hidden], u_low[:, :hidden] = halves(w_up[...])
    pad = u_high.shape[1] - hidden - w_r.shape[0]
    route = jnp.concatenate([w_r[...], jnp.zeros((pad, w_r.shape[1]), F32)], axis=0)
    u_high[:, hidden:], u_low[:, hidden:] = halves(jnp.transpose(route))


def split_kernel(value, high, low):
    high[...], low[...] = halves(value[...])


def hidden_kernel(capacity, relative, blocks, ids, x, gain, chosen, place, *rest):
    parts, hidden_out, slots_out = rest[:blocks], rest[blocks], rest[blocks + 1 :]
    total = parts[0][...]
    for part in parts[1:]:
        total = total + part[...]
    hidden = pick(x, ids[2], hidden_out.shape[0]) + total
    hidden_out[...] = hidden
    xhat, _ = normalize(hidden)
    onehot = slot_matrix(chosen[...], place[...], ids[1] if relative else 0, capacity)
    put_blocks(slots_out, place_rows(onehot.astype(BF16), xhat * gain[...]))


def pair_rows(refs, d):
    return jnp.concatenate([refs[2 * d][...], refs[2 * d + 1][...]], axis=0)


def cot_kernel(blocks, w_down, *rest):
    cots, outs, (w_high, w_low) = rest[: 2 * blocks], rest[2 * blocks : 3 * blocks], rest[-2:]
    w_high[...], w_low[...] = halves(w_down[...])
    for d, out in enumerate(outs):
        out[...] = dot3(halves(pair_rows(cots, d)), (w_high[...], w_low[...]), NT)


def expert_kernel(
    ids, feed, feed_sib, act_grad, u_high, u_low, embed, temp,
    d_own, d_sib, ga_high, ga_low, dp_high, dp_low, slab,
):
    rows = feed.shape[0]
    hidden = act_grad.shape[1]
    experts, router = embed.shape
    wide = u_high.shape[1]
    tokens = jnp.concatenate([feed[...], feed_sib[...]], axis=0)
    split = halves(tokens)
    both = dot3(split, (u_high[...], u_low[...]))
    pre, routed = both[:, :hidden], both[:, hidden : hidden + router]
    da = act_grad[...]

    unit_inv = lax.rsqrt(jnp.sum(routed * routed, axis=-1, keepdims=True) + 1.0)
    unit = routed * unit_inv
    vectors = embed[...]
    vec_inv = lax.rsqrt(jnp.sum(vectors * vectors, axis=-1, keepdims=True) + 1.0)
    vec_unit = vectors * vec_inv
    scale = 1.0 / temp[0, 0]
    logits = dot_full(unit, vec_unit, NT) * scale
    soft = jnp.exp(logits - jnp.max(logits, axis=-1, keepdims=True))
    soft = soft / jnp.sum(soft, axis=-1, keepdims=True)
    mine = jnp.where(lax.broadcasted_iota(jnp.int32, (1, experts), 1) == ids[1], 1.0, 0.0)
    gate = jnp.sum(soft * mine, axis=-1, keepdims=True)

    square = pre * pre
    bend = jnp.tanh(GELU_C * (pre + GELU_A * pre * square))
    side = 0.5 * (1.0 + bend)
    act = pre * side
    slope = side + 0.5 * pre * (1.0 - bend * bend) * (GELU_C * (1.0 + 3.0 * GELU_A * square))
    d_gate = jnp.sum(act * da, axis=-1, keepdims=True)
    d_pre = da * gate * slope

    d_logits = d_gate * gate * (mine - soft)
    d_temp = -jnp.sum(jnp.sum(d_logits * logits, axis=-1, keepdims=True), axis=0, keepdims=True)
    d_raw = d_logits * scale
    d_unit = dot_full(d_raw, vec_unit)
    d_vec = dot_full(d_raw, unit, TN)
    d_vec = vec_inv * (d_vec - vec_unit * jnp.sum(d_vec * vec_unit, axis=-1, keepdims=True))
    d_routed = unit_inv * (d_unit - unit * jnp.sum(d_unit * unit, axis=-1, keepdims=True))

    grads = jnp.concatenate(
        [d_pre, d_routed, jnp.zeros((2 * rows, wide - hidden - router), F32)], axis=1
    )
    high, low = halves(grads)
    dp_high[...], dp_low[...] = high, low
    ga_high[...], ga_low[...] = halves(act * gate)
    d_feed = dot3((high, low), (u_high[...], u_low[...]), NT)
    d_own[...] = d_feed[:rows]
    d_sib[...] = d_feed[rows:]
    slab[...] = jnp.zeros_like(slab)
    proj = dot3(halves(d_routed), split, TN)
    slab[:router, :] = proj
    slab[router : router + experts, :router] = d_vec
    slab[router + experts : router + experts + 1, :1] = d_temp * scale


def expert_out_kernel(blocks, w_down, *rest):
    ga, outs, (w_high, w_low) = rest[: 2 * blocks], rest[2 * blocks : 3 * blocks + 1], rest[-2:]
    own, sib = outs[:blocks], outs[blocks]
    w_high[...], w_low[...] = halves(w_down[...])
    rows = own[0].shape[0]
    for d in range(blocks):
        part = dot3((ga[2 * d][...], ga[2 * d + 1][...]), (w_high[...], w_low[...]))
        own[d][...] = part[:rows]
        sib[d * rows : (d + 1) * rows, :] = part[rows:]


def expert_grad_kernel(blocks, *rest):
    cots, rest = rest[: 2 * blocks], rest[2 * blocks :]
    feeds, rest = rest[: 2 * blocks], rest[2 * blocks :]
    ga, rest = rest[: 2 * blocks], rest[2 * blocks :]
    dp, rest = rest[: 2 * blocks], rest[2 * blocks :]
    up_out, down_out = rest
    hidden = up_out.shape[1]
    for d in range(blocks):
        cot, feed = halves(pair_rows(cots, d)), halves(pair_rows(feeds, d))
        down = dot3((ga[2 * d][...], ga[2 * d + 1][...]), cot, TN)
        up = dot3(feed, (dp[2 * d][:, :hidden], dp[2 * d + 1][:, :hidden]), TN)
        down_out[...] = down if d == 0 else down_out[...] + down
        up_out[...] = up if d == 0 else up_out[...] + up


def sum_kernel(count, *rest):
    total = rest[0][...]
    for ref in rest[1:count]:
        total = total + ref[...]
    put_blocks(rest[count:], total)


def route_back_kernel(capacity, relative, blocks, ids, hidden, cot, gain, chosen, place, *rest):
    slabs, back, out = rest[:blocks], rest[blocks:-1], rest[-1]
    rows = hidden.shape[0]
    xhat, inv = normalize(hidden[...])
    onehot = slot_matrix(chosen[...], place[...], ids[1] if relative else 0, capacity)
    slots = jnp.concatenate([b[...] for b in back], axis=0)
    d_normed = place_rows(jnp.transpose(onehot).astype(BF16), slots)
    gain_row = jnp.sum(d_normed * xhat, axis=0, keepdims=True)
    out[:rows, :] = cot[...] + normalize_back(d_normed, gain[...], xhat, inv)
    slab = slabs[0][...]
    for other in slabs[1:]:
        slab = slab + other[...]
    lines = lax.broadcasted_iota(jnp.int32, (slab.shape[0], 1), 0)
    out[rows:, :] = jnp.where(lines == slab.shape[0] - 1, gain_row, slab)


def mixed_kernel(capacity, relative, ids, hidden, chosen, place, *rest):
    back, out = rest[:-1], rest[-1]
    onehot = slot_matrix(chosen[...], place[...], ids[1] if relative else 0, capacity)
    slots = jnp.concatenate([b[...] for b in back], axis=0)
    out[...] = hidden[...] + place_rows(jnp.transpose(onehot).astype(BF16), slots)


def again_kernel(blocks, ids, gain, x, w_q, w_k, w_v, w_o, xhat_out, high_out, low_out, *rest):
    made, split, rel = rest[:3], rest[3:-1], rest[-1]
    relative_rows(ids, x, rel, blocks)
    xhat, _ = normalize(rel[...])
    xhat_out[...] = xhat
    high, low = halves(xhat * gain[...].reshape(1, -1))
    high_out[...], low_out[...] = high, low
    for i, weight in enumerate((w_q, w_k, w_v)):
        split[2 * i][...], split[2 * i + 1][...] = halves(weight[...])
        product = dot3((high, low), (split[2 * i][...], split[2 * i + 1][...]), NT)
        made[i][...] = product * HEAD_DIM**-0.5 if i == 0 else product
    split[6][...], split[7][...] = halves(w_o[...])


def attend_back_kernel(blocks, first, ids, seg, q, k, v, o_high, o_low, *rest):
    d_hidden, rest = rest[:2], rest[2:]
    tokens, width = q.shape
    rows = tokens // blocks
    if first:
        before, xhat, split, rest = rest[:3], rest[3], rest[4:10], rest[10:]
        dn_out, (dq, dk, dv) = rest[:blocks], rest[blocks:]
        dq[: first * rows, :] = before[0][...]
        dk[...], dv[...] = before[1][...], before[2][...]
    else:
        dq, dk, dv = rest
    row, column = item_mask(ids, seg)
    keys, values = halves(k[...]), halves(v[...])
    here = slice(first * rows, (first + 2) * rows)
    allowed = column == row[:, here]
    grad = jnp.concatenate([d_hidden[0][:rows, :], d_hidden[1][:rows, :]], axis=0)
    d_here = dot3(halves(grad), (o_high[...], o_low[...]), NT)
    for h in range(width // HEAD_DIM):
        mask = head_mask(width, h)
        q_head = halves(q[here, :] * mask)
        d_head = halves(d_here * mask)
        scores = jnp.where(allowed, dot3(keys, q_head, NT), -1e30)
        expo = jnp.exp(scores - jnp.max(scores, axis=0, keepdims=True))
        probs = expo * (1.0 / jnp.sum(expo, axis=0, keepdims=True))
        d_probs = dot3(values, d_head, NT)
        delta = jnp.sum(probs * d_probs, axis=0, keepdims=True)
        d_scores = halves(probs * (d_probs - delta))
        d_value = dot3(halves(probs), d_head)
        d_key = dot3(d_scores, q_head)
        d_query = dot3(d_scores, halves(k[...] * (mask * HEAD_DIM**-0.5)), TN)
        new = h == 0 and not first
        dv[...] = d_value if new else dv[...] + d_value
        dk[...] = d_key if new else dk[...] + d_key
        dq[here, :] = d_query if h == 0 else dq[here, :] + d_query
    if not first:
        return
    d_normed = None
    for i, grad in enumerate((dq, dk, dv)):
        part = dot3(halves(grad[...]), (split[2 * i][...], split[2 * i + 1][...]))
        d_normed = part if d_normed is None else d_normed + part
    gain_row = jnp.sum(d_normed * xhat[...], axis=0, keepdims=True)
    for d, out in enumerate(dn_out):
        out[:rows, :] = d_normed[d * rows : (d + 1) * rows]
        out[rows:, :] = jnp.broadcast_to(gain_row, (8, gain_row.shape[1]))


def weight_grads_kernel(blocks, high, low, dq, dk, dv, ctx, *rest):
    d_hidden, outs = rest[:blocks], rest[blocks:]
    for grad, out in zip((dq, dk, dv), outs):
        out[...] = dot3(halves(grad[...]), (high[...], low[...]), TN)
    rows = ctx.shape[0] // blocks
    total, slab = None, None
    for d, part in enumerate(d_hidden):
        left = ctx[d * rows : (d + 1) * rows, :]
        product = dot3(halves(left), halves(part[:rows, :]), TN)
        total = product if total is None else total + product
        slab = part[rows:, :] if slab is None else slab + part[rows:, :]
    outs[3][...] = total
    outs[4][...] = slab


def norm_back_kernel(ids, x, gain, d_hidden, *rest):
    parts, (out, gain_out) = rest[:-2], rest[-2:]
    rows = out.shape[0]
    total = parts[0][...]
    for part in parts[1:]:
        total = total + part[...]
    xhat, inv = normalize(pick(x, ids[2], rows))
    out[...] = d_hidden[:rows, :] + normalize_back(total[:rows], gain[...], xhat, inv)
    gain_out[...] = total[rows:]


def place_blocks_kernel(ids, *rest):
    parts, out = rest[:-1], rest[-1]
    rows = parts[0].shape[0]
    for d, part in enumerate(parts):
        out[pl.ds(pl.multiple_of((ids[2] ^ d) * rows, rows), rows), :] = part[...]


def small_kernel(router, experts, slab, *rest):
    gains, (g1, g2, proj, vectors, temp) = rest[:-5], rest[-5:]
    gain = gains[0][:1, :]
    for other in gains[1:]:
        gain = gain + other[:1, :]
    last = slab.shape[0]
    g1[...] = gain
    g2[...] = slab[last - 1 : last, :]
    proj[...] = slab[:router, :]
    vectors[...] = slab[router : router + experts, :router]
    temp[...] = slab[router + experts : router + experts + 1, :1]


US = dict(
    attend=10, prep=2, up_weights=2, hidden=1, cot_act=4, expert=3, expert_out=1, out_split=1,
    sum_feed=0, expert_grad=10, route_back=0, again=6, sum_out=0, attend_back=6, weight_grads=0,
    norm_back=0, mixed=0,
)


class Far:
    def __init__(self, buffer, copy, arrives):
        self.buffer, self.copy, self.open = buffer, copy, arrives
        self.shape, self.dtype = buffer.shape, buffer.dtype
        self.next = []

    def wait(self):
        if self.open:
            self.copy.wait()
        self.open = False
        for one in self.next:
            one.copy.start()
        self.next = []

    def send(self):
        self.copy.start()
        self.open = True

    def __getitem__(self, index):
        self.wait()
        return self.buffer[index]

    def __setitem__(self, index, value):
        self.buffer[index] = value


def with_far(kernel, operands, results, early):
    count = len(operands) + len(results)

    def run(*refs):
        refs, buffers, sems = list(refs[: -count - 1]), refs[-count - 1 : -1], refs[-1]
        moved = []
        for j, i in enumerate((*operands, *results)):
            arrives = j < len(operands)
            ends = (refs[i], buffers[j]) if arrives else (buffers[j], refs[i])
            copy = pltpu.make_async_copy(*ends, sems.at[j])
            refs[i] = Far(buffers[j], copy, arrives)
            moved.append(refs[i])
        first = moved[: len(operands)]
        for one in first[:early] if early else first:
            one.copy.start()
        if early:
            first[early - 1].next = first[early:]
        kernel(*refs)
        for one in moved:
            one.wait()

    return run


def call(kernel, ids, args, outs, scratch=(), far=(), sent=(), early=0, name=None, us=1):
    whole, there = pl.BlockSpec(memory_space=pltpu.VMEM), pl.BlockSpec(memory_space=pltpu.HBM)
    lead = [] if ids is None else [ids]
    args = list(args)
    scratch_shapes = [pltpu.VMEM(s, d) for s, d in scratch]
    if far or sent:
        first = len(lead) + len(args)
        scratch_shapes += [pltpu.VMEM(args[i].shape, args[i].dtype) for i in far]
        scratch_shapes += [pltpu.VMEM(*outs[i]) for i in sent]
        scratch_shapes.append(pltpu.SemaphoreType.DMA((len(far) + len(sent),)))
        kernel = with_far(kernel, [len(lead) + i for i in far], [first + i for i in sent], early)
        for i in far:
            args[i] = pltpu.with_memory_space_constraint(args[i], pltpu.HBM)
    return pl.pallas_call(
        kernel,
        out_shape=[
            pltpu.HBM(s, d) if i in sent else jax.ShapeDtypeStruct(s, d)
            for i, (s, d) in enumerate(outs)
        ],
        in_specs=[pl.BlockSpec(memory_space=pltpu.SMEM)] * len(lead)
        + [there if i in far else whole for i in range(len(args))],
        out_specs=[there if i in sent else whole for i in range(len(outs))],
        scratch_shapes=scratch_shapes,
        compiler_params=pltpu.CompilerParams(vmem_limit_bytes=VMEM_LIMIT),
        cost_estimate=cost(us),
        name=name,
    )(*lead, *args)


def cost(us):
    return pl.CostEstimate(flops=int(us * 1.1e9), bytes_accessed=0, transcendentals=0)


def swap(value, axis, shift):
    count = lax.axis_size(axis)
    return lax.ppermute(value, axis, [(i, i ^ shift) for i in range(count)])


def after(values, *done):
    return lax.optimization_barrier((values, done))[0]


def to_planes(blocks):
    if len(blocks) > 1:
        return [blocks[0]] + [swap(b, "ep", k) for k, b in enumerate(blocks) if k]
    return [exchange(blocks[0], "ep")]


def exchange(value, axis):
    count = lax.axis_size(axis)
    split = value.reshape(count, -1, value.shape[-1])
    moved = lax.all_to_all(split, axis, split_axis=0, concat_axis=0, tiled=True)
    return moved.reshape(value.shape)


def gather_blocks(parts):
    return [parts[0]] + [swap(p, "tp", d) for d, p in enumerate(parts) if d]


def gather_tp(block):
    return [block] + [swap(block, "tp", d) for d in range(1, lax.axis_size("tp"))]


def with_core(same):
    return [r for b in same for r in (b, swap(b, "dp", 1))]


def body(
    x, passage, gain1, w_q, w_k, w_v, w_o, gain2, w_r, embed, temp, w_up, w_down, chosen, place, cot
):
    blocks, planes = lax.axis_size("tp"), lax.axis_size("ep")
    ids = jnp.stack([lax.axis_index("dp"), lax.axis_index("ep"), lax.axis_index("tp")])
    ids = ids.astype(jnp.int32)
    tokens, width = x.shape
    rows, local = tokens // blocks, w_q.shape[1]
    w_q, w_k, w_v, w_r = w_q.T, w_k.T, w_v.T, w_r.T
    experts, router = embed.shape
    hidden_units = w_up.shape[2]
    capacity = rows // experts
    pieces = planes if planes <= 4 else 1
    relative = pieces > 1
    slot_shapes = [((rows // pieces, width), F32)] * pieces
    wide = 512
    slab_rows = -(-(router + experts + 2) // 8) * 8
    w_up, w_down = w_up[0], w_down[0]
    chosen, place = chosen.reshape(1, rows), place.reshape(1, rows)
    gain1_line, gain1, gain2 = gain1, gain1.reshape(1, width), gain2.reshape(1, width)
    seg = passage.reshape(blocks, rows)
    temp = temp.reshape(1, 1)

    ctx, *parts = call(
        functools.partial(attend_kernel, blocks), ids, [seg, gain1_line, x, w_q, w_k, w_v, w_o],
        [((tokens, local), F32)] + [((rows, width), F32)] * blocks,
        [((tokens, width), F32)] + [((tokens, local), F32)] * 3,
        far=(0, 1, 2, 3, 4, 5, 6), early=3, name="attend", us=US["attend"],
    )
    got = gather_blocks(parts)
    cot_slots = call(
        functools.partial(prep_kernel, capacity, relative), ids,
        [chosen, place, after(cot, *parts)], slot_shapes, far=(0, 1, 2), name="prep",
        us=US["prep"],
    )
    cot_slots = to_planes(cot_slots)
    u_high, u_low = call(
        up_weights_kernel, None, [w_up, w_r], [((width, wide), BF16)] * 2, name="up_weights",
        us=US["up_weights"],
    )
    cots = gather_tp(jnp.concatenate(cot_slots, axis=0))
    hidden, *slots = call(
        functools.partial(hidden_kernel, capacity, relative, blocks), ids,
        [x, gain2, chosen, place, *after(got, u_high)], [((rows, width), F32)] + slot_shapes,
        name="hidden", us=US["hidden"],
    )

    same = gather_tp(jnp.concatenate(to_planes(slots), axis=0))
    feeds = with_core(same[:1])
    cots = with_core(after(cots, same[0]))
    act_grads = call(
        functools.partial(cot_kernel, blocks), None, [w_down, *after(cots, *feeds)],
        [((2 * rows, hidden_units), F32)] * blocks, [((hidden_units, width), BF16)] * 2,
        name="cot_act", us=US["cot_act"],
    )
    ga, dp, slabs, parts = [], [], [], []
    for d in range(blocks):
        if d:
            feeds += with_core(same[d : d + 1])
        pair = after(feeds[2 * d : 2 * d + 2], *slabs[-1:])
        d_own, d_sib, ga_high, ga_low, dp_high, dp_low, slab = call(
            expert_kernel, ids, [*pair, act_grads[d], u_high, u_low, embed, temp],
            [((rows, width), F32)] * 2
            + [((2 * rows, hidden_units), BF16)] * 2
            + [((2 * rows, wide), BF16)] * 2
            + [((slab_rows, width), F32)],
            name="expert", us=US["expert"],
        )
        ga += [ga_high, ga_low]
        dp += [dp_high, dp_low]
        slabs.append(slab)
        total = d_own + swap(d_sib, "dp", 1)
        parts.append(total if d == 0 else swap(total, "tp", d))
    pieces_back = call(
        functools.partial(sum_kernel, blocks), None, parts, slot_shapes, name="sum_feed",
        us=US["sum_feed"],
    )
    back = to_planes(pieces_back)
    grad_up, grad_down = call(
        functools.partial(expert_grad_kernel, blocks), None,
        [*after(cots, *pieces_back), *feeds, *ga, *dp],
        [((width, hidden_units), F32), ((hidden_units, width), F32)],
        name="expert_grad", us=US["expert_grad"],
    )
    (d_hidden,) = call(
        functools.partial(route_back_kernel, capacity, relative, blocks), ids,
        [hidden, cot, gain2, chosen, place, *slabs, *after(back, grad_up)],
        [((rows + slab_rows, width), F32)], name="route_back", us=US["route_back"],
    )

    d_hiddens = gather_tp(d_hidden)
    xhat, high, low, q, k, v, *split = call(
        functools.partial(again_kernel, blocks), ids,
        [gain1_line, after(x, d_hidden), w_q, w_k, w_v, w_o],
        [((tokens, width), F32)] + [((tokens, width), BF16)] * 2 + [((tokens, local), F32)] * 3
        + [((local, width), BF16)] * 8,
        [((tokens, width), F32)], far=(0, 1, 2, 3, 4, 5), early=2, name="again", us=US["again"],
    )
    *own, sib = call(
        functools.partial(expert_out_kernel, blocks), None, [after(w_down, high), *ga],
        [((rows, width), F32)] * blocks + [((blocks * rows, width), F32)],
        [((hidden_units, width), BF16)] * 2, name="expert_out", us=US["expert_out"],
    )
    half_grads = call(
        functools.partial(attend_back_kernel, blocks, 0), ids,
        [seg, q, k, v, *split[6:], *after(d_hiddens[:2], sib)],
        [((2 * rows, local), F32)] + [((tokens, local), F32)] * 2, name="attend_back",
        us=US["attend_back"],
    )
    *dn, dq, dk, dv = call(
        functools.partial(attend_back_kernel, blocks, 2), ids,
        [seg, q, k, v, *split[6:], *after(d_hiddens[2:], *half_grads), *half_grads, xhat]
        + split[:6],
        [((rows + 8, width), F32)] * blocks + [((tokens, local), F32)] * 3,
        name="attend_back_rest", us=US["attend_back"],
    )
    dn_got = gather_blocks(dn)
    grads = call(
        functools.partial(weight_grads_kernel, blocks), None,
        [high, low, dq, dk, dv, ctx, *d_hiddens],
        [((local, width), F32)] * 4 + [((slab_rows, width), F32)],
        name="weight_grads", us=US["weight_grads"],
    )
    grad_q, grad_k, grad_v, grad_o, small = lax.psum(tuple(grads), ("dp", "ep"))
    d_x, gain = call(
        norm_back_kernel, ids, [x, gain1, d_hidden, *after(dn_got, *grads)],
        [((rows, width), F32), ((8, width), F32)], name="norm_back", us=US["norm_back"],
    )
    d_xs = gather_tp(d_x)
    sib = swap(after(sib, d_x), "dp", 1)
    parts_out = []
    for d in range(blocks):
        total = own[d] + sib[d * rows : (d + 1) * rows]
        parts_out.append(total if d == 0 else swap(total, "tp", d))
    out_pieces = call(
        functools.partial(sum_kernel, blocks), None, parts_out, slot_shapes, name="sum_out",
        us=US["sum_out"],
    )
    out_slots = to_planes(out_pieces)
    (mixed,) = call(
        functools.partial(mixed_kernel, capacity, relative), ids,
        [hidden, chosen, place, *out_slots], [((rows, width), F32)],
        name="mixed", us=US["mixed"],
    )
    (grad_tokens,) = call(
        place_blocks_kernel, ids, d_xs, [((tokens, width), F32)],
        name="grad_tokens", us=0,
    )
    gain = gain + swap(after(gain, mixed), "dp", 1)
    gains = [gain] + [swap(gain, "ep", k) for k in range(1, planes)] if relative else [lax.psum(gain, "ep")]
    grad_g1, grad_g2, grad_proj, grad_embed, grad_temp = call(
        functools.partial(small_kernel, router, experts), None, [after(small, *gains), *gains],
        [((1, width), F32), ((1, width), F32), ((router, width), F32)]
        + [((experts, router), F32), ((1, 1), F32)],
        name="small", us=0,
    )
    return (
        mixed,
        grad_tokens,
        grad_g1.reshape(width),
        grad_q.T,
        grad_k.T,
        grad_v.T,
        grad_o,
        grad_g2.reshape(width),
        grad_proj.T,
        grad_embed,
        grad_temp.reshape(1),
        grad_up[None],
        grad_down[None],
    )


def solution(mesh):
    in_specs = (
        P(("dp", "ep"), None),
        P(("dp", "ep")),
        P(),
        P(None, "tp"),
        P(None, "tp"),
        P(None, "tp"),
        P("tp", None),
        P(),
        P(),
        P(),
        P(),
        P("ep", None, ("dp", "tp")),
        P("ep", ("dp", "tp"), None),
        P(("dp", "ep", "tp")),
        P(("dp", "ep", "tp")),
        P(("dp", "ep", "tp"), None),
    )
    out_specs = (
        P(("dp", "ep", "tp"), None),
        P(("dp", "ep"), None),
        P(),
        P(None, "tp"),
        P(None, "tp"),
        P(None, "tp"),
        P("tp", None),
        P(),
        P(),
        P(),
        P(),
        P("ep", None, ("dp", "tp")),
        P("ep", ("dp", "tp"), None),
    )
    return jax.shard_map(body, mesh=mesh, in_specs=in_specs, out_specs=out_specs, check_vma=False)
```

```python
import functools

import jax
import jax.numpy as jnp
from jax import lax
from jax.experimental import pallas as pl
from jax.experimental.pallas import tpu as pltpu
from jax.sharding import PartitionSpec as P

HEAD_DIM = 64
EPS = 1e-05
F32 = jnp.float32
BF16 = jnp.bfloat16
NN = (((1,), (0,)), ((), ()))
NT = (((1,), (1,)), ((), ()))
TN = (((0,), (0,)), ((), ()))
VMEM_LIMIT = 14 * 1024 * 1024
GELU_C = 0.7978845608028654
GELU_A = 0.044715


def halves(value):
    high = value.astype(BF16)
    return high, (value - high.astype(F32)).astype(BF16)


def dot1(left, right, dims):
    return lax.dot_general(left, right, dims, preferred_element_type=F32)


def dot3(left, right, dims=NN):
    small = dot1(left[0], right[1], dims) + dot1(left[1], right[0], dims)
    return small + dot1(left[0], right[0], dims)


def dot_full(left, right, dims=NN):
    return lax.dot_general(
        left, right, dims, precision=lax.Precision.HIGHEST, preferred_element_type=F32
    )


def place_rows(onehot, value, dims=NN):
    first = value.astype(BF16)
    rest = value - first.astype(F32)
    second = rest.astype(BF16)
    third = (rest - second.astype(F32)).astype(BF16)
    small = dot1(onehot, second, dims) + dot1(onehot, third, dims)
    return dot1(onehot, first, dims) + small


def normalize(values):
    center = values - jnp.mean(values, axis=-1, keepdims=True)
    inv = lax.rsqrt(jnp.mean(center * center, axis=-1, keepdims=True) + EPS)
    return center * inv, inv


def normalize_back(grad, gain, xhat, inv):
    scaled = grad * gain
    first = jnp.mean(scaled, axis=-1, keepdims=True)
    second = jnp.mean(scaled * xhat, axis=-1, keepdims=True)
    return inv * (scaled - first - xhat * second)


def slot_matrix(chosen_row, place_row, base, capacity):
    count = chosen_row.shape[1]
    column = (chosen_row ^ base) * capacity + place_row
    column = jnp.where(place_row >= 0, column, -1)
    slots = lax.broadcasted_iota(jnp.int32, (count, count), 0)
    return jnp.where(slots == column, 1.0, 0.0)


def pick(ref, index, size):
    return ref[pl.ds(pl.multiple_of(index * size, size), size), :]


def put_blocks(outs, value):
    size = outs[0].shape[0]
    for k, out in enumerate(outs):
        out[...] = value[k * size : (k + 1) * size]


def prep_kernel(capacity, relative, ids, chosen, place, cot, *slots_out):
    onehot = slot_matrix(chosen[...], place[...], ids[1] if relative else 0, capacity)
    put_blocks(slots_out, place_rows(onehot.astype(BF16), cot[...]))


def relative_rows(ids, x, out, blocks):
    size = x.shape[0] // blocks
    for d in range(blocks):
        out[d * size : (d + 1) * size, :] = pick(x, ids[2] ^ d, size)


def item_mask(ids, seg):
    row = [seg[pl.ds(ids[2] ^ d, 1), :] for d in range(seg.shape[0])]
    row = jnp.concatenate(row, axis=1).astype(F32)
    return row, jnp.transpose(jnp.broadcast_to(row, (8, row.shape[1])))[:, :1]


def head_mask(width, head):
    lane = lax.broadcasted_iota(jnp.int32, (1, width), 1)
    return jnp.where(lane // HEAD_DIM == head, 1.0, 0.0)


def attend_kernel(blocks, ids, seg, gain, x, w_q, w_k, w_v, w_o, ctx_out, *rest):
    part_out, (rel, query, key, value) = rest[:blocks], rest[blocks:]
    tokens, width = x.shape[0], w_q.shape[0]
    relative_rows(ids, x, rel, blocks)
    xhat, _ = normalize(rel[...])
    normed = halves(xhat * gain[...].reshape(1, -1))
    query[...] = dot3(normed, halves(w_q[...]), NT) * HEAD_DIM**-0.5
    key[...] = dot3(normed, halves(w_k[...]), NT)
    value[...] = dot3(normed, halves(w_v[...]), NT)
    row, column = item_mask(ids, seg)
    keys = halves(key[...])
    weight = halves(w_o[...])
    chunk = 256
    rows = tokens // blocks
    for c in range(tokens // chunk):
        here = slice(c * chunk, (c + 1) * chunk)
        allowed = column[here] == row
        total = None
        for h in range(width // HEAD_DIM):
            mask = head_mask(width, h)
            scores = dot3(halves(query[here, :] * mask), keys, NT)
            scores = jnp.where(allowed, scores, -1e30)
            expo = jnp.exp(scores - jnp.max(scores, axis=-1, keepdims=True))
            norm = 1.0 / jnp.sum(expo, axis=-1, keepdims=True)
            part = dot3(halves(expo), halves(value[...] * mask)) * norm
            total = part if total is None else total + part
        ctx_out[here, :] = total
        product = dot3(halves(total), weight)
        for i in range(chunk // rows):
            part_out[c * (chunk // rows) + i][...] = product[i * rows : (i + 1) * rows]


def up_weights_kernel(w_up, w_up_sib, w_r, u_high, u_low):
    hidden = w_up.shape[1]
    u_high[:, :hidden], u_low[:, :hidden] = halves(w_up[...])
    u_high[:, hidden : 2 * hidden], u_low[:, hidden : 2 * hidden] = halves(w_up_sib[...])
    pad = u_high.shape[1] - 2 * hidden - w_r.shape[0]
    route = jnp.concatenate([w_r[...], jnp.zeros((pad, w_r.shape[1]), F32)], axis=0)
    u_high[:, 2 * hidden :], u_low[:, 2 * hidden :] = halves(jnp.transpose(route))


def hidden_kernel(capacity, relative, blocks, ids, x, gain, chosen, place, *rest):
    parts, hidden_out, slots_out = rest[:blocks], rest[blocks], rest[blocks + 1 :]
    total = parts[0][...]
    for part in parts[1:]:
        total = total + part[...]
    hidden = pick(x, ids[2], hidden_out.shape[0]) + total
    hidden_out[...] = hidden
    xhat, _ = normalize(hidden)
    onehot = slot_matrix(chosen[...], place[...], ids[1] if relative else 0, capacity)
    put_blocks(slots_out, place_rows(onehot.astype(BF16), xhat * gain[...]))


def stack(refs):
    return jnp.concatenate([ref[...] for ref in refs], axis=0)


def pair_refs(refs, pairs):
    return [refs[2 * d : 2 * d + 2] for d in range(pairs - 1)] + [refs[2 * pairs - 2 :]]


def cot_kernel(blocks, w_down, w_down_sib, *rest):
    w_high, w_low = rest[-2:]
    pairs = blocks // 2
    cots, outs = pair_refs(rest[: -2 - pairs], pairs), rest[-2 - pairs : -2]
    hidden = w_down.shape[0]
    w_high[:hidden, :], w_low[:hidden, :] = halves(w_down[...])
    w_high[hidden:, :], w_low[hidden:, :] = halves(w_down_sib[...])
    for refs, out in zip(cots, outs):
        out[...] = dot3(halves(stack(refs)), (w_high[...], w_low[...]), NT)


def expert_kernel(ids, act_grad, u_high, u_low, embed, temp, *rest):
    feeds, (d_feed_out, d_next_out, ga_high, ga_low, dp_high, dp_low, slab) = rest[:-7], rest[-7:]
    rows = d_feed_out.shape[0]
    hidden = act_grad.shape[1]
    experts, router = embed.shape
    wide = u_high.shape[1]
    split = halves(stack(feeds))
    both = dot3(split, (u_high[...], u_low[...]))
    pre, routed = both[:, :hidden], both[:, hidden : hidden + router]
    da = act_grad[...]

    unit_inv = lax.rsqrt(jnp.sum(routed * routed, axis=-1, keepdims=True) + 1.0)
    unit = routed * unit_inv
    vectors = embed[...]
    vec_inv = lax.rsqrt(jnp.sum(vectors * vectors, axis=-1, keepdims=True) + 1.0)
    vec_unit = vectors * vec_inv
    scale = 1.0 / temp[0, 0]
    logits = dot_full(unit, vec_unit, NT) * scale
    soft = jnp.exp(logits - jnp.max(logits, axis=-1, keepdims=True))
    soft = soft / jnp.sum(soft, axis=-1, keepdims=True)
    mine = jnp.where(lax.broadcasted_iota(jnp.int32, (1, experts), 1) == ids[1], 1.0, 0.0)
    gate = jnp.sum(soft * mine, axis=-1, keepdims=True)

    square = pre * pre
    bend = jnp.tanh(GELU_C * (pre + GELU_A * pre * square))
    side = 0.5 * (1.0 + bend)
    act = pre * side
    slope = side + 0.5 * pre * (1.0 - bend * bend) * (GELU_C * (1.0 + 3.0 * GELU_A * square))
    d_gate = jnp.sum(act * da, axis=-1, keepdims=True)
    d_pre = da * gate * slope

    d_logits = d_gate * gate * (mine - soft)
    d_temp = -jnp.sum(jnp.sum(d_logits * logits, axis=-1, keepdims=True), axis=0, keepdims=True)
    d_raw = d_logits * scale
    d_unit = dot_full(d_raw, vec_unit)
    d_vec = dot_full(d_raw, unit, TN)
    d_vec = vec_inv * (d_vec - vec_unit * jnp.sum(d_vec * vec_unit, axis=-1, keepdims=True))
    d_routed = unit_inv * (d_unit - unit * jnp.sum(d_unit * unit, axis=-1, keepdims=True))

    grads = jnp.concatenate(
        [d_pre, d_routed, jnp.zeros((2 * rows, wide - hidden - router), F32)], axis=1
    )
    high, low = halves(grads)
    dp_high[...], dp_low[...] = high, low
    ga_high[...], ga_low[...] = halves(act * gate)
    d_feed = dot3((high, low), (u_high[...], u_low[...]), NT)
    d_feed_out[...] = d_feed[:rows]
    d_next_out[...] = d_feed[rows:]
    slab[...] = jnp.zeros_like(slab)
    proj = dot3(halves(d_routed), split, TN)
    slab[:router, :] = proj
    slab[router : router + experts, :router] = d_vec
    slab[router + experts : router + experts + 1, :1] = d_temp * scale


def expert_out_kernel(blocks, w_high, w_low, *rest):
    ga, outs = rest[:blocks], rest[blocks:]
    rows = outs[0].shape[0]
    for d in range(blocks // 2):
        part = dot3((ga[2 * d][...], ga[2 * d + 1][...]), (w_high[...], w_low[...]))
        outs[2 * d][...] = part[:rows]
        outs[2 * d + 1][...] = part[rows:]


def expert_grad_kernel(blocks, *rest):
    rest, (up_out, up_sib, down_out, down_sib) = rest[:-4], rest[-4:]
    rest, ga, dp = rest[: -2 * blocks], rest[-2 * blocks : -blocks], rest[-blocks:]
    cots = pair_refs(rest[: len(rest) // 2], blocks // 2)
    feeds = pair_refs(rest[len(rest) // 2 :], blocks // 2)
    hidden = up_out.shape[1]
    for d in range(blocks // 2):
        cot, feed = halves(stack(cots[d])), halves(stack(feeds[d]))
        for i, (up, down) in enumerate(((up_out, down_out), (up_sib, down_sib))):
            part = slice(i * hidden, (i + 1) * hidden)
            down_part = dot3((ga[2 * d][:, part], ga[2 * d + 1][:, part]), cot, TN)
            up_part = dot3(feed, (dp[2 * d][:, part], dp[2 * d + 1][:, part]), TN)
            down[...] = down_part if d == 0 else down[...] + down_part
            up[...] = up_part if d == 0 else up[...] + up_part


def sum_kernel(count, *rest):
    total = rest[0][...]
    for ref in rest[1:count]:
        total = total + ref[...]
    put_blocks(rest[count:], total)


def route_back_kernel(capacity, relative, blocks, ids, hidden, cot, gain, chosen, place, *rest):
    slabs, back, out = rest[: blocks // 2], rest[blocks // 2 : -1], rest[-1]
    rows = hidden.shape[0]
    xhat, inv = normalize(hidden[...])
    onehot = slot_matrix(chosen[...], place[...], ids[1] if relative else 0, capacity)
    slots = jnp.concatenate([b[...] for b in back], axis=0)
    d_normed = place_rows(jnp.transpose(onehot).astype(BF16), slots)
    gain_row = jnp.sum(d_normed * xhat, axis=0, keepdims=True)
    out[:rows, :] = cot[...] + normalize_back(d_normed, gain[...], xhat, inv)
    slab = slabs[0][...]
    for other in slabs[1:]:
        slab = slab + other[...]
    lines = lax.broadcasted_iota(jnp.int32, (slab.shape[0], 1), 0)
    out[rows:, :] = jnp.where(lines == slab.shape[0] - 1, gain_row, slab)


def mixed_kernel(capacity, relative, ids, hidden, chosen, place, *rest):
    back, out = rest[:-1], rest[-1]
    onehot = slot_matrix(chosen[...], place[...], ids[1] if relative else 0, capacity)
    slots = jnp.concatenate([b[...] for b in back], axis=0)
    out[...] = hidden[...] + place_rows(jnp.transpose(onehot).astype(BF16), slots)


def again_kernel(blocks, ids, gain, x, w_q, w_k, w_v, w_o, xhat_out, high_out, low_out, *rest):
    made, split, rel = rest[:3], rest[3:-1], rest[-1]
    relative_rows(ids, x, rel, blocks)
    xhat, _ = normalize(rel[...])
    xhat_out[...] = xhat
    high, low = halves(xhat * gain[...].reshape(1, -1))
    high_out[...], low_out[...] = high, low
    for i, weight in enumerate((w_q, w_k, w_v)):
        split[2 * i][...], split[2 * i + 1][...] = halves(weight[...])
        product = dot3((high, low), (split[2 * i][...], split[2 * i + 1][...]), NT)
        made[i][...] = product * HEAD_DIM**-0.5 if i == 0 else product
    split[6][...], split[7][...] = halves(w_o[...])


def token_rows(refs, rows, blocks):
    whole = [ref[...] for ref in refs[: blocks - 1]] + [stack(refs[blocks - 1 :])]
    others = whole[0][rows:]
    for value in whole[1:]:
        others = others + value[rows:]
    return [value[:rows] for value in whole], others


def attend_back_kernel(blocks, first, ids, seg, q, k, v, o_high, o_low, *rest):
    tokens, width = q.shape
    rows = tokens // blocks
    count = len(rest) - (10 + blocks + 4 if first else 3)
    d_hidden, rest = rest[:count], rest[count:]
    if first:
        before, xhat, split, rest = rest[:3], rest[3], rest[4:10], rest[10:]
        dn_out, (gain_out, dq, dk, dv) = rest[:blocks], rest[blocks:]
        dq[: first * rows, :] = before[0][...]
        dk[...], dv[...] = before[1][...], before[2][...]
    else:
        dq, dk, dv = rest
    row, column = item_mask(ids, seg)
    keys, values = halves(k[...]), halves(v[...])
    here = slice(first * rows, (first + 2) * rows)
    allowed = column == row[:, here]
    grad, _ = token_rows(d_hidden, rows, 2)
    grad = jnp.concatenate(grad, axis=0)
    d_here = dot3(halves(grad), (o_high[...], o_low[...]), NT)
    for h in range(width // HEAD_DIM):
        mask = head_mask(width, h)
        q_head = halves(q[here, :] * mask)
        d_head = halves(d_here * mask)
        scores = jnp.where(allowed, dot3(keys, q_head, NT), -1e30)
        expo = jnp.exp(scores - jnp.max(scores, axis=0, keepdims=True))
        probs = expo * (1.0 / jnp.sum(expo, axis=0, keepdims=True))
        d_probs = dot3(values, d_head, NT)
        delta = jnp.sum(probs * d_probs, axis=0, keepdims=True)
        d_scores = halves(probs * (d_probs - delta))
        d_value = dot3(halves(probs), d_head)
        d_key = dot3(d_scores, q_head)
        d_query = dot3(d_scores, halves(k[...] * (mask * HEAD_DIM**-0.5)), TN)
        new = h == 0 and not first
        dv[...] = d_value if new else dv[...] + d_value
        dk[...] = d_key if new else dk[...] + d_key
        dq[here, :] = d_query if h == 0 else dq[here, :] + d_query
    if not first:
        return
    d_normed = None
    for i, grad in enumerate((dq, dk, dv)):
        part = dot3(halves(grad[...]), (split[2 * i][...], split[2 * i + 1][...]))
        d_normed = part if d_normed is None else d_normed + part
    put_blocks(dn_out, d_normed)
    gain_out[...] = jnp.sum(d_normed * xhat[...], axis=0, keepdims=True)


def share_rows(count, slab_rows, shares):
    each = -(-slab_rows // shares)
    return count // shares, each, count // shares + -(-(each + 1) // 8) * 8


def weight_grads_kernel(blocks, shares, ids, high, low, dq, dk, dv, ctx, gain, *rest):
    d_hidden, (own, sib, grads) = rest[:-3], rest[-3:]
    width = dq.shape[1]
    for i, grad in enumerate((dq, dk, dv)):
        grads[i * width : (i + 1) * width, :] = dot3(halves(grad[...]), (high[...], low[...]), TN)
    rows = ctx.shape[0] // blocks
    total = None
    d_rows, slab = token_rows(d_hidden, rows, blocks)
    for d, part in enumerate(d_rows):
        left = ctx[d * rows : (d + 1) * rows, :]
        product = dot3(halves(left), halves(part), TN)
        total = product if total is None else total + product
    grads[3 * width : 4 * width, :] = total
    count = slab.shape[0]
    weights, each, stride = share_rows(4 * width, count, shares)
    for i in range(shares):
        few = max(min(each, count - i * each), 0)
        start = 4 * width + i * (stride - weights)
        if few:
            grads[start : start + few, :] = slab[i * each : i * each + few]
        stop = start + stride - weights
        grads[stop - 1 : stop, :] = gain[...]
    for c, out in enumerate((own, sib)):
        for j in range(shares // 2):
            index = (ids[0] ^ c) * (shares // 2) + j
            start = pl.multiple_of(index * weights, 8)
            out[j * stride : j * stride + weights, :] = grads[pl.ds(start, weights), :]
            start = pl.multiple_of(4 * width + index * (stride - weights), 8)
            out[j * stride + weights : (j + 1) * stride, :] = grads[pl.ds(start, stride - weights), :]


def join_kernel(count, *rest):
    total = rest[0][...]
    for ref in rest[1:count]:
        total = total + ref[...]
    rest[-2][...] = total
    rest[-1][...] = total[-8:]


def norm_back_kernel(ids, x, gain, d_hidden, *rest):
    parts, out = rest[:-1], rest[-1]
    rows = out.shape[0]
    total = parts[0][...]
    for part in parts[1:]:
        total = total + part[...]
    xhat, inv = normalize(pick(x, ids[2], rows))
    out[...] = d_hidden[:rows, :] + normalize_back(total, gain[...], xhat, inv)


def place_blocks_kernel(ids, *rest):
    parts, out = rest[:-1], rest[-1]
    rows = parts[0].shape[0]
    blocks = out.shape[0] // rows
    for d in range(blocks):
        value = parts[d][...] if d < blocks - 1 else stack(parts[d:])
        out[pl.ds(pl.multiple_of((ids[2] ^ d) * rows, rows), rows), :] = value


def split_planes_kernel(ids, own, other, *outs):
    size = outs[0].shape[0]
    for k, out in enumerate(outs):
        here = pl.ds(pl.multiple_of((ids[1] ^ k) * size, 8), size)
        out[...] = own[here, :] + other[here, :]


def finish_kernel(router, experts, pieces, shares, ids, *rest):
    parts, gains, rest = rest[: 2 * pieces], rest[2 * pieces : -11], rest[-11:]
    q_out, k_out, v_out, o_out, g1, g2, proj, vectors, temp, full, small = rest
    width = q_out.shape[0]
    count = -(-(router + experts + 2) // 8) * 8
    weights, each, stride = share_rows(4 * width, count, shares)
    many = shares // (2 * pieces)
    for c in range(2):
        for k in range(pieces):
            index = (ids[0] ^ c) * pieces + (ids[1] ^ k if pieces > 1 else 0)
            part = parts[c * pieces + k]
            for j in range(many):
                here = pl.multiple_of((index * many + j) * weights, 8)
                full[pl.ds(here, weights), :] = part[j * stride : j * stride + weights, :]
                here = pl.multiple_of((index * many + j) * (stride - weights), 8)
                full_small = part[j * stride + weights : (j + 1) * stride, :]
                small[pl.ds(here, stride - weights), :] = full_small
    for i in range(1, shares):
        few = max(min(each, count - i * each), 0)
        start = i * (stride - weights)
        if few:
            small[i * each : i * each + few, :] = small[start : start + few, :]
    put_blocks((q_out, k_out, v_out, o_out), full)
    gain = gains[0][-1:, :]
    for other in gains[1:]:
        gain = gain + other[-1:, :]
    g1[...] = gain.reshape(-1)
    g2[...] = small[count - 1 : count, :].reshape(-1)
    proj[...] = small[:router, :]
    vectors[...] = small[router : router + experts, :router]
    temp[...] = small[router + experts : router + experts + 1, :1]


US = dict(
    attend=10, prep=2, up_weights=2, hidden=1, cot_act=4, expert=3, expert_out=1, out_split=1,
    sum_feed=0, expert_grad=10, route_back=0, again=6, sum_out=0, attend_back=6, weight_grads=0,
    norm_back=0, mixed=0, join=0,
)


class Far:
    def __init__(self, buffer, copy, arrives):
        self.buffer, self.copy, self.open = buffer, copy, arrives
        self.shape, self.dtype = buffer.shape, buffer.dtype
        self.next = []

    def wait(self):
        if self.open:
            self.copy.wait()
        self.open = False
        for one in self.next:
            one.copy.start()
        self.next = []

    def send(self):
        self.copy.start()
        self.open = True

    def __getitem__(self, index):
        self.wait()
        return self.buffer[index]

    def __setitem__(self, index, value):
        self.buffer[index] = value


def with_far(kernel, operands, results, early):
    count = len(operands) + len(results)

    def run(*refs):
        refs, buffers, sems = list(refs[: -count - 1]), refs[-count - 1 : -1], refs[-1]
        moved = []
        for j, i in enumerate((*operands, *results)):
            arrives = j < len(operands)
            ends = (refs[i], buffers[j]) if arrives else (buffers[j], refs[i])
            copy = pltpu.make_async_copy(*ends, sems.at[j])
            refs[i] = Far(buffers[j], copy, arrives)
            moved.append(refs[i])
        first = moved[: len(operands)]
        for one in first[:early] if early else first:
            one.copy.start()
        if early:
            first[early - 1].next = first[early:]
        kernel(*refs)
        for one in moved:
            one.wait()

    return run


def call(kernel, ids, args, outs, scratch=(), far=(), sent=(), early=0, name=None, us=1):
    whole, there = pl.BlockSpec(memory_space=pltpu.VMEM), pl.BlockSpec(memory_space=pltpu.HBM)
    lead = [] if ids is None else [ids]
    args = list(args)
    scratch_shapes = [pltpu.VMEM(s, d) for s, d in scratch]
    if far or sent:
        first = len(lead) + len(args)
        scratch_shapes += [pltpu.VMEM(args[i].shape, args[i].dtype) for i in far]
        scratch_shapes += [pltpu.VMEM(*outs[i]) for i in sent]
        scratch_shapes.append(pltpu.SemaphoreType.DMA((len(far) + len(sent),)))
        kernel = with_far(kernel, [len(lead) + i for i in far], [first + i for i in sent], early)
        for i in far:
            args[i] = pltpu.with_memory_space_constraint(args[i], pltpu.HBM)
    return pl.pallas_call(
        kernel,
        out_shape=[
            pltpu.HBM(s, d) if i in sent else jax.ShapeDtypeStruct(s, d)
            for i, (s, d) in enumerate(outs)
        ],
        in_specs=[pl.BlockSpec(memory_space=pltpu.SMEM)] * len(lead)
        + [there if i in far else whole for i in range(len(args))],
        out_specs=[there if i in sent else whole for i in range(len(outs))],
        scratch_shapes=scratch_shapes,
        compiler_params=pltpu.CompilerParams(vmem_limit_bytes=VMEM_LIMIT),
        cost_estimate=cost(us),
        name=name,
    )(*lead, *args)


def cost(us):
    return pl.CostEstimate(flops=int(us * 1.1e9), bytes_accessed=0, transcendentals=0)


def swap(value, axis, shift):
    count = lax.axis_size(axis)
    return lax.ppermute(value, axis, [(i, i ^ shift) for i in range(count)])


def after(values, *done):
    return lax.optimization_barrier((values, done))[0]


def to_planes(blocks):
    if len(blocks) > 1:
        return [blocks[0]] + [swap(b, "ep", k) for k, b in enumerate(blocks) if k]
    return [exchange(blocks[0], "ep")]


def exchange(value, axis):
    count = lax.axis_size(axis)
    split = value.reshape(count, -1, value.shape[-1])
    moved = lax.all_to_all(split, axis, split_axis=0, concat_axis=0, tiled=True)
    return moved.reshape(value.shape)


def gather_blocks(parts):
    return [parts[0]] + [swap(p, "tp", d) for d, p in enumerate(parts) if d]


def gather_tp(block):
    count, cut = lax.axis_size("tp"), 64
    if count != 4:
        return [block] + [swap(block, "tp", d) for d in range(1, count)]
    first, second = swap(block, "tp", 1), swap(block, "tp", 2)
    return [block, first, second, swap(first[:cut], "tp", 2), swap(second[cut:], "tp", 1)]


def body(
    x, passage, gain1, w_q, w_k, w_v, w_o, gain2, w_r, embed, temp, w_up, w_down, chosen, place, cot
):
    blocks, planes = lax.axis_size("tp"), lax.axis_size("ep")
    ids = jnp.stack([lax.axis_index("dp"), lax.axis_index("ep"), lax.axis_index("tp")])
    ids = ids.astype(jnp.int32)
    tokens, width = x.shape
    rows, local = tokens // blocks, w_q.shape[1]
    w_q, w_k, w_v, w_r = w_q.T, w_k.T, w_v.T, w_r.T
    experts, router = embed.shape
    hidden_units = w_up.shape[2]
    capacity = rows // experts
    pieces = planes if planes <= 4 else 1
    relative = pieces > 1
    slot_shapes = [((rows // pieces, width), F32)] * pieces
    wide = -(-(2 * hidden_units + router) // 128) * 128
    slab_rows = -(-(router + experts + 2) // 8) * 8
    w_up, w_down = w_up[0], w_down[0]
    chosen, place = chosen.reshape(1, rows), place.reshape(1, rows)
    gain1_line, gain1, gain2 = gain1, gain1.reshape(1, width), gain2.reshape(1, width)
    seg = passage.reshape(blocks, rows)
    temp = temp.reshape(1, 1)

    ctx, *parts = call(
        functools.partial(attend_kernel, blocks), ids, [seg, gain1_line, x, w_q, w_k, w_v, w_o],
        [((tokens, local), F32)] + [((rows, width), F32)] * blocks,
        [((tokens, width), F32)] + [((tokens, local), F32)] * 3,
        far=(0, 1, 2, 3, 4, 5, 6), early=3, name="attend", us=US["attend"],
    )
    got = gather_blocks(parts)
    w_up_sib, w_down_sib = swap(w_up, "dp", 1), swap(w_down, "dp", 1)
    slots = call(
        functools.partial(prep_kernel, capacity, relative), ids,
        [chosen, place, after(cot, *parts, w_up_sib, w_down_sib)], slot_shapes, far=(0, 1, 2), name="prep",
        us=US["prep"],
    )
    cot_slots = to_planes(slots)
    u_high, u_low = call(
        up_weights_kernel, None, [w_up, w_up_sib, w_r], [((width, wide), BF16)] * 2, name="up_weights",
        us=US["up_weights"],
    )
    cot_rows = jnp.concatenate(cot_slots, axis=0)
    cots = gather_tp(after(cot_rows, *got))
    hidden, *slots = call(
        functools.partial(hidden_kernel, capacity, relative, blocks), ids,
        [x, gain2, chosen, place, *after(got, u_high, cot_rows)], [((rows, width), F32)] + slot_shapes,
        name="hidden", us=US["hidden"],
    )

    same = gather_tp(jnp.concatenate(to_planes(slots), axis=0))
    *act_grads, w_high, w_low = call(
        functools.partial(cot_kernel, blocks), None,
        [w_down, w_down_sib, *after(cots, hidden)],
        [((2 * rows, 2 * hidden_units), F32)] * (blocks // 2)
        + [((2 * hidden_units, width), BF16)] * 2,
        name="cot_act", us=US["cot_act"],
    )
    ga, dp, slabs, parts = [], [], [], []
    for d in range(0, blocks, 2):
        *d_feeds, ga_high, ga_low, dp_high, dp_low, slab = call(
            expert_kernel, ids,
            [act_grads[d // 2], u_high, u_low, embed, temp]
            + after(same[d : d + 2] if d + 2 < blocks else same[d:], *slabs),
            [((rows, width), F32)] * 2
            + [((2 * rows, 2 * hidden_units), BF16)] * 2
            + [((2 * rows, wide), BF16)] * 2
            + [((slab_rows, width), F32)],
            name="expert", us=US["expert"],
        )
        ga += [ga_high, ga_low]
        dp += [dp_high, dp_low]
        slabs.append(slab)
        parts += [swap(f, "tp", d + i) if d + i else f for i, f in enumerate(d_feeds)]
    outs = call(
        functools.partial(expert_out_kernel, blocks), None, [w_high, w_low, *ga],
        [((rows, width), F32)] * blocks, name="expert_out", us=US["expert_out"],
    )
    pieces_back = call(
        functools.partial(sum_kernel, blocks), None, after(parts, *outs), slot_shapes,
        name="sum_feed", us=US["sum_feed"],
    )
    back = to_planes(pieces_back)
    grad_up, up_sib, grad_down, down_sib = call(
        functools.partial(expert_grad_kernel, blocks), None,
        [*after(cots, *pieces_back), *same, *ga, *dp],
        [((width, hidden_units), F32)] * 2 + [((hidden_units, width), F32)] * 2,
        name="expert_grad", us=US["expert_grad"],
    )
    (d_hidden,) = call(
        functools.partial(route_back_kernel, capacity, relative, blocks), ids,
        [hidden, cot, gain2, chosen, place, *slabs, *after(back, grad_up)],
        [((rows + slab_rows, width), F32)], name="route_back", us=US["route_back"],
    )

    d_hiddens = gather_tp(d_hidden)
    xhat, high, low, q, k, v, *split = call(
        functools.partial(again_kernel, blocks), ids,
        [gain1_line, after(x, d_hidden), w_q, w_k, w_v, w_o],
        [((tokens, width), F32)] + [((tokens, width), BF16)] * 2 + [((tokens, local), F32)] * 3
        + [((local, width), BF16)] * 8,
        [((tokens, width), F32)], far=(0, 1, 2, 3, 4, 5), early=2, name="again", us=US["again"],
    )
    half_grads = call(
        functools.partial(attend_back_kernel, blocks, 0), ids,
        [seg, q, k, v, *split[6:], *after(d_hiddens[:2], high)],
        [((2 * rows, local), F32)] + [((tokens, local), F32)] * 2, name="attend_back",
        us=US["attend_back"],
    )
    *dn, gain_row, dq, dk, dv = call(
        functools.partial(attend_back_kernel, blocks, 2), ids,
        [seg, q, k, v, *split[6:], *after(d_hiddens[2:], *half_grads), *half_grads, xhat]
        + split[:6],
        [((rows, width), F32)] * blocks + [((1, width), F32)] + [((tokens, local), F32)] * 3,
        name="attend_back_rest", us=US["attend_back"],
    )
    dn_got = gather_blocks(dn)
    shares = 2 * pieces if relative else 8
    stride = share_rows(4 * local, slab_rows, shares)[2]
    half_rows = stride * shares // 2
    small_rows = stride * shares - 4 * local
    own_part, sib_part = call(
        functools.partial(weight_grads_kernel, blocks, shares), ids,
        [high, low, dq, dk, dv, ctx, gain_row, *d_hiddens], [((half_rows, width), F32)] * 2,
        [((4 * local + small_rows, width), F32)], name="weight_grads", us=US["weight_grads"],
    )
    other_part = swap(sib_part, "dp", 1)
    grad_up = grad_up + swap(up_sib, "dp", 1)
    grad_down = grad_down + swap(down_sib, "dp", 1)
    if relative:
        core = call(
            split_planes_kernel, ids, [own_part, other_part],
            [((half_rows // pieces, width), F32)] * pieces, name="split_planes", us=0,
        )
        share_got = to_planes(core)
        dn_got = after(dn_got, *core, grad_up, grad_down)
    (d_x,) = call(
        norm_back_kernel, ids, [x, gain1, d_hidden, *dn_got], [((rows, width), F32)],
        name="norm_back", us=US["norm_back"],
    )
    d_xs = gather_tp(d_x)
    if relative:
        share, gain = call(
            functools.partial(join_kernel, pieces), None, share_got,
            [((stride, width), F32), ((8, width), F32)], name="join", us=US["join"],
        )
        parts = [share] + [swap(share, "ep", k) for k in range(1, pieces)]
    else:
        parts = [lax.psum(own_part + other_part, "ep")]
        share, gain = parts[0], parts[0][-8:]
    parts = parts + [swap(p, "dp", 1) for p in parts]
    gains = gather_blocks([after(gain, *parts[pieces:])] * blocks)
    near = after(outs, share)
    parts_out = gather_blocks(near)
    out_pieces = call(
        functools.partial(sum_kernel, blocks), None, parts_out, slot_shapes, name="sum_out",
        us=US["sum_out"],
    )
    out_slots = to_planes(out_pieces)
    (mixed,) = call(
        functools.partial(mixed_kernel, capacity, relative), ids,
        [hidden, chosen, place, *out_slots], [((rows, width), F32)],
        name="mixed", us=US["mixed"],
    )
    (grad_tokens,) = call(
        place_blocks_kernel, ids, d_xs, [((tokens, width), F32)],
        name="grad_tokens", us=0,
    )
    grad_q, grad_k, grad_v, grad_o, grad_g1, grad_g2, grad_proj, grad_embed, grad_temp = call(
        functools.partial(finish_kernel, router, experts, pieces, shares), ids,
        [*parts, *gains],
        [((local, width), F32)] * 4 + [((width,), F32)] * 2 + [((router, width), F32)]
        + [((experts, router), F32), ((1, 1), F32)],
        [((4 * local, width), F32), ((small_rows, width), F32)], name="finish", us=0,
    )
    return (
        mixed,
        grad_tokens,
        grad_g1,
        grad_q.T,
        grad_k.T,
        grad_v.T,
        grad_o,
        grad_g2,
        grad_proj.T,
        grad_embed,
        grad_temp.reshape(1),
        grad_up[None],
        grad_down[None],
    )


def solution(mesh):
    in_specs = (
        P(("dp", "ep"), None),
        P(("dp", "ep")),
        P(),
        P(None, "tp"),
        P(None, "tp"),
        P(None, "tp"),
        P("tp", None),
        P(),
        P(),
        P(),
        P(),
        P("ep", None, ("dp", "tp")),
        P("ep", ("dp", "tp"), None),
        P(("dp", "ep", "tp")),
        P(("dp", "ep", "tp")),
        P(("dp", "ep", "tp"), None),
    )
    out_specs = (
        P(("dp", "ep", "tp"), None),
        P(("dp", "ep"), None),
        P(),
        P(None, "tp"),
        P(None, "tp"),
        P(None, "tp"),
        P("tp", None),
        P(),
        P(),
        P(),
        P(),
        P("ep", None, ("dp", "tp")),
        P("ep", ("dp", "tp"), None),
    )
    return jax.shard_map(body, mesh=mesh, in_specs=in_specs, out_specs=out_specs, check_vma=False)
```

```python
import functools

import jax
import jax.numpy as jnp
from jax import lax
from jax.experimental import pallas as pl
from jax.experimental.pallas import tpu as pltpu
from jax.sharding import PartitionSpec as P

HEAD_DIM = 64
EPS = 1e-05
F32 = jnp.float32
BF16 = jnp.bfloat16
NN = (((1,), (0,)), ((), ()))
NT = (((1,), (1,)), ((), ()))
TN = (((0,), (0,)), ((), ()))
VMEM_LIMIT = 14 * 1024 * 1024
GELU_C = 0.7978845608028654
GELU_A = 0.044715


def halves(value):
    high = value.astype(BF16)
    return high, (value - high.astype(F32)).astype(BF16)


def dot1(left, right, dims):
    return lax.dot_general(left, right, dims, preferred_element_type=F32)


def dot3(left, right, dims=NN):
    small = dot1(left[0], right[1], dims) + dot1(left[1], right[0], dims)
    return small + dot1(left[0], right[0], dims)


def dot_full(left, right, dims=NN):
    return lax.dot_general(
        left, right, dims, precision=lax.Precision.HIGHEST, preferred_element_type=F32
    )


def place_rows(onehot, value, dims=NN):
    first = value.astype(BF16)
    rest = value - first.astype(F32)
    second = rest.astype(BF16)
    third = (rest - second.astype(F32)).astype(BF16)
    small = dot1(onehot, second, dims) + dot1(onehot, third, dims)
    return dot1(onehot, first, dims) + small


def normalize(values):
    center = values - jnp.mean(values, axis=-1, keepdims=True)
    inv = lax.rsqrt(jnp.mean(center * center, axis=-1, keepdims=True) + EPS)
    return center * inv, inv


def normalize_back(grad, gain, xhat, inv):
    scaled = grad * gain
    first = jnp.mean(scaled, axis=-1, keepdims=True)
    second = jnp.mean(scaled * xhat, axis=-1, keepdims=True)
    return inv * (scaled - first - xhat * second)


def slot_matrix(chosen_row, place_row, base, capacity):
    count = chosen_row.shape[1]
    column = (chosen_row ^ base) * capacity + place_row
    column = jnp.where(place_row >= 0, column, -1)
    slots = lax.broadcasted_iota(jnp.int32, (count, count), 0)
    return jnp.where(slots == column, 1.0, 0.0)


def pick(ref, index, size):
    return ref[pl.ds(pl.multiple_of(index * size, size), size), :]


def put_blocks(outs, value):
    size = outs[0].shape[0]
    for k, out in enumerate(outs):
        out[...] = value[k * size : (k + 1) * size]


def prep_kernel(capacity, relative, ids, chosen, place, cot, *slots_out):
    onehot = slot_matrix(chosen[...], place[...], ids[1] if relative else 0, capacity)
    put_blocks(slots_out, place_rows(onehot.astype(BF16), cot[...]))


def relative_rows(ids, x, out, blocks):
    size = x.shape[0] // blocks
    for d in range(blocks):
        out[d * size : (d + 1) * size, :] = pick(x, ids[2] ^ d, size)


def item_mask(ids, seg):
    row = [seg[pl.ds(ids[2] ^ d, 1), :] for d in range(seg.shape[0])]
    row = jnp.concatenate(row, axis=1).astype(F32)
    return row, jnp.transpose(jnp.broadcast_to(row, (8, row.shape[1])))[:, :1]


def head_mask(width, head):
    lane = lax.broadcasted_iota(jnp.int32, (1, width), 1)
    return jnp.where(lane // HEAD_DIM == head, 1.0, 0.0)


def attend_kernel(blocks, ids, seg, gain, x, w_q, w_k, w_v, w_o, ctx_out, *rest):
    part_out, (rel, query, key, value) = rest[:blocks], rest[blocks:]
    tokens, width = x.shape[0], w_q.shape[0]
    relative_rows(ids, x, rel, blocks)
    xhat, _ = normalize(rel[...])
    normed = halves(xhat * gain[...].reshape(1, -1))
    query[...] = dot3(normed, halves(w_q[...]), NT) * HEAD_DIM**-0.5
    key[...] = dot3(normed, halves(w_k[...]), NT)
    value[...] = dot3(normed, halves(w_v[...]), NT)
    row, column = item_mask(ids, seg)
    keys = halves(key[...])
    weight = halves(w_o[...])
    chunk = 256
    rows = tokens // blocks
    for c in range(tokens // chunk):
        here = slice(c * chunk, (c + 1) * chunk)
        allowed = column[here] == row
        total = None
        for h in range(width // HEAD_DIM):
            mask = head_mask(width, h)
            scores = dot3(halves(query[here, :] * mask), keys, NT)
            scores = jnp.where(allowed, scores, -1e30)
            expo = jnp.exp(scores - jnp.max(scores, axis=-1, keepdims=True))
            norm = 1.0 / jnp.sum(expo, axis=-1, keepdims=True)
            part = dot3(halves(expo), halves(value[...] * mask)) * norm
            total = part if total is None else total + part
        ctx_out[here, :] = total
        product = dot3(halves(total), weight)
        for i in range(chunk // rows):
            part_out[c * (chunk // rows) + i][...] = product[i * rows : (i + 1) * rows]


def up_weights_kernel(w_up, w_up_sib, w_r, u_high, u_low):
    hidden = w_up.shape[1]
    u_high[:, :hidden], u_low[:, :hidden] = halves(w_up[...])
    u_high[:, hidden : 2 * hidden], u_low[:, hidden : 2 * hidden] = halves(w_up_sib[...])
    pad = u_high.shape[1] - 2 * hidden - w_r.shape[0]
    route = jnp.concatenate([w_r[...], jnp.zeros((pad, w_r.shape[1]), F32)], axis=0)
    u_high[:, 2 * hidden :], u_low[:, 2 * hidden :] = halves(jnp.transpose(route))


def hidden_kernel(capacity, relative, blocks, ids, x, gain, chosen, place, *rest):
    parts, hidden_out, slots_out = rest[:blocks], rest[blocks], rest[blocks + 1 :]
    total = parts[0][...]
    for part in parts[1:]:
        total = total + part[...]
    hidden = pick(x, ids[2], hidden_out.shape[0]) + total
    hidden_out[...] = hidden
    xhat, _ = normalize(hidden)
    onehot = slot_matrix(chosen[...], place[...], ids[1] if relative else 0, capacity)
    put_blocks(slots_out, place_rows(onehot.astype(BF16), xhat * gain[...]))


def stack(refs):
    return jnp.concatenate([ref[...] for ref in refs], axis=0)


def pair_refs(refs, pairs):
    return [refs[2 * d : 2 * d + 2] for d in range(pairs - 1)] + [refs[2 * pairs - 2 :]]


def cot_kernel(blocks, w_down, w_down_sib, *rest):
    w_high, w_low = rest[-2:]
    pairs = blocks // 2
    cots, outs = pair_refs(rest[: -2 - pairs], pairs), rest[-2 - pairs : -2]
    hidden = w_down.shape[0]
    w_high[:hidden, :], w_low[:hidden, :] = halves(w_down[...])
    w_high[hidden:, :], w_low[hidden:, :] = halves(w_down_sib[...])
    for refs, out in zip(cots, outs):
        out[...] = dot3(halves(stack(refs)), (w_high[...], w_low[...]), NT)


def expert_kernel(ids, act_grad, u_high, u_low, embed, temp, *rest):
    feeds, (d_feed_out, d_next_out, ga_high, ga_low, dp_high, dp_low, slab) = rest[:-7], rest[-7:]
    rows = d_feed_out.shape[0]
    hidden = act_grad.shape[1]
    experts, router = embed.shape
    wide = u_high.shape[1]
    split = halves(stack(feeds))
    both = dot3(split, (u_high[...], u_low[...]))
    pre, routed = both[:, :hidden], both[:, hidden : hidden + router]
    da = act_grad[...]

    unit_inv = lax.rsqrt(jnp.sum(routed * routed, axis=-1, keepdims=True) + 1.0)
    unit = routed * unit_inv
    vectors = embed[...]
    vec_inv = lax.rsqrt(jnp.sum(vectors * vectors, axis=-1, keepdims=True) + 1.0)
    vec_unit = vectors * vec_inv
    scale = 1.0 / temp[0, 0]
    logits = dot_full(unit, vec_unit, NT) * scale
    soft = jnp.exp(logits - jnp.max(logits, axis=-1, keepdims=True))
    soft = soft / jnp.sum(soft, axis=-1, keepdims=True)
    mine = jnp.where(lax.broadcasted_iota(jnp.int32, (1, experts), 1) == ids[1], 1.0, 0.0)
    gate = jnp.sum(soft * mine, axis=-1, keepdims=True)

    square = pre * pre
    bend = jnp.tanh(GELU_C * (pre + GELU_A * pre * square))
    side = 0.5 * (1.0 + bend)
    act = pre * side
    slope = side + 0.5 * pre * (1.0 - bend * bend) * (GELU_C * (1.0 + 3.0 * GELU_A * square))
    d_gate = jnp.sum(act * da, axis=-1, keepdims=True)
    d_pre = da * gate * slope

    d_logits = d_gate * gate * (mine - soft)
    d_temp = -jnp.sum(jnp.sum(d_logits * logits, axis=-1, keepdims=True), axis=0, keepdims=True)
    d_raw = d_logits * scale
    d_unit = dot_full(d_raw, vec_unit)
    d_vec = dot_full(d_raw, unit, TN)
    d_vec = vec_inv * (d_vec - vec_unit * jnp.sum(d_vec * vec_unit, axis=-1, keepdims=True))
    d_routed = unit_inv * (d_unit - unit * jnp.sum(d_unit * unit, axis=-1, keepdims=True))

    grads = jnp.concatenate(
        [d_pre, d_routed, jnp.zeros((2 * rows, wide - hidden - router), F32)], axis=1
    )
    high, low = halves(grads)
    dp_high[...], dp_low[...] = high, low
    ga_high[...], ga_low[...] = halves(act * gate)
    d_feed = dot3((high, low), (u_high[...], u_low[...]), NT)
    d_feed_out[...] = d_feed[:rows]
    d_next_out[...] = d_feed[rows:]
    slab[...] = jnp.zeros_like(slab)
    proj = dot3(halves(d_routed), split, TN)
    slab[:router, :] = proj
    slab[router : router + experts, :router] = d_vec
    slab[router + experts : router + experts + 1, :1] = d_temp * scale


def expert_out_kernel(blocks, w_high, w_low, *rest):
    ga, outs = rest[:blocks], rest[blocks:]
    rows = outs[0].shape[0]
    for d in range(blocks // 2):
        part = dot3((ga[2 * d][...], ga[2 * d + 1][...]), (w_high[...], w_low[...]))
        outs[2 * d][...] = part[:rows]
        outs[2 * d + 1][...] = part[rows:]


def expert_grad_kernel(blocks, *rest):
    rest, (up_out, up_sib, down_out, down_sib) = rest[:-4], rest[-4:]
    rest, ga, dp = rest[: -2 * blocks], rest[-2 * blocks : -blocks], rest[-blocks:]
    cots = pair_refs(rest[: len(rest) // 2], blocks // 2)
    feeds = pair_refs(rest[len(rest) // 2 :], blocks // 2)
    hidden = up_out.shape[1]
    for d in range(blocks // 2):
        cot, feed = halves(stack(cots[d])), halves(stack(feeds[d]))
        for i, (up, down) in enumerate(((up_out, down_out), (up_sib, down_sib))):
            part = slice(i * hidden, (i + 1) * hidden)
            down_part = dot3((ga[2 * d][:, part], ga[2 * d + 1][:, part]), cot, TN)
            up_part = dot3(feed, (dp[2 * d][:, part], dp[2 * d + 1][:, part]), TN)
            down[...] = down_part if d == 0 else down[...] + down_part
            up[...] = up_part if d == 0 else up[...] + up_part


def sum_kernel(count, *rest):
    total = rest[0][...]
    for ref in rest[1:count]:
        total = total + ref[...]
    put_blocks(rest[count:], total)


def route_back_kernel(capacity, relative, blocks, ids, hidden, cot, gain, chosen, place, *rest):
    slabs, back, out = rest[: blocks // 2], rest[blocks // 2 : -1], rest[-1]
    rows = hidden.shape[0]
    xhat, inv = normalize(hidden[...])
    onehot = slot_matrix(chosen[...], place[...], ids[1] if relative else 0, capacity)
    slots = jnp.concatenate([b[...] for b in back], axis=0)
    d_normed = place_rows(jnp.transpose(onehot).astype(BF16), slots)
    gain_row = jnp.sum(d_normed * xhat, axis=0, keepdims=True)
    out[:rows, :] = cot[...] + normalize_back(d_normed, gain[...], xhat, inv)
    slab = slabs[0][...]
    for other in slabs[1:]:
        slab = slab + other[...]
    lines = lax.broadcasted_iota(jnp.int32, (slab.shape[0], 1), 0)
    out[rows:, :] = jnp.where(lines == slab.shape[0] - 1, gain_row, slab)


def mixed_kernel(capacity, relative, ids, hidden, chosen, place, *rest):
    back, out = rest[:-1], rest[-1]
    onehot = slot_matrix(chosen[...], place[...], ids[1] if relative else 0, capacity)
    slots = jnp.concatenate([b[...] for b in back], axis=0)
    out[...] = hidden[...] + place_rows(jnp.transpose(onehot).astype(BF16), slots)


def again_kernel(blocks, ids, gain, x, w_q, w_k, w_v, w_o, xhat_out, high_out, low_out, *rest):
    made, split, rel = rest[:3], rest[3:-1], rest[-1]
    relative_rows(ids, x, rel, blocks)
    xhat, _ = normalize(rel[...])
    xhat_out[...] = xhat
    high, low = halves(xhat * gain[...].reshape(1, -1))
    high_out[...], low_out[...] = high, low
    for i, weight in enumerate((w_q, w_k, w_v)):
        split[2 * i][...], split[2 * i + 1][...] = halves(weight[...])
        product = dot3((high, low), (split[2 * i][...], split[2 * i + 1][...]), NT)
        made[i][...] = product * HEAD_DIM**-0.5 if i == 0 else product
    split[6][...], split[7][...] = halves(w_o[...])


def token_rows(refs, rows, blocks):
    whole = [ref[...] for ref in refs[: blocks - 1]] + [stack(refs[blocks - 1 :])]
    others = whole[0][rows:]
    for value in whole[1:]:
        others = others + value[rows:]
    return [value[:rows] for value in whole], others


def attend_back_kernel(blocks, first, ids, seg, q, k, v, o_high, o_low, *rest):
    tokens, width = q.shape
    rows = tokens // blocks
    count = len(rest) - (10 + blocks + 4 if first else 3)
    d_hidden, rest = rest[:count], rest[count:]
    if first:
        before, xhat, split, rest = rest[:3], rest[3], rest[4:10], rest[10:]
        dn_out, (gain_out, dq, dk, dv) = rest[:blocks], rest[blocks:]
        dq[: first * rows, :] = before[0][...]
        dk[...], dv[...] = before[1][...], before[2][...]
    else:
        dq, dk, dv = rest
    row, column = item_mask(ids, seg)
    keys, values = halves(k[...]), halves(v[...])
    here = slice(first * rows, (first + 2) * rows)
    allowed = column == row[:, here]
    grad, _ = token_rows(d_hidden, rows, 2)
    grad = jnp.concatenate(grad, axis=0)
    d_here = dot3(halves(grad), (o_high[...], o_low[...]), NT)
    for h in range(width // HEAD_DIM):
        mask = head_mask(width, h)
        q_head = halves(q[here, :] * mask)
        d_head = halves(d_here * mask)
        scores = jnp.where(allowed, dot3(keys, q_head, NT), -1e30)
        expo = jnp.exp(scores - jnp.max(scores, axis=0, keepdims=True))
        probs = expo * (1.0 / jnp.sum(expo, axis=0, keepdims=True))
        d_probs = dot3(values, d_head, NT)
        delta = jnp.sum(probs * d_probs, axis=0, keepdims=True)
        d_scores = halves(probs * (d_probs - delta))
        d_value = dot3(halves(probs), d_head)
        d_key = dot3(d_scores, q_head)
        d_query = dot3(d_scores, halves(k[...] * (mask * HEAD_DIM**-0.5)), TN)
        new = h == 0 and not first
        dv[...] = d_value if new else dv[...] + d_value
        dk[...] = d_key if new else dk[...] + d_key
        dq[here, :] = d_query if h == 0 else dq[here, :] + d_query
    if not first:
        return
    d_normed = None
    for i, grad in enumerate((dq, dk, dv)):
        part = dot3(halves(grad[...]), (split[2 * i][...], split[2 * i + 1][...]))
        d_normed = part if d_normed is None else d_normed + part
    put_blocks(dn_out, d_normed)
    gain_out[...] = jnp.sum(d_normed * xhat[...], axis=0, keepdims=True)


def small_each(slab_rows, shares):
    return -(-slab_rows // shares)


def weight_grads_kernel(blocks, shares, ids, high, low, dq, dk, dv, ctx, gain, *rest):
    d_hidden, (own, sib, grads, small) = rest[:-4], rest[-4:]
    width = dq.shape[1]
    for i, grad in enumerate((dq, dk, dv)):
        grads[i * width : (i + 1) * width, :] = dot3(halves(grad[...]), (high[...], low[...]), TN)
    rows = ctx.shape[0] // blocks
    total = None
    d_rows, slab = token_rows(d_hidden, rows, blocks)
    for d, part in enumerate(d_rows):
        left = ctx[d * rows : (d + 1) * rows, :]
        product = dot3(halves(left), halves(part), TN)
        total = product if total is None else total + product
    grads[3 * width : 4 * width, :] = total
    count, half = slab.shape[0], 4 * width // (2 * shares)
    each = small_each(count, shares)
    small[...] = jnp.broadcast_to(gain[...], small.shape)
    for i in range(shares):
        few = max(min(each, count - i * each), 0)
        if few:
            small[8 * i : 8 * i + few, :] = slab[i * each : i * each + few]
    many = shares // 2
    for c, out in enumerate((own, sib)):
        for j in range(many):
            index = (ids[0] ^ c) * many + j
            at = j * (half + 8)
            out[at : at + half, :] = pick(grads, 2 * index, half)
            out[at + half : at + half + 8, :] = pick(small, index, 8)
            at = many * (half + 8) + j * half
            out[at : at + half, :] = pick(grads, 2 * index + 1, half)


def track_sums_kernel(ids, own, other, keep_a, send_a, keep_b, send_b):
    size_a, size_b = keep_a.shape[0] // 2, keep_b.shape[0] // 2
    outs = ((keep_a, (0, 2)), (send_a, (1, 3)), (keep_b, (0, 1)), (send_b, (2, 3)))
    for i, (out, planes) in enumerate(outs):
        size, first = (size_a, 0) if i < 2 else (size_b, 4 * size_a)
        for j, k in enumerate(planes):
            here = pl.ds(pl.multiple_of(first + (ids[1] ^ k) * size, 8), size)
            out[j * size : (j + 1) * size, :] = own[here, :] + other[here, :]


def track_halves_kernel(keep_a, got_a, keep_b, got_b, own_a, send_a, own_b, send_b):
    for keep, got, own, send in ((keep_a, got_a, own_a, send_a), (keep_b, got_b, own_b, send_b)):
        size = own.shape[0]
        own[...] = keep[:size, :] + got[:size, :]
        send[...] = keep[size:, :] + got[size:, :]


def join_kernel(own_a, got_a, own_b, got_b, share_a, share_b, gain_out):
    total = own_a[...] + got_a[...]
    share_a[...] = total
    share_b[...] = own_b[...] + got_b[...]
    gain_out[...] = total[-8:]


def pair_kernel(own_a, got_a, own_b, got_b, pair_a, pair_b):
    put_blocks((pair_a,), stack((own_a, got_a)))
    put_blocks((pair_b,), stack((own_b, got_b)))


def norm_back_kernel(ids, x, gain, d_hidden, *rest):
    parts, out = rest[:-1], rest[-1]
    rows = out.shape[0]
    total = parts[0][...]
    for part in parts[1:]:
        total = total + part[...]
    xhat, inv = normalize(pick(x, ids[2], rows))
    out[...] = d_hidden[:rows, :] + normalize_back(total, gain[...], xhat, inv)


def place_blocks_kernel(ids, *rest):
    parts, out = rest[:-1], rest[-1]
    rows = parts[0].shape[0]
    blocks = out.shape[0] // rows
    for d in range(blocks):
        value = parts[d][...] if d < blocks - 1 else stack(parts[d:])
        out[pl.ds(pl.multiple_of((ids[2] ^ d) * rows, rows), rows), :] = value


def finish_kernel(router, experts, shares, tracks, ids, *rest):
    parts, gains, rest = rest[: 2 * tracks], rest[2 * tracks : -11], rest[-11:]
    q_out, k_out, v_out, o_out, g1, g2, proj, vectors, temp, full, small = rest
    width = q_out.shape[0]
    count = -(-(router + experts + 2) // 8) * 8
    half, many = 4 * width // (2 * shares), shares // 2
    each = small_each(count, shares)

    def keep(index, track, value):
        full[pl.ds(pl.multiple_of((2 * index + track) * half, 8), half), :] = value[:half]
        if track == 0:
            small[pl.ds(pl.multiple_of(index * 8, 8), 8), :] = value[half:]

    for c in range(2):
        if tracks == 1:
            part = parts[c]
            for j in range(many):
                at = j * (half + 8)
                keep((ids[0] ^ c) * many + j, 0, part[at : at + half + 8, :])
                at = many * (half + 8) + j * half
                keep((ids[0] ^ c) * many + j, 1, part[at : at + half, :])
            continue
        for i, planes in enumerate(((0, 2), (1, 3), (0, 1), (2, 3))):
            part, track = parts[c * tracks + i], i // 2
            size = part.shape[0] // 2
            for j, k in enumerate(planes):
                index = (ids[0] ^ c) * many + (ids[1] ^ k)
                keep(index, track, part[j * size : (j + 1) * size, :])
    for i in range(1, shares):
        few = max(min(each, count - i * each), 0)
        if few:
            small[i * each : i * each + few, :] = small[8 * i : 8 * i + few, :]
    put_blocks((q_out, k_out, v_out, o_out), full)
    gain = gains[0][-1:, :]
    for other in gains[1:]:
        gain = gain + other[-1:, :]
    g1[...] = gain.reshape(-1)
    g2[...] = small[count - 1 : count, :].reshape(-1)
    proj[...] = small[:router, :]
    vectors[...] = small[router : router + experts, :router]
    temp[...] = small[router + experts : router + experts + 1, :1]


US = dict(
    attend=10, prep=2, up_weights=2, hidden=1, cot_act=4, expert=3, expert_out=1, out_split=1,
    sum_feed=0, expert_grad=10, route_back=0, again=6, sum_out=0, attend_back=6, weight_grads=0,
    norm_back=0, mixed=0, join=0,
)


class Far:
    def __init__(self, buffer, copy, arrives):
        self.buffer, self.copy, self.open = buffer, copy, arrives
        self.shape, self.dtype = buffer.shape, buffer.dtype
        self.next = []

    def wait(self):
        if self.open:
            self.copy.wait()
        self.open = False
        for one in self.next:
            one.copy.start()
        self.next = []

    def send(self):
        self.copy.start()
        self.open = True

    def __getitem__(self, index):
        self.wait()
        return self.buffer[index]

    def __setitem__(self, index, value):
        self.buffer[index] = value


def with_far(kernel, operands, results, early):
    count = len(operands) + len(results)

    def run(*refs):
        refs, buffers, sems = list(refs[: -count - 1]), refs[-count - 1 : -1], refs[-1]
        moved = []
        for j, i in enumerate((*operands, *results)):
            arrives = j < len(operands)
            ends = (refs[i], buffers[j]) if arrives else (buffers[j], refs[i])
            copy = pltpu.make_async_copy(*ends, sems.at[j])
            refs[i] = Far(buffers[j], copy, arrives)
            moved.append(refs[i])
        first = moved[: len(operands)]
        for one in first[:early] if early else first:
            one.copy.start()
        if early:
            first[early - 1].next = first[early:]
        kernel(*refs)
        for one in moved:
            one.wait()

    return run


def call(kernel, ids, args, outs, scratch=(), far=(), sent=(), early=0, name=None, us=1):
    whole, there = pl.BlockSpec(memory_space=pltpu.VMEM), pl.BlockSpec(memory_space=pltpu.HBM)
    lead = [] if ids is None else [ids]
    args = list(args)
    scratch_shapes = [pltpu.VMEM(s, d) for s, d in scratch]
    if far or sent:
        first = len(lead) + len(args)
        scratch_shapes += [pltpu.VMEM(args[i].shape, args[i].dtype) for i in far]
        scratch_shapes += [pltpu.VMEM(*outs[i]) for i in sent]
        scratch_shapes.append(pltpu.SemaphoreType.DMA((len(far) + len(sent),)))
        kernel = with_far(kernel, [len(lead) + i for i in far], [first + i for i in sent], early)
        for i in far:
            args[i] = pltpu.with_memory_space_constraint(args[i], pltpu.HBM)
    return pl.pallas_call(
        kernel,
        out_shape=[
            pltpu.HBM(s, d) if i in sent else jax.ShapeDtypeStruct(s, d)
            for i, (s, d) in enumerate(outs)
        ],
        in_specs=[pl.BlockSpec(memory_space=pltpu.SMEM)] * len(lead)
        + [there if i in far else whole for i in range(len(args))],
        out_specs=[there if i in sent else whole for i in range(len(outs))],
        scratch_shapes=scratch_shapes,
        compiler_params=pltpu.CompilerParams(vmem_limit_bytes=VMEM_LIMIT),
        cost_estimate=cost(us),
        name=name,
    )(*lead, *args)


def cost(us):
    return pl.CostEstimate(flops=int(us * 1.1e9), bytes_accessed=0, transcendentals=0)


def swap(value, axis, shift):
    count = lax.axis_size(axis)
    return lax.ppermute(value, axis, [(i, i ^ shift) for i in range(count)])


def after(values, *done):
    return lax.optimization_barrier((values, done))[0]


def to_planes(blocks):
    if len(blocks) > 1:
        return [blocks[0]] + [swap(b, "ep", k) for k, b in enumerate(blocks) if k]
    return [exchange(blocks[0], "ep")]


def exchange(value, axis):
    count = lax.axis_size(axis)
    split = value.reshape(count, -1, value.shape[-1])
    moved = lax.all_to_all(split, axis, split_axis=0, concat_axis=0, tiled=True)
    return moved.reshape(value.shape)


def gather_blocks(parts):
    return [parts[0]] + [swap(p, "tp", d) for d, p in enumerate(parts) if d]


def gather_tp(block):
    count, cut = lax.axis_size("tp"), 64
    if count != 4:
        return [block] + [swap(block, "tp", d) for d in range(1, count)]
    first, second = swap(block, "tp", 1), swap(block, "tp", 2)
    return [block, first, second, swap(first[:cut], "tp", 2), swap(second[cut:], "tp", 1)]


def body(
    x, passage, gain1, w_q, w_k, w_v, w_o, gain2, w_r, embed, temp, w_up, w_down, chosen, place, cot
):
    blocks, planes = lax.axis_size("tp"), lax.axis_size("ep")
    ids = jnp.stack([lax.axis_index("dp"), lax.axis_index("ep"), lax.axis_index("tp")])
    ids = ids.astype(jnp.int32)
    tokens, width = x.shape
    rows, local = tokens // blocks, w_q.shape[1]
    w_q, w_k, w_v, w_r = w_q.T, w_k.T, w_v.T, w_r.T
    experts, router = embed.shape
    hidden_units = w_up.shape[2]
    capacity = rows // experts
    pieces = planes if planes <= 4 else 1
    relative = pieces > 1
    slot_shapes = [((rows // pieces, width), F32)] * pieces
    wide = -(-(2 * hidden_units + router) // 128) * 128
    slab_rows = -(-(router + experts + 2) // 8) * 8
    w_up, w_down = w_up[0], w_down[0]
    chosen, place = chosen.reshape(1, rows), place.reshape(1, rows)
    gain1_line, gain1, gain2 = gain1, gain1.reshape(1, width), gain2.reshape(1, width)
    seg = passage.reshape(blocks, rows)
    temp = temp.reshape(1, 1)

    ctx, *parts = call(
        functools.partial(attend_kernel, blocks), ids, [seg, gain1_line, x, w_q, w_k, w_v, w_o],
        [((tokens, local), F32)] + [((rows, width), F32)] * blocks,
        [((tokens, width), F32)] + [((tokens, local), F32)] * 3,
        far=(0, 1, 2, 3, 4, 5, 6), early=3, name="attend", us=US["attend"],
    )
    got = gather_blocks(parts)
    w_up_sib, w_down_sib = swap(w_up, "dp", 1), swap(w_down, "dp", 1)
    slots = call(
        functools.partial(prep_kernel, capacity, relative), ids,
        [chosen, place, after(cot, *parts, w_up_sib, w_down_sib)], slot_shapes, far=(0, 1, 2), name="prep",
        us=US["prep"],
    )
    cot_slots = to_planes(slots)
    u_high, u_low = call(
        up_weights_kernel, None, [w_up, w_up_sib, w_r], [((width, wide), BF16)] * 2, name="up_weights",
        us=US["up_weights"],
    )
    cot_rows = jnp.concatenate(cot_slots, axis=0)
    cots = gather_tp(after(cot_rows, *got))
    hidden, *slots = call(
        functools.partial(hidden_kernel, capacity, relative, blocks), ids,
        [x, gain2, chosen, place, *after(got, u_high, cot_rows)], [((rows, width), F32)] + slot_shapes,
        name="hidden", us=US["hidden"],
    )

    same = gather_tp(jnp.concatenate(to_planes(slots), axis=0))
    *act_grads, w_high, w_low = call(
        functools.partial(cot_kernel, blocks), None,
        [w_down, w_down_sib, *after(cots, hidden)],
        [((2 * rows, 2 * hidden_units), F32)] * (blocks // 2)
        + [((2 * hidden_units, width), BF16)] * 2,
        name="cot_act", us=US["cot_act"],
    )
    ga, dp, slabs, parts = [], [], [], []
    for d in range(0, blocks, 2):
        *d_feeds, ga_high, ga_low, dp_high, dp_low, slab = call(
            expert_kernel, ids,
            [act_grads[d // 2], u_high, u_low, embed, temp]
            + after(same[d : d + 2] if d + 2 < blocks else same[d:], *slabs),
            [((rows, width), F32)] * 2
            + [((2 * rows, 2 * hidden_units), BF16)] * 2
            + [((2 * rows, wide), BF16)] * 2
            + [((slab_rows, width), F32)],
            name="expert", us=US["expert"],
        )
        ga += [ga_high, ga_low]
        dp += [dp_high, dp_low]
        slabs.append(slab)
        parts += [swap(f, "tp", d + i) if d + i else f for i, f in enumerate(d_feeds)]
    outs = call(
        functools.partial(expert_out_kernel, blocks), None, [w_high, w_low, *ga],
        [((rows, width), F32)] * blocks, name="expert_out", us=US["expert_out"],
    )
    pieces_back = call(
        functools.partial(sum_kernel, blocks), None, after(parts, *outs), slot_shapes,
        name="sum_feed", us=US["sum_feed"],
    )
    back = to_planes(pieces_back)
    grad_up, up_sib, grad_down, down_sib = call(
        functools.partial(expert_grad_kernel, blocks), None,
        [*after(cots, *pieces_back), *same, *ga, *dp],
        [((width, hidden_units), F32)] * 2 + [((hidden_units, width), F32)] * 2,
        name="expert_grad", us=US["expert_grad"],
    )
    (d_hidden,) = call(
        functools.partial(route_back_kernel, capacity, relative, blocks), ids,
        [hidden, cot, gain2, chosen, place, *slabs, *after(back, grad_up)],
        [((rows + slab_rows, width), F32)], name="route_back", us=US["route_back"],
    )

    up_got, down_got = swap(up_sib, "dp", 1), swap(down_sib, "dp", 1)

    d_hiddens = gather_tp(d_hidden)
    xhat, high, low, q, k, v, *split = call(
        functools.partial(again_kernel, blocks), ids,
        [gain1_line, after(x, d_hidden), w_q, w_k, w_v, w_o],
        [((tokens, width), F32)] + [((tokens, width), BF16)] * 2 + [((tokens, local), F32)] * 3
        + [((local, width), BF16)] * 8,
        [((tokens, width), F32)], far=(0, 1, 2, 3, 4, 5), early=2, name="again", us=US["again"],
    )
    half_grads = call(
        functools.partial(attend_back_kernel, blocks, 0), ids,
        [seg, q, k, v, *split[6:], *after(d_hiddens[:2], high)],
        [((2 * rows, local), F32)] + [((tokens, local), F32)] * 2, name="attend_back",
        us=US["attend_back"],
    )
    *dn, gain_row, dq, dk, dv = call(
        functools.partial(attend_back_kernel, blocks, 2), ids,
        [seg, q, k, v, *split[6:], *after(d_hiddens[2:], *half_grads, up_got, down_got), *half_grads, xhat]
        + split[:6],
        [((rows, width), F32)] * blocks + [((1, width), F32)] + [((tokens, local), F32)] * 3,
        name="attend_back_rest", us=US["attend_back"],
    )
    dn_got = gather_blocks(dn)
    shares, tracked = 8, planes == 4
    half = 4 * local // (2 * shares)
    size_a, size_b = half + 8, half
    own_part, sib_part = call(
        functools.partial(weight_grads_kernel, blocks, shares), ids,
        [high, low, dq, dk, dv, ctx, gain_row, *d_hiddens],
        [((shares // 2 * (size_a + size_b), width), F32)] * 2,
        [((4 * local, width), F32), ((8 * shares, width), F32)], name="weight_grads",
        us=US["weight_grads"],
    )
    other_part = swap(sib_part, "dp", 1)
    grad_up, grad_down = grad_up + up_got, grad_down + down_got
    dn_got = after(dn_got, grad_up, grad_down)
    if tracked:
        keep_a, send_a, keep_b, send_b = call(
            track_sums_kernel, ids, [own_part, other_part],
            [((2 * size_a, width), F32)] * 2 + [((2 * size_b, width), F32)] * 2,
            name="track_sums", us=0,
        )
        got_a, got_b = swap(send_a, "ep", 1), swap(send_b, "ep", 2)
        dn_got = after(dn_got, keep_a)
    (d_x,) = call(
        norm_back_kernel, ids, [x, gain1, d_hidden, *dn_got], [((rows, width), F32)],
        name="norm_back", us=US["norm_back"],
    )
    d_xs = gather_tp(d_x)
    if tracked:
        own_a, send_a, own_b, send_b = call(
            track_halves_kernel, None, [keep_a, got_a, keep_b, got_b],
            [((size_a, width), F32)] * 2 + [((size_b, width), F32)] * 2, name="track_halves",
            us=0,
        )
        share_a, share_b, gain = call(
            join_kernel, None, [own_a, swap(send_a, "ep", 2), own_b, swap(send_b, "ep", 1)],
            [((size_a, width), F32), ((size_b, width), F32), ((8, width), F32)], name="join",
            us=US["join"],
        )
        pair_a, pair_b = call(
            pair_kernel, None, [share_a, swap(share_a, "ep", 2), share_b, swap(share_b, "ep", 1)],
            [((2 * size_a, width), F32), ((2 * size_b, width), F32)], name="pair", us=0,
        )
        parts = [pair_a, swap(pair_a, "ep", 1), pair_b, swap(pair_b, "ep", 2)]
    else:
        parts = [lax.psum(own_part + other_part, "ep")]
        share_a, gain = parts[0], parts[0][half : half + 8]
    tracks = len(parts)
    parts = parts + [swap(p, "dp", 1) for p in parts]
    gains = gather_blocks([after(gain, *parts[tracks:])] * blocks)
    near = after(outs, share_a)
    parts_out = gather_blocks(near)
    out_pieces = call(
        functools.partial(sum_kernel, blocks), None, parts_out, slot_shapes, name="sum_out",
        us=US["sum_out"],
    )
    out_slots = to_planes(out_pieces)
    (mixed,) = call(
        functools.partial(mixed_kernel, capacity, relative), ids,
        [hidden, chosen, place, *out_slots], [((rows, width), F32)],
        name="mixed", us=US["mixed"],
    )
    (grad_tokens,) = call(
        place_blocks_kernel, ids, d_xs, [((tokens, width), F32)],
        name="grad_tokens", us=0,
    )
    grad_q, grad_k, grad_v, grad_o, grad_g1, grad_g2, grad_proj, grad_embed, grad_temp = call(
        functools.partial(finish_kernel, router, experts, shares, tracks), ids,
        [*parts, *gains],
        [((local, width), F32)] * 4 + [((width,), F32)] * 2 + [((router, width), F32)]
        + [((experts, router), F32), ((1, 1), F32)],
        [((4 * local, width), F32), ((8 * shares, width), F32)], name="finish", us=0,
    )
    return (
        mixed,
        grad_tokens,
        grad_g1,
        grad_q.T,
        grad_k.T,
        grad_v.T,
        grad_o,
        grad_g2,
        grad_proj.T,
        grad_embed,
        grad_temp.reshape(1),
        grad_up[None],
        grad_down[None],
    )


def solution(mesh):
    in_specs = (
        P(("dp", "ep"), None),
        P(("dp", "ep")),
        P(),
        P(None, "tp"),
        P(None, "tp"),
        P(None, "tp"),
        P("tp", None),
        P(),
        P(),
        P(),
        P(),
        P("ep", None, ("dp", "tp")),
        P("ep", ("dp", "tp"), None),
        P(("dp", "ep", "tp")),
        P(("dp", "ep", "tp")),
        P(("dp", "ep", "tp"), None),
    )
    out_specs = (
        P(("dp", "ep", "tp"), None),
        P(("dp", "ep"), None),
        P(),
        P(None, "tp"),
        P(None, "tp"),
        P(None, "tp"),
        P("tp", None),
        P(),
        P(),
        P(),
        P(),
        P("ep", None, ("dp", "tp")),
        P("ep", ("dp", "tp"), None),
    )
    return jax.shard_map(body, mesh=mesh, in_specs=in_specs, out_specs=out_specs, check_vma=False)
```

```python
import functools

import jax
import jax.numpy as jnp
from jax import lax
from jax.experimental import pallas as pl
from jax.experimental.pallas import tpu as pltpu
from jax.sharding import PartitionSpec as P

HEAD_DIM = 64
EPS = 1e-05
F32 = jnp.float32
BF16 = jnp.bfloat16
NN = (((1,), (0,)), ((), ()))
NT = (((1,), (1,)), ((), ()))
TN = (((0,), (0,)), ((), ()))
VMEM_LIMIT = 14 * 1024 * 1024
GELU_C = 0.7978845608028654
GELU_A = 0.044715


def halves(value):
    high = value.astype(BF16)
    return high, (value - high.astype(F32)).astype(BF16)


def dot1(left, right, dims):
    return lax.dot_general(left, right, dims, preferred_element_type=F32)


def dot3(left, right, dims=NN):
    small = dot1(left[0], right[1], dims) + dot1(left[1], right[0], dims)
    return small + dot1(left[0], right[0], dims)


def dot_full(left, right, dims=NN):
    return lax.dot_general(
        left, right, dims, precision=lax.Precision.HIGHEST, preferred_element_type=F32
    )


def place_rows(onehot, value, dims=NN):
    first = value.astype(BF16)
    rest = value - first.astype(F32)
    second = rest.astype(BF16)
    third = (rest - second.astype(F32)).astype(BF16)
    small = dot1(onehot, second, dims) + dot1(onehot, third, dims)
    return dot1(onehot, first, dims) + small


def normalize(values):
    center = values - jnp.mean(values, axis=-1, keepdims=True)
    inv = lax.rsqrt(jnp.mean(center * center, axis=-1, keepdims=True) + EPS)
    return center * inv, inv


def normalize_back(grad, gain, xhat, inv):
    scaled = grad * gain
    first = jnp.mean(scaled, axis=-1, keepdims=True)
    second = jnp.mean(scaled * xhat, axis=-1, keepdims=True)
    return inv * (scaled - first - xhat * second)


def slot_matrix(chosen_row, place_row, base, capacity):
    count = chosen_row.shape[1]
    column = (chosen_row ^ base) * capacity + place_row
    column = jnp.where(place_row >= 0, column, -1)
    slots = lax.broadcasted_iota(jnp.int32, (count, count), 0)
    return jnp.where(slots == column, 1.0, 0.0)


def pick(ref, index, size):
    return ref[pl.ds(pl.multiple_of(index * size, size), size), :]


def put_blocks(outs, value):
    size = outs[0].shape[0]
    for k, out in enumerate(outs):
        out[...] = value[k * size : (k + 1) * size]


def prep_kernel(capacity, relative, ids, chosen, place, cot, *slots_out):
    onehot = slot_matrix(chosen[...], place[...], ids[1] if relative else 0, capacity)
    put_blocks(slots_out, place_rows(onehot.astype(BF16), cot[...]))


def relative_rows(ids, x, out, blocks):
    size = x.shape[0] // blocks
    for d in range(blocks):
        out[d * size : (d + 1) * size, :] = pick(x, ids[2] ^ d, size)


def item_mask(ids, seg):
    row = [seg[pl.ds(ids[2] ^ d, 1), :] for d in range(seg.shape[0])]
    row = jnp.concatenate(row, axis=1).astype(F32)
    return row, jnp.transpose(jnp.broadcast_to(row, (8, row.shape[1])))[:, :1]


def head_mask(width, head):
    lane = lax.broadcasted_iota(jnp.int32, (1, width), 1)
    return jnp.where(lane // HEAD_DIM == head, 1.0, 0.0)


def attend_kernel(blocks, ids, seg, gain, x, w_q, w_k, w_v, w_o, ctx_out, *rest):
    part_out, (rel, query, key, value, sems) = rest[:blocks], rest[blocks:]
    tokens, width = x.shape[0], w_q.shape[0]
    size = tokens // blocks
    copies = []
    for d in range(blocks):
        there = pl.ds(pl.multiple_of((ids[2] ^ d) * size, size), size)
        here = rel.at[d * size : (d + 1) * size, :]
        copies.append(pltpu.make_async_copy(x.at[there, :], here, sems.at[d]))
        copies[-1].start()
    scale, normed = gain[...].reshape(1, -1), []
    for d, copy in enumerate(copies):
        copy.wait()
        xhat, _ = normalize(rel[d * size : (d + 1) * size, :])
        normed.append(halves(xhat * scale))
    normed = [jnp.concatenate(part, axis=0) for part in zip(*normed)]
    query[...] = dot3(normed, halves(w_q[...]), NT) * HEAD_DIM**-0.5
    key[...] = dot3(normed, halves(w_k[...]), NT)
    value[...] = dot3(normed, halves(w_v[...]), NT)
    row, column = item_mask(ids, seg)
    keys = halves(key[...])
    weight = halves(w_o[...])
    chunk = 256
    rows = tokens // blocks
    for c in range(tokens // chunk):
        here = slice(c * chunk, (c + 1) * chunk)
        allowed = column[here] == row
        total = None
        for h in range(width // HEAD_DIM):
            mask = head_mask(width, h)
            scores = dot3(halves(query[here, :] * mask), keys, NT)
            scores = jnp.where(allowed, scores, -1e30)
            expo = jnp.exp(scores - jnp.max(scores, axis=-1, keepdims=True))
            norm = 1.0 / jnp.sum(expo, axis=-1, keepdims=True)
            part = dot3(halves(expo), halves(value[...] * mask)) * norm
            total = part if total is None else total + part
        ctx_out[here, :] = total
        product = dot3(halves(total), weight)
        for i in range(chunk // rows):
            part_out[c * (chunk // rows) + i][...] = product[i * rows : (i + 1) * rows]


def up_weights_kernel(w_up, w_up_sib, w_r, u_high, u_low):
    hidden = w_up.shape[1]
    u_high[:, :hidden], u_low[:, :hidden] = halves(w_up[...])
    u_high[:, hidden : 2 * hidden], u_low[:, hidden : 2 * hidden] = halves(w_up_sib[...])
    pad = u_high.shape[1] - 2 * hidden - w_r.shape[0]
    route = jnp.concatenate([w_r[...], jnp.zeros((pad, w_r.shape[1]), F32)], axis=0)
    u_high[:, 2 * hidden :], u_low[:, 2 * hidden :] = halves(jnp.transpose(route))


def hidden_kernel(capacity, relative, blocks, ids, x, gain, chosen, place, *rest):
    parts, hidden_out, slots_out = rest[:blocks], rest[blocks], rest[blocks + 1 :]
    total = parts[0][...]
    for part in parts[1:]:
        total = total + part[...]
    hidden = pick(x, ids[2], hidden_out.shape[0]) + total
    hidden_out[...] = hidden
    xhat, _ = normalize(hidden)
    onehot = slot_matrix(chosen[...], place[...], ids[1] if relative else 0, capacity)
    put_blocks(slots_out, place_rows(onehot.astype(BF16), xhat * gain[...]))


def stack(refs):
    return jnp.concatenate([ref[...] for ref in refs], axis=0)


def pair_refs(refs, pairs):
    return [refs[2 * d : 2 * d + 2] for d in range(pairs - 1)] + [refs[2 * pairs - 2 :]]


def cot_kernel(w_down, w_down_sib, *rest):
    cots, (out, w_high, w_low) = rest[:-3], rest[-3:]
    hidden = w_down.shape[0]
    w_high[:hidden, :], w_low[:hidden, :] = halves(w_down[...])
    w_high[hidden:, :], w_low[hidden:, :] = halves(w_down_sib[...])
    out[...] = dot3(halves(stack(cots)), (w_high[...], w_low[...]), NT)


def cot_rest_kernel(w_high, w_low, *rest):
    rest[-1][...] = dot3(halves(stack(rest[:-1])), (w_high[...], w_low[...]), NT)


def expert_kernel(ids, act_grad, u_high, u_low, embed, temp, *rest):
    feeds, (d_feed_out, d_next_out, ga_high, ga_low, dp_high, dp_low, slab) = rest[:-7], rest[-7:]
    rows = d_feed_out.shape[0]
    hidden = act_grad.shape[1]
    experts, router = embed.shape
    wide = u_high.shape[1]
    split = halves(stack(feeds))
    both = dot3(split, (u_high[...], u_low[...]))
    pre, routed = both[:, :hidden], both[:, hidden : hidden + router]
    da = act_grad[...]

    unit_inv = lax.rsqrt(jnp.sum(routed * routed, axis=-1, keepdims=True) + 1.0)
    unit = routed * unit_inv
    vectors = embed[...]
    vec_inv = lax.rsqrt(jnp.sum(vectors * vectors, axis=-1, keepdims=True) + 1.0)
    vec_unit = vectors * vec_inv
    scale = 1.0 / temp[0, 0]
    logits = dot_full(unit, vec_unit, NT) * scale
    soft = jnp.exp(logits - jnp.max(logits, axis=-1, keepdims=True))
    soft = soft / jnp.sum(soft, axis=-1, keepdims=True)
    mine = jnp.where(lax.broadcasted_iota(jnp.int32, (1, experts), 1) == ids[1], 1.0, 0.0)
    gate = jnp.sum(soft * mine, axis=-1, keepdims=True)

    square = pre * pre
    bend = jnp.tanh(GELU_C * (pre + GELU_A * pre * square))
    side = 0.5 * (1.0 + bend)
    act = pre * side
    slope = side + 0.5 * pre * (1.0 - bend * bend) * (GELU_C * (1.0 + 3.0 * GELU_A * square))
    d_gate = jnp.sum(act * da, axis=-1, keepdims=True)
    d_pre = da * gate * slope

    d_logits = d_gate * gate * (mine - soft)
    d_temp = -jnp.sum(jnp.sum(d_logits * logits, axis=-1, keepdims=True), axis=0, keepdims=True)
    d_raw = d_logits * scale
    d_unit = dot_full(d_raw, vec_unit)
    d_vec = dot_full(d_raw, unit, TN)
    d_vec = vec_inv * (d_vec - vec_unit * jnp.sum(d_vec * vec_unit, axis=-1, keepdims=True))
    d_routed = unit_inv * (d_unit - unit * jnp.sum(d_unit * unit, axis=-1, keepdims=True))

    grads = jnp.concatenate(
        [d_pre, d_routed, jnp.zeros((2 * rows, wide - hidden - router), F32)], axis=1
    )
    high, low = halves(grads)
    dp_high[...], dp_low[...] = high, low
    ga_high[...], ga_low[...] = halves(act * gate)
    d_feed = dot3((high, low), (u_high[...], u_low[...]), NT)
    d_feed_out[...] = d_feed[:rows]
    d_next_out[...] = d_feed[rows:]
    slab[...] = jnp.zeros_like(slab)
    proj = dot3(halves(d_routed), split, TN)
    slab[:router, :] = proj
    slab[router : router + experts, :router] = d_vec
    slab[router + experts : router + experts + 1, :1] = d_temp * scale


def expert_out_kernel(blocks, w_high, w_low, *rest):
    ga, outs = rest[:blocks], rest[blocks:]
    rows = outs[0].shape[0]
    for d in range(blocks // 2):
        part = dot3((ga[2 * d][...], ga[2 * d + 1][...]), (w_high[...], w_low[...]))
        outs[2 * d][...] = part[:rows]
        outs[2 * d + 1][...] = part[rows:]


def expert_grad_kernel(blocks, *rest):
    rest, (up_out, up_sib, down_out, down_sib) = rest[:-4], rest[-4:]
    rest, ga, dp = rest[: -2 * blocks], rest[-2 * blocks : -blocks], rest[-blocks:]
    cots = pair_refs(rest[: len(rest) // 2], blocks // 2)
    feeds = pair_refs(rest[len(rest) // 2 :], blocks // 2)
    hidden = up_out.shape[1]
    for d in range(blocks // 2):
        cot, feed = halves(stack(cots[d])), halves(stack(feeds[d]))
        for i, (up, down) in enumerate(((up_out, down_out), (up_sib, down_sib))):
            part = slice(i * hidden, (i + 1) * hidden)
            down_part = dot3((ga[2 * d][:, part], ga[2 * d + 1][:, part]), cot, TN)
            up_part = dot3(feed, (dp[2 * d][:, part], dp[2 * d + 1][:, part]), TN)
            down[...] = down_part if d == 0 else down[...] + down_part
            up[...] = up_part if d == 0 else up[...] + up_part


def sum_kernel(count, *rest):
    total = rest[0][...]
    for ref in rest[1:count]:
        total = total + ref[...]
    put_blocks(rest[count:], total)


def route_back_kernel(capacity, relative, blocks, ids, hidden, cot, gain, chosen, place, *rest):
    slabs, back, out = rest[: blocks // 2], rest[blocks // 2 : -1], rest[-1]
    rows = hidden.shape[0]
    xhat, inv = normalize(hidden[...])
    onehot = slot_matrix(chosen[...], place[...], ids[1] if relative else 0, capacity)
    slots = jnp.concatenate([b[...] for b in back], axis=0)
    d_normed = place_rows(jnp.transpose(onehot).astype(BF16), slots)
    gain_row = jnp.sum(d_normed * xhat, axis=0, keepdims=True)
    out[:rows, :] = cot[...] + normalize_back(d_normed, gain[...], xhat, inv)
    slab = slabs[0][...]
    for other in slabs[1:]:
        slab = slab + other[...]
    lines = lax.broadcasted_iota(jnp.int32, (slab.shape[0], 1), 0)
    out[rows:, :] = jnp.where(lines == slab.shape[0] - 1, gain_row, slab)


def mixed_kernel(capacity, relative, ids, hidden, chosen, place, *rest):
    back, out = rest[:-1], rest[-1]
    onehot = slot_matrix(chosen[...], place[...], ids[1] if relative else 0, capacity)
    slots = jnp.concatenate([b[...] for b in back], axis=0)
    out[...] = hidden[...] + place_rows(jnp.transpose(onehot).astype(BF16), slots)


def again_kernel(blocks, ids, gain, x, w_q, w_k, w_v, w_o, xhat_out, high_out, low_out, *rest):
    made, split, rel = rest[:3], rest[3:-1], rest[-1]
    relative_rows(ids, x, rel, blocks)
    xhat, _ = normalize(rel[...])
    xhat_out[...] = xhat
    high, low = halves(xhat * gain[...].reshape(1, -1))
    high_out[...], low_out[...] = high, low
    for i, weight in enumerate((w_q, w_k, w_v)):
        split[2 * i][...], split[2 * i + 1][...] = halves(weight[...])
        product = dot3((high, low), (split[2 * i][...], split[2 * i + 1][...]), NT)
        made[i][...] = product * HEAD_DIM**-0.5 if i == 0 else product
    split[6][...], split[7][...] = halves(w_o[...])


def token_rows(refs, rows, blocks):
    whole = [ref[...] for ref in refs[: blocks - 1]] + [stack(refs[blocks - 1 :])]
    others = whole[0][rows:]
    for value in whole[1:]:
        others = others + value[rows:]
    return [value[:rows] for value in whole], others


def attend_back_kernel(blocks, first, ids, seg, q, k, v, o_high, o_low, *rest):
    tokens, width = q.shape
    rows = tokens // blocks
    count = len(rest) - (10 + blocks + 4 if first else 3)
    d_hidden, rest = rest[:count], rest[count:]
    if first:
        before, xhat, split, rest = rest[:3], rest[3], rest[4:10], rest[10:]
        dn_out, (gain_out, dq, dk, dv) = rest[:blocks], rest[blocks:]
        dq[: first * rows, :] = before[0][...]
        dk[...], dv[...] = before[1][...], before[2][...]
    else:
        dq, dk, dv = rest
    row, column = item_mask(ids, seg)
    keys, values = halves(k[...]), halves(v[...])
    here = slice(first * rows, (first + 2) * rows)
    allowed = column == row[:, here]
    grad, _ = token_rows(d_hidden, rows, 2)
    grad = jnp.concatenate(grad, axis=0)
    d_here = dot3(halves(grad), (o_high[...], o_low[...]), NT)
    for h in range(width // HEAD_DIM):
        mask = head_mask(width, h)
        q_head = halves(q[here, :] * mask)
        d_head = halves(d_here * mask)
        scores = jnp.where(allowed, dot3(keys, q_head, NT), -1e30)
        expo = jnp.exp(scores - jnp.max(scores, axis=0, keepdims=True))
        probs = expo * (1.0 / jnp.sum(expo, axis=0, keepdims=True))
        d_probs = dot3(values, d_head, NT)
        delta = jnp.sum(probs * d_probs, axis=0, keepdims=True)
        d_scores = halves(probs * (d_probs - delta))
        d_value = dot3(halves(probs), d_head)
        d_key = dot3(d_scores, q_head)
        d_query = dot3(d_scores, halves(k[...] * (mask * HEAD_DIM**-0.5)), TN)
        new = h == 0 and not first
        dv[...] = d_value if new else dv[...] + d_value
        dk[...] = d_key if new else dk[...] + d_key
        dq[here, :] = d_query if h == 0 else dq[here, :] + d_query
    if not first:
        return
    d_normed = None
    for i, grad in enumerate((dq, dk, dv)):
        part = dot3(halves(grad[...]), (split[2 * i][...], split[2 * i + 1][...]))
        d_normed = part if d_normed is None else d_normed + part
    put_blocks(dn_out, d_normed)
    gain_out[...] = jnp.sum(d_normed * xhat[...], axis=0, keepdims=True)


def small_each(slab_rows, shares):
    return -(-slab_rows // shares)


def weight_grads_kernel(blocks, shares, ids, high, low, dq, dk, dv, ctx, gain, *rest):
    d_hidden, (own, sib, grads, small) = rest[:-4], rest[-4:]
    width = dq.shape[1]
    for i, grad in enumerate((dq, dk, dv)):
        grads[i * width : (i + 1) * width, :] = dot3(halves(grad[...]), (high[...], low[...]), TN)
    rows = ctx.shape[0] // blocks
    total = None
    d_rows, slab = token_rows(d_hidden, rows, blocks)
    for d, part in enumerate(d_rows):
        left = ctx[d * rows : (d + 1) * rows, :]
        product = dot3(halves(left), halves(part), TN)
        total = product if total is None else total + product
    grads[3 * width : 4 * width, :] = total
    count, half = slab.shape[0], 4 * width // (2 * shares)
    each = small_each(count, shares)
    small[...] = jnp.broadcast_to(gain[...], small.shape)
    for i in range(shares):
        few = max(min(each, count - i * each), 0)
        if few:
            small[8 * i : 8 * i + few, :] = slab[i * each : i * each + few]
    many = shares // 2
    for c, out in enumerate((own, sib)):
        for j in range(many):
            index = (ids[0] ^ c) * many + j
            at = j * (half + 8)
            out[at : at + half, :] = pick(grads, 2 * index, half)
            out[at + half : at + half + 8, :] = pick(small, index, 8)
            at = many * (half + 8) + j * half
            out[at : at + half, :] = pick(grads, 2 * index + 1, half)


def track_sums_kernel(ids, own, other, keep_a, send_a, keep_b, send_b):
    size_a, size_b = keep_a.shape[0] // 2, keep_b.shape[0] // 2
    outs = ((keep_a, (0, 2)), (send_a, (1, 3)), (keep_b, (0, 1)), (send_b, (2, 3)))
    for i, (out, planes) in enumerate(outs):
        size, first = (size_a, 0) if i < 2 else (size_b, 4 * size_a)
        for j, k in enumerate(planes):
            here = pl.ds(pl.multiple_of(first + (ids[1] ^ k) * size, 8), size)
            out[j * size : (j + 1) * size, :] = own[here, :] + other[here, :]


def track_halves_kernel(keep_a, got_a, keep_b, got_b, own_a, send_a, own_b, send_b):
    for keep, got, own, send in ((keep_a, got_a, own_a, send_a), (keep_b, got_b, own_b, send_b)):
        size = own.shape[0]
        own[...] = keep[:size, :] + got[:size, :]
        send[...] = keep[size:, :] + got[size:, :]


def join_kernel(own_a, got_a, own_b, got_b, share_a, share_b, gain_out):
    total = own_a[...] + got_a[...]
    share_a[...] = total
    share_b[...] = own_b[...] + got_b[...]
    gain_out[...] = total[-8:]


def pair_kernel(own_a, got_a, own_b, got_b, pair_a, pair_b):
    put_blocks((pair_a,), stack((own_a, got_a)))
    put_blocks((pair_b,), stack((own_b, got_b)))


def norm_back_kernel(ids, x, gain, d_hidden, *rest):
    parts, out = rest[:-1], rest[-1]
    rows = out.shape[0]
    total = parts[0][...]
    for part in parts[1:]:
        total = total + part[...]
    xhat, inv = normalize(pick(x, ids[2], rows))
    out[...] = d_hidden[:rows, :] + normalize_back(total, gain[...], xhat, inv)


def place_blocks_kernel(ids, *rest):
    parts, out = rest[:-1], rest[-1]
    rows = parts[0].shape[0]
    blocks = out.shape[0] // rows
    for d in range(blocks):
        value = parts[d][...] if d < blocks - 1 else stack(parts[d:])
        out[pl.ds(pl.multiple_of((ids[2] ^ d) * rows, rows), rows), :] = value


def finish_kernel(router, experts, shares, tracks, ids, *rest):
    parts, gains, rest = rest[: 2 * tracks], rest[2 * tracks : -11], rest[-11:]
    q_out, k_out, v_out, o_out, g1, g2, proj, vectors, temp, full, small = rest
    width = q_out.shape[0]
    count = -(-(router + experts + 2) // 8) * 8
    half, many = 4 * width // (2 * shares), shares // 2
    each = small_each(count, shares)

    def keep(index, track, value):
        full[pl.ds(pl.multiple_of((2 * index + track) * half, 8), half), :] = value[:half]
        if track == 0:
            small[pl.ds(pl.multiple_of(index * 8, 8), 8), :] = value[half:]

    for c in range(2):
        if tracks == 1:
            part = parts[c]
            for j in range(many):
                at = j * (half + 8)
                keep((ids[0] ^ c) * many + j, 0, part[at : at + half + 8, :])
                at = many * (half + 8) + j * half
                keep((ids[0] ^ c) * many + j, 1, part[at : at + half, :])
            continue
        for i, planes in enumerate(((0, 2), (1, 3), (0, 1), (2, 3))):
            part, track = parts[c * tracks + i], i // 2
            size = part.shape[0] // 2
            for j, k in enumerate(planes):
                index = (ids[0] ^ c) * many + (ids[1] ^ k)
                keep(index, track, part[j * size : (j + 1) * size, :])
    for i in range(1, shares):
        few = max(min(each, count - i * each), 0)
        if few:
            small[i * each : i * each + few, :] = small[8 * i : 8 * i + few, :]
    put_blocks((q_out, k_out, v_out, o_out), full)
    gain = gains[0][-1:, :]
    for other in gains[1:]:
        gain = gain + other[-1:, :]
    g1[...] = gain.reshape(-1)
    g2[...] = small[count - 1 : count, :].reshape(-1)
    proj[...] = small[:router, :]
    vectors[...] = small[router : router + experts, :router]
    temp[...] = small[router + experts : router + experts + 1, :1]


US = dict(
    attend=10, prep=2, up_weights=2, hidden=1, cot_act=4, expert=3, expert_out=1, out_split=1,
    sum_feed=0, expert_grad=10, route_back=0, again=6, sum_out=0, attend_back=6, weight_grads=0,
    norm_back=0, mixed=0, join=0,
)


class Far:
    def __init__(self, buffer, copy, arrives):
        self.buffer, self.copy, self.open = buffer, copy, arrives
        self.shape, self.dtype = buffer.shape, buffer.dtype
        self.next = []

    def wait(self):
        if self.open:
            self.copy.wait()
        self.open = False
        for one in self.next:
            one.copy.start()
        self.next = []

    def send(self):
        self.copy.start()
        self.open = True

    def __getitem__(self, index):
        self.wait()
        return self.buffer[index]

    def __setitem__(self, index, value):
        self.buffer[index] = value


def with_far(kernel, operands, results, early):
    count = len(operands) + len(results)

    def run(*refs):
        refs, buffers, sems = list(refs[: -count - 1]), refs[-count - 1 : -1], refs[-1]
        moved = []
        for j, i in enumerate((*operands, *results)):
            arrives = j < len(operands)
            ends = (refs[i], buffers[j]) if arrives else (buffers[j], refs[i])
            copy = pltpu.make_async_copy(*ends, sems.at[j])
            refs[i] = Far(buffers[j], copy, arrives)
            moved.append(refs[i])
        first = moved[: len(operands)]
        for one in first[:early] if early else first:
            one.copy.start()
        if early:
            first[early - 1].next = first[early:]
        kernel(*refs)
        for one in moved:
            one.wait()

    return run


def call(kernel, ids, args, outs, scratch=(), far=(), raw=(), sent=(), early=0, name=None, us=1):
    whole, there = pl.BlockSpec(memory_space=pltpu.VMEM), pl.BlockSpec(memory_space=pltpu.HBM)
    lead = [] if ids is None else [ids]
    args = list(args)
    scratch_shapes = [pltpu.VMEM(*s) if isinstance(s, tuple) else s for s in scratch]
    if far or sent:
        first = len(lead) + len(args)
        scratch_shapes += [pltpu.VMEM(args[i].shape, args[i].dtype) for i in far]
        scratch_shapes += [pltpu.VMEM(*outs[i]) for i in sent]
        scratch_shapes.append(pltpu.SemaphoreType.DMA((len(far) + len(sent),)))
        kernel = with_far(kernel, [len(lead) + i for i in far], [first + i for i in sent], early)
    for i in (*far, *raw):
        args[i] = pltpu.with_memory_space_constraint(args[i], pltpu.HBM)
    return pl.pallas_call(
        kernel,
        out_shape=[
            pltpu.HBM(s, d) if i in sent else jax.ShapeDtypeStruct(s, d)
            for i, (s, d) in enumerate(outs)
        ],
        in_specs=[pl.BlockSpec(memory_space=pltpu.SMEM)] * len(lead)
        + [there if i in far or i in raw else whole for i in range(len(args))],
        out_specs=[there if i in sent else whole for i in range(len(outs))],
        scratch_shapes=scratch_shapes,
        compiler_params=pltpu.CompilerParams(vmem_limit_bytes=VMEM_LIMIT),
        cost_estimate=cost(us),
        name=name,
    )(*lead, *args)


def cost(us):
    return pl.CostEstimate(flops=int(us * 1.1e9), bytes_accessed=0, transcendentals=0)


def swap(value, axis, shift):
    count = lax.axis_size(axis)
    return lax.ppermute(value, axis, [(i, i ^ shift) for i in range(count)])


def after(values, *done):
    return lax.optimization_barrier((values, done))[0]


def to_planes(blocks):
    if len(blocks) > 1:
        return [blocks[0]] + [swap(b, "ep", k) for k, b in enumerate(blocks) if k]
    return [exchange(blocks[0], "ep")]


def exchange(value, axis):
    count = lax.axis_size(axis)
    split = value.reshape(count, -1, value.shape[-1])
    moved = lax.all_to_all(split, axis, split_axis=0, concat_axis=0, tiled=True)
    return moved.reshape(value.shape)


def gather_blocks(parts):
    return [parts[0]] + [swap(p, "tp", d) for d, p in enumerate(parts) if d]


def gather_tp(block):
    count, cut = lax.axis_size("tp"), 64
    if count != 4:
        return [block] + [swap(block, "tp", d) for d in range(1, count)]
    first, second = swap(block, "tp", 1), swap(block, "tp", 2)
    return [block, first, second, swap(first[:cut], "tp", 2), swap(second[cut:], "tp", 1)]


def body(
    x, passage, gain1, w_q, w_k, w_v, w_o, gain2, w_r, embed, temp, w_up, w_down, chosen, place, cot
):
    blocks, planes = lax.axis_size("tp"), lax.axis_size("ep")
    ids = jnp.stack([lax.axis_index("dp"), lax.axis_index("ep"), lax.axis_index("tp")])
    ids = ids.astype(jnp.int32)
    tokens, width = x.shape
    rows, local = tokens // blocks, w_q.shape[1]
    w_q, w_k, w_v, w_r = w_q.T, w_k.T, w_v.T, w_r.T
    experts, router = embed.shape
    hidden_units = w_up.shape[2]
    capacity = rows // experts
    pieces = planes if planes <= 4 else 1
    relative = pieces > 1
    slot_shapes = [((rows // pieces, width), F32)] * pieces
    wide = -(-(2 * hidden_units + router) // 128) * 128
    slab_rows = -(-(router + experts + 2) // 8) * 8
    w_up, w_down = w_up[0], w_down[0]
    chosen, place = chosen.reshape(1, rows), place.reshape(1, rows)
    gain1_line, gain1, gain2 = gain1, gain1.reshape(1, width), gain2.reshape(1, width)
    seg = passage.reshape(blocks, rows)
    temp = temp.reshape(1, 1)

    ctx, *parts = call(
        functools.partial(attend_kernel, blocks), ids, [seg, gain1_line, x, w_q, w_k, w_v, w_o],
        [((tokens, local), F32)] + [((rows, width), F32)] * blocks,
        [((tokens, width), F32)] + [((tokens, local), F32)] * 3
        + [pltpu.SemaphoreType.DMA((blocks,))],
        far=(0, 1, 3, 4, 5, 6), raw=(2,), early=2, name="attend", us=US["attend"],
    )
    got = gather_blocks(parts)
    w_up_sib, w_down_sib = swap(w_up, "dp", 1), swap(w_down, "dp", 1)
    slots = call(
        functools.partial(prep_kernel, capacity, relative), ids,
        [chosen, place, after(cot, *parts, w_up_sib, w_down_sib)], slot_shapes, far=(0, 1, 2), name="prep",
        us=US["prep"],
    )
    cot_slots = to_planes(slots)
    u_high, u_low = call(
        up_weights_kernel, None, [w_up, w_up_sib, w_r], [((width, wide), BF16)] * 2, name="up_weights",
        us=US["up_weights"],
    )
    cot_rows = jnp.concatenate(cot_slots, axis=0)
    cots = gather_tp(after(cot_rows, *got))
    hidden, *slots = call(
        functools.partial(hidden_kernel, capacity, relative, blocks), ids,
        [x, gain2, chosen, place, *after(got, u_high, cot_rows)], [((rows, width), F32)] + slot_shapes,
        name="hidden", us=US["hidden"],
    )

    same = gather_tp(jnp.concatenate(to_planes(slots), axis=0))
    act_shape = [((2 * rows, 2 * hidden_units), F32)]
    first, w_high, w_low = call(
        cot_kernel, None, [w_down, w_down_sib, *after(cots[:2], hidden)],
        act_shape + [((2 * hidden_units, width), BF16)] * 2, name="cot_act", us=US["cot_act"],
    )
    act_grads = [first]
    ga, dp, slabs, parts = [], [], [], []
    for d in range(0, blocks, 2):
        if d:
            ends = cots[d : d + 2] if d + 2 < blocks else cots[d:]
            act_grads += call(
                cot_rest_kernel, None, [w_high, w_low, *after(ends, *slabs)], act_shape,
                name="cot_act_rest", us=0,
            )
        *d_feeds, ga_high, ga_low, dp_high, dp_low, slab = call(
            expert_kernel, ids,
            [act_grads[d // 2], u_high, u_low, embed, temp]
            + after(same[d : d + 2] if d + 2 < blocks else same[d:], *slabs),
            [((rows, width), F32)] * 2
            + [((2 * rows, 2 * hidden_units), BF16)] * 2
            + [((2 * rows, wide), BF16)] * 2
            + [((slab_rows, width), F32)],
            name="expert", us=US["expert"],
        )
        ga += [ga_high, ga_low]
        dp += [dp_high, dp_low]
        slabs.append(slab)
        parts += [swap(f, "tp", d + i) if d + i else f for i, f in enumerate(d_feeds)]
    outs = call(
        functools.partial(expert_out_kernel, blocks), None, [w_high, w_low, *ga],
        [((rows, width), F32)] * blocks, name="expert_out", us=US["expert_out"],
    )
    pieces_back = call(
        functools.partial(sum_kernel, blocks), None, after(parts, *outs), slot_shapes,
        name="sum_feed", us=US["sum_feed"],
    )
    back = to_planes(pieces_back)
    grad_up, up_sib, grad_down, down_sib = call(
        functools.partial(expert_grad_kernel, blocks), None,
        [*after(cots, *pieces_back), *same, *ga, *dp],
        [((width, hidden_units), F32)] * 2 + [((hidden_units, width), F32)] * 2,
        name="expert_grad", us=US["expert_grad"],
    )
    (d_hidden,) = call(
        functools.partial(route_back_kernel, capacity, relative, blocks), ids,
        [hidden, cot, gain2, chosen, place, *slabs, *after(back, grad_up)],
        [((rows + slab_rows, width), F32)], name="route_back", us=US["route_back"],
    )

    up_got, down_got = swap(up_sib, "dp", 1), swap(down_sib, "dp", 1)

    d_hiddens = gather_tp(d_hidden)
    xhat, high, low, q, k, v, *split = call(
        functools.partial(again_kernel, blocks), ids,
        [gain1_line, after(x, d_hidden), w_q, w_k, w_v, w_o],
        [((tokens, width), F32)] + [((tokens, width), BF16)] * 2 + [((tokens, local), F32)] * 3
        + [((local, width), BF16)] * 8,
        [((tokens, width), F32)], far=(0, 1, 2, 3, 4, 5), early=2, name="again", us=US["again"],
    )
    half_grads = call(
        functools.partial(attend_back_kernel, blocks, 0), ids,
        [seg, q, k, v, *split[6:], *after(d_hiddens[:2], high)],
        [((2 * rows, local), F32)] + [((tokens, local), F32)] * 2, name="attend_back",
        us=US["attend_back"],
    )
    *dn, gain_row, dq, dk, dv = call(
        functools.partial(attend_back_kernel, blocks, 2), ids,
        [seg, q, k, v, *split[6:], *after(d_hiddens[2:], *half_grads, up_got, down_got), *half_grads, xhat]
        + split[:6],
        [((rows, width), F32)] * blocks + [((1, width), F32)] + [((tokens, local), F32)] * 3,
        name="attend_back_rest", us=US["attend_back"],
    )
    dn_got = gather_blocks(dn)
    shares, tracked = 8, planes == 4
    half = 4 * local // (2 * shares)
    size_a, size_b = half + 8, half
    own_part, sib_part = call(
        functools.partial(weight_grads_kernel, blocks, shares), ids,
        [high, low, dq, dk, dv, ctx, gain_row, *d_hiddens],
        [((shares // 2 * (size_a + size_b), width), F32)] * 2,
        [((4 * local, width), F32), ((8 * shares, width), F32)], name="weight_grads",
        us=US["weight_grads"],
    )
    other_part = swap(sib_part, "dp", 1)
    grad_up, grad_down = grad_up + up_got, grad_down + down_got
    dn_got = after(dn_got, grad_up, grad_down)
    if tracked:
        keep_a, send_a, keep_b, send_b = call(
            track_sums_kernel, ids, [own_part, other_part],
            [((2 * size_a, width), F32)] * 2 + [((2 * size_b, width), F32)] * 2,
            name="track_sums", us=0,
        )
        got_a, got_b = swap(send_a, "ep", 1), swap(send_b, "ep", 2)
        dn_got = after(dn_got, keep_a)
    (d_x,) = call(
        norm_back_kernel, ids, [x, gain1, d_hidden, *dn_got], [((rows, width), F32)],
        name="norm_back", us=US["norm_back"],
    )
    d_xs = gather_tp(d_x)
    if tracked:
        own_a, send_a, own_b, send_b = call(
            track_halves_kernel, None, [keep_a, got_a, keep_b, got_b],
            [((size_a, width), F32)] * 2 + [((size_b, width), F32)] * 2, name="track_halves",
            us=0,
        )
        share_a, share_b, gain = call(
            join_kernel, None, [own_a, swap(send_a, "ep", 2), own_b, swap(send_b, "ep", 1)],
            [((size_a, width), F32), ((size_b, width), F32), ((8, width), F32)], name="join",
            us=US["join"],
        )
        pair_a, pair_b = call(
            pair_kernel, None, [share_a, swap(share_a, "ep", 2), share_b, swap(share_b, "ep", 1)],
            [((2 * size_a, width), F32), ((2 * size_b, width), F32)], name="pair", us=0,
        )
        parts = [pair_a, swap(pair_a, "ep", 1), pair_b, swap(pair_b, "ep", 2)]
    else:
        parts = [lax.psum(own_part + other_part, "ep")]
        share_a, gain = parts[0], parts[0][half : half + 8]
    tracks = len(parts)
    parts = parts + [swap(p, "dp", 1) for p in parts]
    gains = gather_blocks([after(gain, *parts[tracks:])] * blocks)
    near = after(outs, share_a)
    parts_out = gather_blocks(near)
    out_pieces = call(
        functools.partial(sum_kernel, blocks), None, parts_out, slot_shapes, name="sum_out",
        us=US["sum_out"],
    )
    out_slots = to_planes(out_pieces)
    (mixed,) = call(
        functools.partial(mixed_kernel, capacity, relative), ids,
        [hidden, chosen, place, *out_slots], [((rows, width), F32)],
        name="mixed", us=US["mixed"],
    )
    (grad_tokens,) = call(
        place_blocks_kernel, ids, d_xs, [((tokens, width), F32)],
        name="grad_tokens", us=0,
    )
    grad_q, grad_k, grad_v, grad_o, grad_g1, grad_g2, grad_proj, grad_embed, grad_temp = call(
        functools.partial(finish_kernel, router, experts, shares, tracks), ids,
        [*parts, *gains],
        [((local, width), F32)] * 4 + [((width,), F32)] * 2 + [((router, width), F32)]
        + [((experts, router), F32), ((1, 1), F32)],
        [((4 * local, width), F32), ((8 * shares, width), F32)], name="finish", us=0,
    )
    return (
        mixed,
        grad_tokens,
        grad_g1,
        grad_q.T,
        grad_k.T,
        grad_v.T,
        grad_o,
        grad_g2,
        grad_proj.T,
        grad_embed,
        grad_temp.reshape(1),
        grad_up[None],
        grad_down[None],
    )


def solution(mesh):
    in_specs = (
        P(("dp", "ep"), None),
        P(("dp", "ep")),
        P(),
        P(None, "tp"),
        P(None, "tp"),
        P(None, "tp"),
        P("tp", None),
        P(),
        P(),
        P(),
        P(),
        P("ep", None, ("dp", "tp")),
        P("ep", ("dp", "tp"), None),
        P(("dp", "ep", "tp")),
        P(("dp", "ep", "tp")),
        P(("dp", "ep", "tp"), None),
    )
    out_specs = (
        P(("dp", "ep", "tp"), None),
        P(("dp", "ep"), None),
        P(),
        P(None, "tp"),
        P(None, "tp"),
        P(None, "tp"),
        P("tp", None),
        P(),
        P(),
        P(),
        P(),
        P("ep", None, ("dp", "tp")),
        P("ep", ("dp", "tp"), None),
    )
    return jax.shard_map(body, mesh=mesh, in_specs=in_specs, out_specs=out_specs, check_vma=False)
```

```python
import functools

import jax
import jax.numpy as jnp
from jax import lax
from jax.experimental import pallas as pl
from jax.experimental.pallas import tpu as pltpu
from jax.sharding import PartitionSpec as P

HEAD_DIM = 64
EPS = 1e-05
F32 = jnp.float32
BF16 = jnp.bfloat16
NN = (((1,), (0,)), ((), ()))
NT = (((1,), (1,)), ((), ()))
TN = (((0,), (0,)), ((), ()))
VMEM_LIMIT = 24 * 1024 * 1024
GELU_C = 0.7978845608028654
GELU_A = 0.044715


def halves(value):
    high = value.astype(BF16)
    return high, (value - high.astype(F32)).astype(BF16)


def dot1(left, right, dims):
    return lax.dot_general(left, right, dims, preferred_element_type=F32)


def dot3(left, right, dims=NN):
    small = dot1(left[0], right[1], dims) + dot1(left[1], right[0], dims)
    return small + dot1(left[0], right[0], dims)


def dot_full(left, right, dims=NN):
    return lax.dot_general(
        left, right, dims, precision=lax.Precision.HIGHEST, preferred_element_type=F32
    )


def place_rows(onehot, value, dims=NN):
    first = value.astype(BF16)
    rest = value - first.astype(F32)
    second = rest.astype(BF16)
    third = (rest - second.astype(F32)).astype(BF16)
    small = dot1(onehot, second, dims) + dot1(onehot, third, dims)
    return dot1(onehot, first, dims) + small


def normalize(values):
    center = values - jnp.mean(values, axis=-1, keepdims=True)
    inv = lax.rsqrt(jnp.mean(center * center, axis=-1, keepdims=True) + EPS)
    return center * inv, inv


def normalize_back(grad, gain, xhat, inv):
    scaled = grad * gain
    first = jnp.mean(scaled, axis=-1, keepdims=True)
    second = jnp.mean(scaled * xhat, axis=-1, keepdims=True)
    return inv * (scaled - first - xhat * second)


def slot_matrix(chosen_row, place_row, base, capacity):
    count = chosen_row.shape[1]
    column = (chosen_row ^ base) * capacity + place_row
    column = jnp.where(place_row >= 0, column, -1)
    slots = lax.broadcasted_iota(jnp.int32, (count, count), 0)
    return jnp.where(slots == column, 1.0, 0.0)


def pick(ref, index, size):
    return ref[pl.ds(pl.multiple_of(index * size, size), size), :]


def put_blocks(outs, value):
    size = outs[0].shape[0]
    for k, out in enumerate(outs):
        out[...] = value[k * size : (k + 1) * size]


def prep_kernel(capacity, relative, ids, chosen, place, cot, *slots_out):
    onehot = slot_matrix(chosen[...], place[...], ids[1] if relative else 0, capacity)
    put_blocks(slots_out, place_rows(onehot.astype(BF16), cot[...]))


def relative_rows(ids, x, out, blocks):
    size = x.shape[0] // blocks
    for d in range(blocks):
        out[d * size : (d + 1) * size, :] = pick(x, ids[2] ^ d, size)


def item_mask(ids, seg):
    row = [seg[pl.ds(ids[2] ^ d, 1), :] for d in range(seg.shape[0])]
    row = jnp.concatenate(row, axis=1).astype(F32)
    return row, jnp.transpose(jnp.broadcast_to(row, (8, row.shape[1])))[:, :1]


def head_mask(width, head):
    lane = lax.broadcasted_iota(jnp.int32, (1, width), 1)
    return jnp.where(lane // HEAD_DIM == head, 1.0, 0.0)


def attend_kernel(blocks, ids, seg, gain, x, w_q, w_k, w_v, w_o, ctx_out, *rest):
    part_out, (rel, query, key, value, sems) = rest[:blocks], rest[blocks:]
    tokens, width = x.shape[0], w_q.shape[0]
    size = tokens // blocks
    copies = []
    for d in range(blocks):
        there = pl.ds(pl.multiple_of((ids[2] ^ d) * size, size), size)
        here = rel.at[d * size : (d + 1) * size, :]
        copies.append(pltpu.make_async_copy(x.at[there, :], here, sems.at[d]))
        copies[-1].start()
    scale, normed = gain[...].reshape(1, -1), []
    for d, copy in enumerate(copies):
        copy.wait()
        xhat, _ = normalize(rel[d * size : (d + 1) * size, :])
        normed.append(halves(xhat * scale))
    normed = [jnp.concatenate(part, axis=0) for part in zip(*normed)]
    query[...] = dot3(normed, halves(w_q[...]), NT) * HEAD_DIM**-0.5
    key[...] = dot3(normed, halves(w_k[...]), NT)
    value[...] = dot3(normed, halves(w_v[...]), NT)
    row, column = item_mask(ids, seg)
    keys = halves(key[...])
    weight = halves(w_o[...])
    chunk = tokens
    rows = tokens // blocks
    for c in range(tokens // chunk):
        here = slice(c * chunk, (c + 1) * chunk)
        allowed = column[here] == row
        total = None
        for h in range(width // HEAD_DIM):
            mask = head_mask(width, h)
            scores = dot3(halves(query[here, :] * mask), keys, NT)
            scores = jnp.where(allowed, scores, -1e30)
            expo = jnp.exp(scores - jnp.max(scores, axis=-1, keepdims=True))
            norm = 1.0 / jnp.sum(expo, axis=-1, keepdims=True)
            part = dot3(halves(expo), halves(value[...] * mask)) * norm
            total = part if total is None else total + part
        ctx_out[here, :] = total
        product = dot3(halves(total), weight)
        for i in range(chunk // rows):
            part_out[c * (chunk // rows) + i][...] = product[i * rows : (i + 1) * rows]


def up_weights_kernel(w_up, w_up_sib, w_r, u_high, u_low):
    hidden = w_up.shape[1]
    u_high[:, :hidden], u_low[:, :hidden] = halves(w_up[...])
    u_high[:, hidden : 2 * hidden], u_low[:, hidden : 2 * hidden] = halves(w_up_sib[...])
    pad = u_high.shape[1] - 2 * hidden - w_r.shape[0]
    route = jnp.concatenate([w_r[...], jnp.zeros((pad, w_r.shape[1]), F32)], axis=0)
    u_high[:, 2 * hidden :], u_low[:, 2 * hidden :] = halves(jnp.transpose(route))


def hidden_kernel(capacity, relative, blocks, ids, x, gain, chosen, place, *rest):
    parts, hidden_out, slots_out = rest[:blocks], rest[blocks], rest[blocks + 1 :]
    total = parts[0][...]
    for part in parts[1:]:
        total = total + part[...]
    hidden = pick(x, ids[2], hidden_out.shape[0]) + total
    hidden_out[...] = hidden
    xhat, _ = normalize(hidden)
    onehot = slot_matrix(chosen[...], place[...], ids[1] if relative else 0, capacity)
    put_blocks(slots_out, place_rows(onehot.astype(BF16), xhat * gain[...]))


def stack(refs):
    return jnp.concatenate([ref[...] for ref in refs], axis=0)


def pair_refs(refs, pairs):
    return [refs[2 * d : 2 * d + 2] for d in range(pairs - 1)] + [refs[2 * pairs - 2 :]]


def cot_kernel(w_down, w_down_sib, *rest):
    cots, (out, w_high, w_low) = rest[:-3], rest[-3:]
    hidden = w_down.shape[0]
    w_high[:hidden, :], w_low[:hidden, :] = halves(w_down[...])
    w_high[hidden:, :], w_low[hidden:, :] = halves(w_down_sib[...])
    out[...] = dot3(halves(stack(cots)), (w_high[...], w_low[...]), NT)


def cot_rest_kernel(w_high, w_low, *rest):
    rest[-1][...] = dot3(halves(stack(rest[:-1])), (w_high[...], w_low[...]), NT)


def expert_kernel(ids, act_grad, u_high, u_low, embed, temp, *rest):
    feeds, (d_feed_out, d_next_out, ga_high, ga_low, dp_high, dp_low, slab) = rest[:-7], rest[-7:]
    rows = d_feed_out.shape[0]
    hidden = act_grad.shape[1]
    experts, router = embed.shape
    wide = u_high.shape[1]
    split = halves(stack(feeds))
    both = dot3(split, (u_high[...], u_low[...]))
    pre, routed = both[:, :hidden], both[:, hidden : hidden + router]
    da = act_grad[...]

    unit_inv = lax.rsqrt(jnp.sum(routed * routed, axis=-1, keepdims=True) + 1.0)
    unit = routed * unit_inv
    vectors = embed[...]
    vec_inv = lax.rsqrt(jnp.sum(vectors * vectors, axis=-1, keepdims=True) + 1.0)
    vec_unit = vectors * vec_inv
    scale = 1.0 / temp[0, 0]
    logits = dot_full(unit, vec_unit, NT) * scale
    soft = jnp.exp(logits - jnp.max(logits, axis=-1, keepdims=True))
    soft = soft / jnp.sum(soft, axis=-1, keepdims=True)
    mine = jnp.where(lax.broadcasted_iota(jnp.int32, (1, experts), 1) == ids[1], 1.0, 0.0)
    gate = jnp.sum(soft * mine, axis=-1, keepdims=True)

    square = pre * pre
    bend = jnp.tanh(GELU_C * (pre + GELU_A * pre * square))
    side = 0.5 * (1.0 + bend)
    act = pre * side
    slope = side + 0.5 * pre * (1.0 - bend * bend) * (GELU_C * (1.0 + 3.0 * GELU_A * square))
    d_gate = jnp.sum(act * da, axis=-1, keepdims=True)
    d_pre = da * gate * slope

    d_logits = d_gate * gate * (mine - soft)
    d_temp = -jnp.sum(jnp.sum(d_logits * logits, axis=-1, keepdims=True), axis=0, keepdims=True)
    d_raw = d_logits * scale
    d_unit = dot_full(d_raw, vec_unit)
    d_vec = dot_full(d_raw, unit, TN)
    d_vec = vec_inv * (d_vec - vec_unit * jnp.sum(d_vec * vec_unit, axis=-1, keepdims=True))
    d_routed = unit_inv * (d_unit - unit * jnp.sum(d_unit * unit, axis=-1, keepdims=True))

    grads = jnp.concatenate(
        [d_pre, d_routed, jnp.zeros((2 * rows, wide - hidden - router), F32)], axis=1
    )
    high, low = halves(grads)
    dp_high[...], dp_low[...] = high, low
    ga_high[...], ga_low[...] = halves(act * gate)
    d_feed = dot3((high, low), (u_high[...], u_low[...]), NT)
    d_feed_out[...] = d_feed[:rows]
    d_next_out[...] = d_feed[rows:]
    slab[...] = jnp.zeros_like(slab)
    proj = dot3(halves(d_routed), split, TN)
    slab[:router, :] = proj
    slab[router : router + experts, :router] = d_vec
    slab[router + experts : router + experts + 1, :1] = d_temp * scale


def expert_out_kernel(blocks, w_high, w_low, *rest):
    ga, outs = rest[:blocks], rest[blocks:]
    rows = outs[0].shape[0]
    for d in range(blocks // 2):
        part = dot3((ga[2 * d][...], ga[2 * d + 1][...]), (w_high[...], w_low[...]))
        outs[2 * d][...] = part[:rows]
        outs[2 * d + 1][...] = part[rows:]


def expert_grad_kernel(blocks, *rest):
    rest, (up_out, up_sib, down_out, down_sib) = rest[:-4], rest[-4:]
    rest, ga, dp = rest[: -2 * blocks], rest[-2 * blocks : -blocks], rest[-blocks:]
    cots = pair_refs(rest[: len(rest) // 2], blocks // 2)
    feeds = pair_refs(rest[len(rest) // 2 :], blocks // 2)
    hidden = up_out.shape[1]
    for d in range(blocks // 2):
        cot, feed = halves(stack(cots[d])), halves(stack(feeds[d]))
        for i, (up, down) in enumerate(((up_out, down_out), (up_sib, down_sib))):
            part = slice(i * hidden, (i + 1) * hidden)
            down_part = dot3((ga[2 * d][:, part], ga[2 * d + 1][:, part]), cot, TN)
            up_part = dot3(feed, (dp[2 * d][:, part], dp[2 * d + 1][:, part]), TN)
            down[...] = down_part if d == 0 else down[...] + down_part
            up[...] = up_part if d == 0 else up[...] + up_part


def sum_kernel(count, *rest):
    total = rest[0][...]
    for ref in rest[1:count]:
        total = total + ref[...]
    put_blocks(rest[count:], total)


def route_back_kernel(capacity, relative, blocks, ids, hidden, cot, gain, chosen, place, *rest):
    slabs, back, out = rest[: blocks // 2], rest[blocks // 2 : -1], rest[-1]
    rows = hidden.shape[0]
    xhat, inv = normalize(hidden[...])
    onehot = slot_matrix(chosen[...], place[...], ids[1] if relative else 0, capacity)
    slots = jnp.concatenate([b[...] for b in back], axis=0)
    d_normed = place_rows(jnp.transpose(onehot).astype(BF16), slots)
    gain_row = jnp.sum(d_normed * xhat, axis=0, keepdims=True)
    out[:rows, :] = cot[...] + normalize_back(d_normed, gain[...], xhat, inv)
    slab = slabs[0][...]
    for other in slabs[1:]:
        slab = slab + other[...]
    lines = lax.broadcasted_iota(jnp.int32, (slab.shape[0], 1), 0)
    out[rows:, :] = jnp.where(lines == slab.shape[0] - 1, gain_row, slab)


def mixed_kernel(capacity, relative, ids, hidden, chosen, place, *rest):
    back, out = rest[:-1], rest[-1]
    onehot = slot_matrix(chosen[...], place[...], ids[1] if relative else 0, capacity)
    slots = jnp.concatenate([b[...] for b in back], axis=0)
    out[...] = hidden[...] + place_rows(jnp.transpose(onehot).astype(BF16), slots)


def again_kernel(blocks, ids, gain, x, w_q, w_k, w_v, w_o, xhat_out, high_out, low_out, *rest):
    made, split, rel = rest[:3], rest[3:-1], rest[-1]
    relative_rows(ids, x, rel, blocks)
    xhat, _ = normalize(rel[...])
    xhat_out[...] = xhat
    high, low = halves(xhat * gain[...].reshape(1, -1))
    high_out[...], low_out[...] = high, low
    for i, weight in enumerate((w_q, w_k, w_v)):
        split[2 * i][...], split[2 * i + 1][...] = halves(weight[...])
        product = dot3((high, low), (split[2 * i][...], split[2 * i + 1][...]), NT)
        made[i][...] = product * HEAD_DIM**-0.5 if i == 0 else product
    split[6][...], split[7][...] = halves(w_o[...])


def token_rows(refs, rows, blocks):
    whole = [ref[...] for ref in refs[: blocks - 1]] + [stack(refs[blocks - 1 :])]
    others = whole[0][rows:]
    for value in whole[1:]:
        others = others + value[rows:]
    return [value[:rows] for value in whole], others


def attend_back_kernel(blocks, first, ids, seg, q, k, v, o_high, o_low, *rest):
    tokens, width = q.shape
    rows = tokens // blocks
    count = len(rest) - (10 + blocks + 4 if first else 3)
    d_hidden, rest = rest[:count], rest[count:]
    if first:
        before, xhat, split, rest = rest[:3], rest[3], rest[4:10], rest[10:]
        dn_out, (gain_out, dq, dk, dv) = rest[:blocks], rest[blocks:]
        dq[: first * rows, :] = before[0][...]
        dk[...], dv[...] = before[1][...], before[2][...]
    else:
        dq, dk, dv = rest
    row, column = item_mask(ids, seg)
    keys, values = halves(k[...]), halves(v[...])
    here = slice(first * rows, (first + 2) * rows)
    allowed = column == row[:, here]
    grad, _ = token_rows(d_hidden, rows, 2)
    grad = jnp.concatenate(grad, axis=0)
    d_here = dot3(halves(grad), (o_high[...], o_low[...]), NT)
    for h in range(width // HEAD_DIM):
        mask = head_mask(width, h)
        q_head = halves(q[here, :] * mask)
        d_head = halves(d_here * mask)
        scores = jnp.where(allowed, dot3(keys, q_head, NT), -1e30)
        expo = jnp.exp(scores - jnp.max(scores, axis=0, keepdims=True))
        probs = expo * (1.0 / jnp.sum(expo, axis=0, keepdims=True))
        d_probs = dot3(values, d_head, NT)
        delta = jnp.sum(probs * d_probs, axis=0, keepdims=True)
        d_scores = halves(probs * (d_probs - delta))
        d_value = dot3(halves(probs), d_head)
        d_key = dot3(d_scores, q_head)
        d_query = dot3(d_scores, halves(k[...] * (mask * HEAD_DIM**-0.5)), TN)
        new = h == 0 and not first
        dv[...] = d_value if new else dv[...] + d_value
        dk[...] = d_key if new else dk[...] + d_key
        dq[here, :] = d_query if h == 0 else dq[here, :] + d_query
    if not first:
        return
    d_normed = None
    for i, grad in enumerate((dq, dk, dv)):
        part = dot3(halves(grad[...]), (split[2 * i][...], split[2 * i + 1][...]))
        d_normed = part if d_normed is None else d_normed + part
    put_blocks(dn_out, d_normed)
    gain_out[...] = jnp.sum(d_normed * xhat[...], axis=0, keepdims=True)


def small_each(slab_rows, shares):
    return -(-slab_rows // shares)


def weight_grads_kernel(blocks, shares, ids, high, low, dq, dk, dv, ctx, gain, *rest):
    d_hidden, (own, sib, grads, small) = rest[:-4], rest[-4:]
    width = dq.shape[1]
    for i, grad in enumerate((dq, dk, dv)):
        grads[i * width : (i + 1) * width, :] = dot3(halves(grad[...]), (high[...], low[...]), TN)
    rows = ctx.shape[0] // blocks
    total = None
    d_rows, slab = token_rows(d_hidden, rows, blocks)
    for d, part in enumerate(d_rows):
        left = ctx[d * rows : (d + 1) * rows, :]
        product = dot3(halves(left), halves(part), TN)
        total = product if total is None else total + product
    grads[3 * width : 4 * width, :] = total
    count, half = slab.shape[0], 4 * width // (2 * shares)
    each = small_each(count, shares)
    small[...] = jnp.broadcast_to(gain[...], small.shape)
    for i in range(shares):
        few = max(min(each, count - i * each), 0)
        if few:
            small[8 * i : 8 * i + few, :] = slab[i * each : i * each + few]
    many = shares // 2
    for c, out in enumerate((own, sib)):
        for j in range(many):
            index = (ids[0] ^ c) * many + j
            at = j * (half + 8)
            out[at : at + half, :] = pick(grads, 2 * index, half)
            out[at + half : at + half + 8, :] = pick(small, index, 8)
            at = many * (half + 8) + j * half
            out[at : at + half, :] = pick(grads, 2 * index + 1, half)


def track_sums_kernel(ids, own, other, keep_a, send_a, keep_b, send_b):
    size_a, size_b = keep_a.shape[0] // 2, keep_b.shape[0] // 2
    outs = ((keep_a, (0, 2)), (send_a, (1, 3)), (keep_b, (0, 1)), (send_b, (2, 3)))
    for i, (out, planes) in enumerate(outs):
        size, first = (size_a, 0) if i < 2 else (size_b, 4 * size_a)
        for j, k in enumerate(planes):
            here = pl.ds(pl.multiple_of(first + (ids[1] ^ k) * size, 8), size)
            out[j * size : (j + 1) * size, :] = own[here, :] + other[here, :]


def track_halves_kernel(keep_a, got_a, keep_b, got_b, own_a, send_a, own_b, send_b):
    for keep, got, own, send in ((keep_a, got_a, own_a, send_a), (keep_b, got_b, own_b, send_b)):
        size = own.shape[0]
        own[...] = keep[:size, :] + got[:size, :]
        send[...] = keep[size:, :] + got[size:, :]


def join_kernel(own_a, got_a, own_b, got_b, share_a, share_b, gain_out):
    total = own_a[...] + got_a[...]
    share_a[...] = total
    share_b[...] = own_b[...] + got_b[...]
    gain_out[...] = total[-8:]


def pair_kernel(own_a, got_a, own_b, got_b, pair_a, pair_b):
    put_blocks((pair_a,), stack((own_a, got_a)))
    put_blocks((pair_b,), stack((own_b, got_b)))


def norm_back_kernel(ids, x, gain, d_hidden, *rest):
    parts, out = rest[:-1], rest[-1]
    rows = out.shape[0]
    total = parts[0][...]
    for part in parts[1:]:
        total = total + part[...]
    xhat, inv = normalize(pick(x, ids[2], rows))
    out[...] = d_hidden[:rows, :] + normalize_back(total, gain[...], xhat, inv)


def place_blocks_kernel(ids, *rest):
    parts, out = rest[:-1], rest[-1]
    rows = parts[0].shape[0]
    blocks = out.shape[0] // rows
    for d in range(blocks):
        value = parts[d][...] if d < blocks - 1 else stack(parts[d:])
        out[pl.ds(pl.multiple_of((ids[2] ^ d) * rows, rows), rows), :] = value


def finish_kernel(router, experts, shares, tracks, ids, *rest):
    parts, gains, rest = rest[: 2 * tracks], rest[2 * tracks : -11], rest[-11:]
    q_out, k_out, v_out, o_out, g1, g2, proj, vectors, temp, full, small = rest
    width = q_out.shape[0]
    count = -(-(router + experts + 2) // 8) * 8
    half, many = 4 * width // (2 * shares), shares // 2
    each = small_each(count, shares)

    def keep(index, track, value):
        full[pl.ds(pl.multiple_of((2 * index + track) * half, 8), half), :] = value[:half]
        if track == 0:
            small[pl.ds(pl.multiple_of(index * 8, 8), 8), :] = value[half:]

    for c in range(2):
        if tracks == 1:
            part = parts[c]
            for j in range(many):
                at = j * (half + 8)
                keep((ids[0] ^ c) * many + j, 0, part[at : at + half + 8, :])
                at = many * (half + 8) + j * half
                keep((ids[0] ^ c) * many + j, 1, part[at : at + half, :])
            continue
        for i, planes in enumerate(((0, 2), (1, 3), (0, 1), (2, 3))):
            part, track = parts[c * tracks + i], i // 2
            size = part.shape[0] // 2
            for j, k in enumerate(planes):
                index = (ids[0] ^ c) * many + (ids[1] ^ k)
                keep(index, track, part[j * size : (j + 1) * size, :])
    for i in range(1, shares):
        few = max(min(each, count - i * each), 0)
        if few:
            small[i * each : i * each + few, :] = small[8 * i : 8 * i + few, :]
    put_blocks((q_out, k_out, v_out, o_out), full)
    gain = gains[0][-1:, :]
    for other in gains[1:]:
        gain = gain + other[-1:, :]
    g1[...] = gain.reshape(-1)
    g2[...] = small[count - 1 : count, :].reshape(-1)
    proj[...] = small[:router, :]
    vectors[...] = small[router : router + experts, :router]
    temp[...] = small[router + experts : router + experts + 1, :1]


US = dict(
    attend=10, prep=2, up_weights=2, hidden=1, cot_act=4, expert=3, expert_out=1, out_split=1,
    sum_feed=0, expert_grad=10, route_back=0, again=6, sum_out=0, attend_back=6, weight_grads=0,
    norm_back=0, mixed=0, join=0,
)


class Far:
    def __init__(self, buffer, copy, arrives):
        self.buffer, self.copy, self.open = buffer, copy, arrives
        self.shape, self.dtype = buffer.shape, buffer.dtype
        self.next = []

    def wait(self):
        if self.open:
            self.copy.wait()
        self.open = False
        for one in self.next:
            one.copy.start()
        self.next = []

    def send(self):
        self.copy.start()
        self.open = True

    def __getitem__(self, index):
        self.wait()
        return self.buffer[index]

    def __setitem__(self, index, value):
        self.buffer[index] = value


def with_far(kernel, operands, results, early):
    count = len(operands) + len(results)

    def run(*refs):
        refs, buffers, sems = list(refs[: -count - 1]), refs[-count - 1 : -1], refs[-1]
        moved = []
        for j, i in enumerate((*operands, *results)):
            arrives = j < len(operands)
            ends = (refs[i], buffers[j]) if arrives else (buffers[j], refs[i])
            copy = pltpu.make_async_copy(*ends, sems.at[j])
            refs[i] = Far(buffers[j], copy, arrives)
            moved.append(refs[i])
        first = moved[: len(operands)]
        for one in first[:early] if early else first:
            one.copy.start()
        if early:
            first[early - 1].next = first[early:]
        kernel(*refs)
        for one in moved:
            one.wait()

    return run


def call(kernel, ids, args, outs, scratch=(), far=(), raw=(), sent=(), early=0, name=None, us=1):
    whole, there = pl.BlockSpec(memory_space=pltpu.VMEM), pl.BlockSpec(memory_space=pltpu.HBM)
    lead = [] if ids is None else [ids]
    args = list(args)
    scratch_shapes = [pltpu.VMEM(*s) if isinstance(s, tuple) else s for s in scratch]
    if far or sent:
        first = len(lead) + len(args)
        scratch_shapes += [pltpu.VMEM(args[i].shape, args[i].dtype) for i in far]
        scratch_shapes += [pltpu.VMEM(*outs[i]) for i in sent]
        scratch_shapes.append(pltpu.SemaphoreType.DMA((len(far) + len(sent),)))
        kernel = with_far(kernel, [len(lead) + i for i in far], [first + i for i in sent], early)
    for i in (*far, *raw):
        args[i] = pltpu.with_memory_space_constraint(args[i], pltpu.HBM)
    return pl.pallas_call(
        kernel,
        out_shape=[
            pltpu.HBM(s, d) if i in sent else jax.ShapeDtypeStruct(s, d)
            for i, (s, d) in enumerate(outs)
        ],
        in_specs=[pl.BlockSpec(memory_space=pltpu.SMEM)] * len(lead)
        + [there if i in far or i in raw else whole for i in range(len(args))],
        out_specs=[there if i in sent else whole for i in range(len(outs))],
        scratch_shapes=scratch_shapes,
        compiler_params=pltpu.CompilerParams(vmem_limit_bytes=VMEM_LIMIT),
        cost_estimate=cost(us),
        name=name,
    )(*lead, *args)


def cost(us):
    return pl.CostEstimate(flops=int(us * 1.1e9), bytes_accessed=0, transcendentals=0)


def swap(value, axis, shift):
    count = lax.axis_size(axis)
    return lax.ppermute(value, axis, [(i, i ^ shift) for i in range(count)])


def after(values, *done):
    return lax.optimization_barrier((values, done))[0]


def to_planes(blocks):
    if len(blocks) > 1:
        return [blocks[0]] + [swap(b, "ep", k) for k, b in enumerate(blocks) if k]
    return [exchange(blocks[0], "ep")]


def exchange(value, axis):
    count = lax.axis_size(axis)
    split = value.reshape(count, -1, value.shape[-1])
    moved = lax.all_to_all(split, axis, split_axis=0, concat_axis=0, tiled=True)
    return moved.reshape(value.shape)


def gather_blocks(parts):
    return [parts[0]] + [swap(p, "tp", d) for d, p in enumerate(parts) if d]


def gather_tp(block):
    count, cut = lax.axis_size("tp"), 64
    if count != 4:
        return [block] + [swap(block, "tp", d) for d in range(1, count)]
    first, second = swap(block, "tp", 1), swap(block, "tp", 2)
    return [block, first, second, swap(first[:cut], "tp", 2), swap(second[cut:], "tp", 1)]


def body(
    x, passage, gain1, w_q, w_k, w_v, w_o, gain2, w_r, embed, temp, w_up, w_down, chosen, place, cot
):
    blocks, planes = lax.axis_size("tp"), lax.axis_size("ep")
    ids = jnp.stack([lax.axis_index("dp"), lax.axis_index("ep"), lax.axis_index("tp")])
    ids = ids.astype(jnp.int32)
    tokens, width = x.shape
    rows, local = tokens // blocks, w_q.shape[1]
    w_q, w_k, w_v, w_r = w_q.T, w_k.T, w_v.T, w_r.T
    experts, router = embed.shape
    hidden_units = w_up.shape[2]
    capacity = rows // experts
    pieces = planes if planes <= 4 else 1
    relative = pieces > 1
    slot_shapes = [((rows // pieces, width), F32)] * pieces
    wide = -(-(2 * hidden_units + router) // 128) * 128
    slab_rows = -(-(router + experts + 2) // 8) * 8
    w_up, w_down = w_up[0], w_down[0]
    chosen, place = chosen.reshape(1, rows), place.reshape(1, rows)
    gain1_line, gain1, gain2 = gain1, gain1.reshape(1, width), gain2.reshape(1, width)
    seg = passage.reshape(blocks, rows)
    temp = temp.reshape(1, 1)

    ctx, *parts = call(
        functools.partial(attend_kernel, blocks), ids, [seg, gain1_line, x, w_q, w_k, w_v, w_o],
        [((tokens, local), F32)] + [((rows, width), F32)] * blocks,
        [((tokens, width), F32)] + [((tokens, local), F32)] * 3
        + [pltpu.SemaphoreType.DMA((blocks,))],
        far=(0, 1, 3, 4, 5, 6), raw=(2,), early=2, name="attend", us=US["attend"],
    )
    got = gather_blocks(parts)
    w_up_sib, w_down_sib = swap(w_up, "dp", 1), swap(w_down, "dp", 1)
    slots = call(
        functools.partial(prep_kernel, capacity, relative), ids,
        [chosen, place, after(cot, *parts, w_up_sib, w_down_sib)], slot_shapes, far=(0, 1, 2), name="prep",
        us=US["prep"],
    )
    cot_slots = to_planes(slots)
    u_high, u_low = call(
        up_weights_kernel, None, [w_up, w_up_sib, w_r], [((width, wide), BF16)] * 2, name="up_weights",
        us=US["up_weights"],
    )
    cot_rows = jnp.concatenate(cot_slots, axis=0)
    cots = gather_tp(after(cot_rows, got[1]))
    hidden, *slots = call(
        functools.partial(hidden_kernel, capacity, relative, blocks), ids,
        [x, gain2, chosen, place, *after(got, u_high, cot_rows)], [((rows, width), F32)] + slot_shapes,
        name="hidden", us=US["hidden"],
    )

    same = gather_tp(jnp.concatenate(to_planes(slots), axis=0))
    act_shape = [((2 * rows, 2 * hidden_units), F32)]
    first, w_high, w_low = call(
        cot_kernel, None, [w_down, w_down_sib, *after(cots[:2], hidden)],
        act_shape + [((2 * hidden_units, width), BF16)] * 2, name="cot_act", us=US["cot_act"],
    )
    act_grads = [first]
    ga, dp, slabs, parts = [], [], [], []
    for d in range(0, blocks, 2):
        if d:
            ends = cots[d : d + 2] if d + 2 < blocks else cots[d:]
            act_grads += call(
                cot_rest_kernel, None, [w_high, w_low, *after(ends, *slabs)], act_shape,
                name="cot_act_rest", us=0,
            )
        *d_feeds, ga_high, ga_low, dp_high, dp_low, slab = call(
            expert_kernel, ids,
            [act_grads[d // 2], u_high, u_low, embed, temp]
            + after(same[d : d + 2] if d + 2 < blocks else same[d:], *slabs),
            [((rows, width), F32)] * 2
            + [((2 * rows, 2 * hidden_units), BF16)] * 2
            + [((2 * rows, wide), BF16)] * 2
            + [((slab_rows, width), F32)],
            name="expert", us=US["expert"],
        )
        ga += [ga_high, ga_low]
        dp += [dp_high, dp_low]
        slabs.append(slab)
        parts += [swap(f, "tp", d + i) if d + i else f for i, f in enumerate(d_feeds)]
    outs = call(
        functools.partial(expert_out_kernel, blocks), None, [w_high, w_low, *ga],
        [((rows, width), F32)] * blocks, name="expert_out", us=US["expert_out"],
    )
    pieces_back = call(
        functools.partial(sum_kernel, blocks), None, after(parts, *outs), slot_shapes,
        name="sum_feed", us=US["sum_feed"],
    )
    back = to_planes(pieces_back)
    grad_up, up_sib, grad_down, down_sib = call(
        functools.partial(expert_grad_kernel, blocks), None,
        [*after(cots, *pieces_back), *same, *ga, *dp],
        [((width, hidden_units), F32)] * 2 + [((hidden_units, width), F32)] * 2,
        name="expert_grad", us=US["expert_grad"],
    )
    (d_hidden,) = call(
        functools.partial(route_back_kernel, capacity, relative, blocks), ids,
        [hidden, cot, gain2, chosen, place, *slabs, *after(back, grad_up)],
        [((rows + slab_rows, width), F32)], name="route_back", us=US["route_back"],
    )

    up_got, down_got = swap(up_sib, "dp", 1), swap(down_sib, "dp", 1)

    d_hiddens = gather_tp(d_hidden)
    xhat, high, low, q, k, v, *split = call(
        functools.partial(again_kernel, blocks), ids,
        [gain1_line, after(x, d_hidden), w_q, w_k, w_v, w_o],
        [((tokens, width), F32)] + [((tokens, width), BF16)] * 2 + [((tokens, local), F32)] * 3
        + [((local, width), BF16)] * 8,
        [((tokens, width), F32)], far=(0, 1, 2, 3, 4, 5), early=2, name="again", us=US["again"],
    )
    half_grads = call(
        functools.partial(attend_back_kernel, blocks, 0), ids,
        [seg, q, k, v, *split[6:], *after(d_hiddens[:2], high)],
        [((2 * rows, local), F32)] + [((tokens, local), F32)] * 2, name="attend_back",
        us=US["attend_back"],
    )
    *dn, gain_row, dq, dk, dv = call(
        functools.partial(attend_back_kernel, blocks, 2), ids,
        [seg, q, k, v, *split[6:], *after(d_hiddens[2:], *half_grads, up_got, down_got), *half_grads, xhat]
        + split[:6],
        [((rows, width), F32)] * blocks + [((1, width), F32)] + [((tokens, local), F32)] * 3,
        name="attend_back_rest", us=US["attend_back"],
    )
    dn_got = gather_blocks(dn)
    shares, tracked = 8, planes == 4
    half = 4 * local // (2 * shares)
    size_a, size_b = half + 8, half
    own_part, sib_part = call(
        functools.partial(weight_grads_kernel, blocks, shares), ids,
        [high, low, dq, dk, dv, ctx, gain_row, *d_hiddens],
        [((shares // 2 * (size_a + size_b), width), F32)] * 2,
        [((4 * local, width), F32), ((8 * shares, width), F32)], name="weight_grads",
        us=US["weight_grads"],
    )
    other_part = swap(sib_part, "dp", 1)
    grad_up, grad_down = grad_up + up_got, grad_down + down_got
    dn_got = after(dn_got, grad_up, grad_down)
    if tracked:
        keep_a, send_a, keep_b, send_b = call(
            track_sums_kernel, ids, [own_part, other_part],
            [((2 * size_a, width), F32)] * 2 + [((2 * size_b, width), F32)] * 2,
            name="track_sums", us=0,
        )
        got_a, got_b = swap(send_a, "ep", 1), swap(send_b, "ep", 2)
        dn_got = after(dn_got, keep_a)
    (d_x,) = call(
        norm_back_kernel, ids, [x, gain1, d_hidden, *dn_got], [((rows, width), F32)],
        name="norm_back", us=US["norm_back"],
    )
    d_xs = gather_tp(d_x)
    if tracked:
        own_a, send_a, own_b, send_b = call(
            track_halves_kernel, None, [keep_a, got_a, keep_b, got_b],
            [((size_a, width), F32)] * 2 + [((size_b, width), F32)] * 2, name="track_halves",
            us=0,
        )
        share_a, share_b, gain = call(
            join_kernel, None, [own_a, swap(send_a, "ep", 2), own_b, swap(send_b, "ep", 1)],
            [((size_a, width), F32), ((size_b, width), F32), ((8, width), F32)], name="join",
            us=US["join"],
        )
        pair_a, pair_b = call(
            pair_kernel, None, [share_a, swap(share_a, "ep", 2), share_b, swap(share_b, "ep", 1)],
            [((2 * size_a, width), F32), ((2 * size_b, width), F32)], name="pair", us=0,
        )
        parts = [pair_a, swap(pair_a, "ep", 1), pair_b, swap(pair_b, "ep", 2)]
    else:
        parts = [lax.psum(own_part + other_part, "ep")]
        share_a, gain = parts[0], parts[0][half : half + 8]
    tracks = len(parts)
    parts = parts + [swap(p, "dp", 1) for p in parts]
    gains = gather_blocks([after(gain, *parts[tracks:])] * blocks)
    near = after(outs, share_a)
    parts_out = gather_blocks(near)
    out_pieces = call(
        functools.partial(sum_kernel, blocks), None, parts_out, slot_shapes, name="sum_out",
        us=US["sum_out"],
    )
    out_slots = to_planes(out_pieces)
    (mixed,) = call(
        functools.partial(mixed_kernel, capacity, relative), ids,
        [hidden, chosen, place, *out_slots], [((rows, width), F32)],
        name="mixed", us=US["mixed"],
    )
    (grad_tokens,) = call(
        place_blocks_kernel, ids, d_xs, [((tokens, width), F32)],
        name="grad_tokens", us=0,
    )
    grad_q, grad_k, grad_v, grad_o, grad_g1, grad_g2, grad_proj, grad_embed, grad_temp = call(
        functools.partial(finish_kernel, router, experts, shares, tracks), ids,
        [*parts, *gains],
        [((local, width), F32)] * 4 + [((width,), F32)] * 2 + [((router, width), F32)]
        + [((experts, router), F32), ((1, 1), F32)],
        [((4 * local, width), F32), ((8 * shares, width), F32)], name="finish", us=0,
    )
    return (
        mixed,
        grad_tokens,
        grad_g1,
        grad_q.T,
        grad_k.T,
        grad_v.T,
        grad_o,
        grad_g2,
        grad_proj.T,
        grad_embed,
        grad_temp.reshape(1),
        grad_up[None],
        grad_down[None],
    )


def solution(mesh):
    in_specs = (
        P(("dp", "ep"), None),
        P(("dp", "ep")),
        P(),
        P(None, "tp"),
        P(None, "tp"),
        P(None, "tp"),
        P("tp", None),
        P(),
        P(),
        P(),
        P(),
        P("ep", None, ("dp", "tp")),
        P("ep", ("dp", "tp"), None),
        P(("dp", "ep", "tp")),
        P(("dp", "ep", "tp")),
        P(("dp", "ep", "tp"), None),
    )
    out_specs = (
        P(("dp", "ep", "tp"), None),
        P(("dp", "ep"), None),
        P(),
        P(None, "tp"),
        P(None, "tp"),
        P(None, "tp"),
        P("tp", None),
        P(),
        P(),
        P(),
        P(),
        P("ep", None, ("dp", "tp")),
        P("ep", ("dp", "tp"), None),
    )
    return jax.shard_map(body, mesh=mesh, in_specs=in_specs, out_specs=out_specs, check_vma=False)
```
